32 devices in a mesh: tm: 4 (over x, core), space: 8 (over z, y).
Axes of the slice: x: 2, y: 2, z: 4, core: 2. Of those that a mesh axis runs over, the one named last changes fastest.
Arguments:
- start_states: float32 [4, 128, 1024], P('tm', 'space'), may hold values from -6 to 6
- sigma: float32 [128, 1024], P('space'), may hold values from 0.05 to 5
- labels: int32 [128, 1024], P('space'), may hold values from 0 to 3
- nu_table: float32 [4], replicated, may hold values from 0.3 to 3
- coil: float32 [128, 1024], P('space'), may hold values from -6 to 6
- waveform: float32 [64], P('tm'), may hold values from -4 to 4
Outputs:
- end_states: float32 [4, 128, 1024], P('tm', 'space')
- traces_out: float32 [64, 8192], P('tm', 'space')
The draws below stay inside these ranges and needn't reach their ends.
All inputs are finite; a program needn't handle non-finite values.
Results may differ from the reference program's by a relative error of at most 0.000026.
Values sent between devices are 32-bit elements; how exact they have to be, the bound alone decides.
No kernel may reach another device: no remote copies, remote signals or barrier semaphores. Data moves between devices by JAX's collectives and lax.ppermute only.
A program may use at most 64 MiB of HBM per device.

```python
import math
import jax
import jax.numpy as jnp
from jax import lax

CX = 16
NY = 1024
STEPS = 16
JACOBI = 8
SWEEPS = 2
MATERIALS = 4
NX = 128
WINDOWS = 4
N_TM = 4
N_SPACE = 8


def touch_ends(values, stream_key, least, high):
    place = [jax.random.randint(jax.random.fold_in(stream_key, axis), (), 0, length) for axis, length in enumerate(values.shape)]
    longest = values.shape.index(max(values.shape))
    beside = place[:longest] + [(place[longest] + 1) % values.shape[longest]] + place[longest + 1:]
    return values.at[tuple(place)].set(least).at[tuple(beside)].set(high)


def block_scale(rng, dims, cuts, least, largest):
    factor_of = 1.0
    for position, blocks in cuts:
        steps = jax.random.uniform(jax.random.fold_in(jax.random.fold_in(rng, 6), position), (blocks,), jnp.float32, least / len(cuts), largest / len(cuts))
        factor_of = factor_of * jnp.repeat(jnp.exp(steps), dims[position] // blocks).reshape((-1,) + (1,) * (len(dims) - 1 - position))
    return factor_of


def normal_values(rng, shape, scale, bound, shards=(), kind=jnp.bfloat16):
    level = block_scale(rng, shape, shards, -0.22, 0.18) if shards else 1.0
    values = jax.random.normal(rng, shape, jnp.float32) * scale * level
    return jnp.minimum(jnp.maximum(values, -bound), bound).astype(kind)


def setup_inputs(seed: int = 0) -> dict:
    key_of = jax.random.split(jax.random.key(seed), 7)
    start_states = normal_values(key_of[0], (WINDOWS, NX, NY), 1.0, 6.0, ((0, 4), (1, 8)), jnp.float32)
    sigma = jnp.clip(jnp.exp(math.log(5.0) - 4.6051702 * jax.random.uniform(key_of[1], (NX, NY), jnp.float32) ** block_scale(key_of[1], (NX, NY), ((0, 8),), -0.2, 0.2)), 0.05, 5.0)
    labels = touch_ends(jax.random.randint(key_of[2], (NX, NY), 0, MATERIALS), jax.random.fold_in(key_of[2], 1), 0, MATERIALS - 1).astype(jnp.int32)
    nu_table = jnp.clip(jnp.exp(jax.random.uniform(key_of[3], (MATERIALS,), jnp.float32, math.log(0.3), math.log(3.0))), 0.3, 3.0)
    coil = normal_values(key_of[4], (NX, NY), 1.0, 6.0, ((0, 8),), jnp.float32)
    waveform = normal_values(key_of[5], (WINDOWS * STEPS,), 1.0, 4.0, ((0, 4),), jnp.float32)
    return {"start_states": start_states, "sigma": sigma, "labels": labels, "nu_table": nu_table, "coil": coil, "waveform": waveform}


THETA = 0.25


def shifted(field, axis, low, high):
    config = [(0, 0, 0)] * field.ndim
    config[axis % field.ndim] = (low, high, 0)
    return lax.pad(field, jnp.zeros((), field.dtype), config)


def next_column(field):
    return shifted(field, -2, -1, 1)


def prev_column(field):
    return shifted(field, -2, 1, -1)


def next_row(field):
    return shifted(field, -1, -1, 1)


def prev_row(field):
    return shifted(field, -1, 1, -1)


def from_next(array, axis):
    moved = jnp.moveaxis(array, axis, 0)
    moved = jnp.concatenate([moved[1:], jnp.zeros_like(moved[:1])], axis=0)
    return jnp.moveaxis(moved, 0, axis)


def from_prev(array, axis):
    moved = jnp.moveaxis(array, axis, 0)
    moved = jnp.concatenate([jnp.zeros_like(moved[:1]), moved[:-1]], axis=0)
    return jnp.moveaxis(moved, 0, axis)


def harmonic(first_nu, second_nu):
    return 2.0 * first_nu * second_nu / (first_nu + second_nu)


def reluctivity(labels, nu_table):
    result = jnp.zeros(labels.shape, jnp.float32)
    for material in range(nu_table.shape[0]):
        result = result + jnp.where(labels == material, nu_table[material], jnp.float32(0.0))
    return result


def coefficients(sigma, nu, first, last):
    kxp = harmonic(nu, next_column(nu))
    kxm = harmonic(nu, prev_column(nu))
    kyp = harmonic(nu, next_row(nu))
    kym = harmonic(nu, prev_row(nu))
    rows = jnp.arange(nu.shape[-1])
    edge_rows = ((rows == 0) | (rows == nu.shape[-1] - 1)).astype(jnp.float32)
    inner = sigma + kxp + kxm + kyp + kym + 2.0 * nu * edge_rows
    left_coef = 2.0 * nu[..., 0, :]
    right_coef = 2.0 * nu[..., -1, :]
    cols = jnp.arange(nu.shape[-2])[:, None]
    at_left = (cols == 0).astype(jnp.float32)
    at_right = (cols == nu.shape[-2] - 1).astype(jnp.float32)
    d_dir = inner + at_left * left_coef[..., None, :] + at_right * right_coef[..., None, :]
    d_neu = inner + at_left * (first * left_coef)[..., None, :] + at_right * (last * right_coef)[..., None, :]
    return (sigma, kxp, kxm, kyp, kym), left_coef, right_coef, d_dir, d_neu


def march(start, couple, diag, coil, waves, left_term, right_term):
    sigma, kxp, kxm, kyp, kym = couple
    cols = jnp.arange(start.shape[-2])[:, None]
    at_left = (cols == 0).astype(jnp.float32)
    at_right = (cols == start.shape[-2] - 1).astype(jnp.float32)

    def advance(previous, inputs):
        wave, left_val, right_val = inputs
        rhs = sigma * previous + coil * wave + at_left * left_val[..., None, :] + at_right * right_val[..., None, :]
        field = previous
        for repeat in range(JACOBI):
            total = rhs + kxp * next_column(field) + kxm * prev_column(field) + kyp * next_row(field) + kym * prev_row(field)
            field = total / diag
        return field, (field[..., 0, :], field[..., -1, :])

    return lax.scan(advance, start, (waves, left_term, right_term))


def reference(start_states, sigma, labels, nu_table, coil, waveform):
    nu = reluctivity(labels, nu_table).reshape(N_SPACE, CX, NY)
    sig = sigma.reshape(N_SPACE, CX, NY)
    coil_blocks = coil.reshape(N_SPACE, CX, NY)
    places = jnp.arange(N_SPACE)
    first = (places == 0).astype(jnp.float32)[:, None]
    last = (places == N_SPACE - 1).astype(jnp.float32)[:, None]
    couple, left_coef, right_coef, d_dir, d_neu = coefficients(sig, nu, first, last)
    waves = waveform.reshape(N_TM, STEPS).T.reshape(STEPS, N_TM, 1, 1, 1)
    zero_waves = jnp.zeros_like(waves)
    states = start_states.reshape(N_TM, N_SPACE, CX, NY)
    traces = jnp.zeros((STEPS, N_TM, N_SPACE, NY), jnp.float32)
    inner_face = 1.0 - last
    ends = states
    for relax_round in range(SWEEPS):
        left_val = from_prev(traces, 2)
        left_term = left_coef * left_val
        right_term = right_coef * traces
        ends, (firsts, lasts) = march(states, couple, d_dir, coil_blocks, waves, left_term, right_term)
        nb_first = from_next(firsts, 2)
        nb_coef = from_next(left_coef, 0)
        flux = inner_face * (right_coef * (lasts - traces) + nb_coef * (nb_first - traces))
        flux_left = from_prev(flux, 2)
        unused, (pfirst, plast) = march(jnp.zeros_like(states), couple, d_neu, coil_blocks, zero_waves, flux_left, flux)
        traces = traces + THETA * inner_face * (plast + from_next(pfirst, 2))
        if relax_round + 1 < SWEEPS:
            states = jnp.roll(ends, 1, axis=0)
    end_states = ends.reshape(N_TM, N_SPACE * CX, NY)
    traces_out = jnp.transpose(traces, (1, 0, 2, 3)).reshape(N_TM * STEPS, N_SPACE * NY)
    return end_states, traces_out
```

```python
import functools

import jax
import jax.numpy as jnp
from jax import lax
from jax.experimental import pallas as pl
from jax.experimental.pallas import tpu as pltpu
from jax.sharding import PartitionSpec as P

JACOBI = 8
SWEEPS = 2
THETA = 0.25

BLOCK = 8
SUB = 8
LANES = 128
DEPTH = 4
LOW = -(DEPTH - 1)
HIGH = BLOCK + DEPTH - 1
ROWS = HIGH - LOW
Q_E, P_O, Q_O, UP_O, DN_O, UP_E, DN_E = range(7)
SIG_E, SIG_O, COIL_E, COIL_O, FACE_E, FACE_O = range(6)
F32 = jnp.float32


def tile_index(axis):
    return lax.broadcasted_iota(jnp.int32, (SUB, LANES), axis)


def next_lane(tile):
    return pltpu.roll(tile, LANES - 1, 1)


def prev_lane(tile):
    return pltpu.roll(tile, 1, 1)


def next_sub(tile):
    return pltpu.roll(tile, SUB - 1, 0)


def prev_sub(tile):
    return pltpu.roll(tile, 1, 0)


def swap_groups(tiles):
    group = tile_index(1) // 16
    for bit in (1, 2, 4):
        new = []
        for j, tile in enumerate(tiles):
            other = tiles[j ^ bit]
            if j & bit:
                new.append(jnp.where((group & bit) != 0, tile, pltpu.roll(other, LANES - 16 * bit, 1)))
            else:
                new.append(jnp.where((group & bit) == 0, tile, pltpu.roll(other, 16 * bit, 1)))
        tiles = new
    return tiles


def to_blocks(tiles):
    lane = tile_index(1)
    order = 8 * (lane % 16) + lane // 16
    return swap_groups([jnp.take_along_axis(tile, order, axis=1) for tile in tiles])


def from_blocks(tiles):
    lane = tile_index(1)
    order = 16 * (lane % 8) + lane // 8
    return [jnp.take_along_axis(tile, order, axis=1) for tile in swap_groups(tiles)]


def load_field(ref, scratch):
    for j in range(BLOCK):
        scratch[16 * j : 16 * j + 16, :] = ref[:, LANES * j : LANES * j + LANES]
    halves = [
        to_blocks([scratch[pl.ds(16 * j + e, SUB, stride=2), :] for j in range(BLOCK)])
        for e in range(2)
    ]
    return halves


def harmonic(first_nu, second_nu):
    return 2.0 * first_nu * second_nu / (first_nu + second_nu)


def spread(tiles):
    rows = {}
    for r in range(LOW, HIGH):
        if r < 0:
            rows[r] = prev_lane(tiles[r + BLOCK])
        elif r >= BLOCK:
            rows[r] = next_lane(tiles[r - BLOCK])
        else:
            rows[r] = tiles[r]
    return rows


def flags():
    place = lax.axis_index("space")
    count = lax.axis_size("space")
    return place % 2 == 0, place > 0, place < count - 1


def plain_kernel(labels_ref, table_ref, sigma_ref, coil_ref, start_ref, nu_out, sigma_out, coil_out, start_out, s0, s1, s2, s3):
    nu = jnp.zeros(labels_ref.shape, F32)
    for material in range(table_ref.shape[0]):
        nu = nu + jnp.where(labels_ref[...] == material, table_ref[material], 0.0)
    for value, scratch, out in ((nu, s0, nu_out), (sigma_ref[...], s1, sigma_out), (coil_ref[...], s2, coil_out), (start_ref[0], s3, start_out)):
        halves = load_field(value, scratch)
        for e in range(2):
            for r in range(BLOCK):
                out[r, e] = halves[e][r]


def unit_up(r):
    return r % BLOCK in (0, 2, 4, 6)


def unit_down(r):
    return r % BLOCK in (2, 4, 6)


def coef_kernel(neumann, nu_ref, sigma_ref, coil_ref, c_out, r_out, scale_out, edge_out):
    _, has_left, has_right = flags()
    sub = tile_index(0)
    lane = tile_index(1)
    nu_e = [nu_ref[r, 0] for r in range(BLOCK)]
    nu_o = [nu_ref[r, 1] for r in range(BLOCK)]
    pair = [harmonic(nu_e[r], nu_o[r]) for r in range(BLOCK)]
    cross_o = [jnp.where(sub == SUB - 1, 0.0, harmonic(nu_o[r], next_sub(nu_e[r]))) for r in range(BLOCK)]
    cross_e = [prev_sub(cross_o[r]) for r in range(BLOCK)]

    def upward(nu):
        ups = [harmonic(nu[r], nu[r + 1]) for r in range(BLOCK - 1)]
        ups.append(jnp.where(lane == LANES - 1, 0.0, harmonic(nu[BLOCK - 1], next_lane(nu[0]))))
        downs = [prev_lane(ups[BLOCK - 1])] + ups[:-1]
        return ups, downs

    up_e, dn_e = upward(nu_e)
    up_o, dn_o = upward(nu_o)
    left_kept = jnp.logical_not(has_left) if neumann else True
    right_kept = jnp.logical_not(has_right) if neumann else True
    inv_e, inv_o, sig_e, sig_o = [], [], [], []
    for r in range(BLOCK):
        d_e = sigma_ref[r, 0] + pair[r] + cross_e[r] + up_e[r] + dn_e[r]
        d_o = sigma_ref[r, 1] + pair[r] + cross_o[r] + up_o[r] + dn_o[r]
        if r in (0, BLOCK - 1):
            on_edge = lane == (0 if r == 0 else LANES - 1)
            d_e = d_e + jnp.where(on_edge, 2.0 * nu_e[r], 0.0)
            d_o = d_o + jnp.where(on_edge, 2.0 * nu_o[r], 0.0)
        d_e = d_e + jnp.where((sub == 0) & left_kept, 2.0 * nu_e[r], 0.0)
        d_o = d_o + jnp.where((sub == SUB - 1) & right_kept, 2.0 * nu_o[r], 0.0)
        inv_e.append(1.0 / d_e)
        inv_o.append(1.0 / d_o)
    scale_e, scale_o = [jnp.ones((SUB, LANES), F32)], []
    for r in range(1, BLOCK):
        if unit_down(r):
            scale_e.append(scale_e[r - 1] * (dn_e[r] * inv_e[r]))
        else:
            scale_e.append(scale_e[r - 1] / (up_e[r - 1] * inv_e[r - 1]))
    for r in range(BLOCK):
        scale_o.append(scale_e[r] / (pair[r] * inv_e[r]))
    rec_e = [inv_e[r] / scale_e[r] for r in range(BLOCK)]
    rec_o = [inv_o[r] / scale_o[r] for r in range(BLOCK)]
    around_e = [prev_lane(scale_e[BLOCK - 1])] + scale_e + [next_lane(scale_e[0])]
    around_o = [prev_lane(scale_o[BLOCK - 1])] + scale_o + [next_lane(scale_o[0])]

    def put(out, slot, tiles, needed=lambda r: True):
        rows = spread(tiles)
        for r in range(LOW, HIGH):
            if needed(r):
                out[r - LOW, slot] = rows[r]

    span = range(BLOCK)
    put(c_out, Q_E, [cross_e[r] * prev_sub(scale_o[r]) * rec_e[r] for r in span])
    put(c_out, P_O, [pair[r] * scale_e[r] * rec_o[r] for r in span])
    put(c_out, Q_O, [cross_o[r] * next_sub(scale_e[r]) * rec_o[r] for r in span])
    put(c_out, UP_O, [up_o[r] * around_o[r + 2] * rec_o[r] for r in span])
    put(c_out, DN_O, [dn_o[r] * around_o[r] * rec_o[r] for r in span])
    put(c_out, UP_E, [up_e[r] * around_e[r + 2] * rec_e[r] for r in span], lambda r: not unit_up(r))
    put(c_out, DN_E, [dn_e[r] * around_e[r] * rec_e[r] for r in span], lambda r: not unit_down(r))
    put(r_out, SIG_E, [sigma_ref[r, 0] * inv_e[r] for r in span])
    put(r_out, SIG_O, [sigma_ref[r, 1] * inv_o[r] for r in span])
    if not neumann:
        put(r_out, COIL_E, [coil_ref[r, 0] * rec_e[r] for r in span])
        put(r_out, COIL_O, [coil_ref[r, 1] * rec_o[r] for r in span])
    put(r_out, FACE_E, [jnp.where((sub == 0) & has_left, rec_e[r], 0.0) for r in span])
    put(r_out, FACE_O, [jnp.where((sub == SUB - 1) & has_right, rec_o[r], 0.0) for r in span])
    for r in range(BLOCK):
        scale_out[r, 0] = scale_e[r]
        scale_out[r, 1] = scale_o[r]
        edge_out[0, r : r + 1] = 2.0 * nu_e[r][0:1]
        edge_out[1, r : r + 1] = 2.0 * nu_o[r][SUB - 1 : SUB]
        edge_out[2, r : r + 1] = scale_e[r][0:1]
        edge_out[3, r : r + 1] = scale_o[r][SUB - 1 : SUB]


def advance(field_e, field_o, rhs, c_ref):
    for turn in range(JACOBI // DEPTH):
        if turn == 0:
            now_e, now_o = field_e, field_o
        else:
            now_e, now_o = haloed(now_e), haloed(now_o)
        for k in range(1, DEPTH + 1):
            new_e, new_o = {}, {}
            for r in range(k - DEPTH, BLOCK + DEPTH - k):
                i = r - LOW
                up = now_e[r + 1] if unit_up(r) else c_ref[i, UP_E] * now_e[r + 1]
                down = now_e[r - 1] if unit_down(r) else c_ref[i, DN_E] * now_e[r - 1]
                new_e[r] = (rhs[r][0] + now_o[r]) + (up + down) + c_ref[i, Q_E] * prev_sub(now_o[r])
                new_o[r] = (
                    (rhs[r][1] + c_ref[i, P_O] * now_e[r])
                    + (c_ref[i, UP_O] * now_o[r + 1] + c_ref[i, DN_O] * now_o[r - 1])
                    + c_ref[i, Q_O] * next_sub(now_e[r])
                )
            now_e, now_o = new_e, new_o
    return now_e, now_o


def haloed(rows):
    out = {r: rows[r] for r in range(BLOCK)}
    for j in range(DEPTH):
        out[j - DEPTH] = prev_lane(rows[BLOCK - DEPTH + j])
        out[BLOCK + j] = next_lane(rows[j])
    return out


def march(start, c_ref, r_ref, wave_ref, left, right, first, last, steps):
    def step(t, carry):
        now_e = haloed(dict(enumerate(carry[:BLOCK])))
        now_o = haloed(dict(enumerate(carry[BLOCK:])))
        rhs = {}
        for r in range(LOW, HIGH):
            i = r - LOW
            b_e = r_ref[i, SIG_E] * now_e[r]
            b_o = r_ref[i, SIG_O] * now_o[r]
            if wave_ref is not None:
                b_e = b_e + r_ref[i, COIL_E] * wave_ref[t]
                b_o = b_o + r_ref[i, COIL_O] * wave_ref[t]
            if left is not None:
                at = pl.ds(t * 3 * BLOCK + BLOCK + r, 1)
                b_e = b_e + r_ref[i, FACE_E] * left[at, :]
                b_o = b_o + r_ref[i, FACE_O] * right[at, :]
            rhs[r] = (b_e, b_o)
        now_e, now_o = advance(now_e, now_o, rhs, c_ref)
        for r in range(BLOCK):
            first[pl.ds(t * BLOCK + r, 1), :] = now_e[r][0:1]
            last[pl.ds(t * BLOCK + r, 1), :] = now_o[r][SUB - 1 : SUB]
        return tuple(now_e[r] for r in range(BLOCK)) + tuple(now_o[r] for r in range(BLOCK))

    return lax.fori_loop(0, steps, step, start)


def put_face(ref, t, tile):
    base = t * 3 * BLOCK
    ref[base : base + BLOCK, :] = prev_lane(tile)
    ref[base + BLOCK : base + 2 * BLOCK, :] = tile
    ref[base + 2 * BLOCK : base + 3 * BLOCK, :] = next_lane(tile)


def at_step(ref, t):
    return ref[t * BLOCK : (t + 1) * BLOCK, :]


def dirichlet_kernel(sweep, steps, *refs):
    if sweep == 0:
        (start_ref, c_ref, r_ref, scale_ref, edge_ref, wave_ref, ends, ev_out, od_out, first, last) = refs
        left = right = None
    else:
        (start_ref, c_ref, r_ref, scale_ref, edge_ref, wave_ref, ev_own, od_own, ev_got, od_got,
         ends, ev_out, od_out, g_left, g_right, first, last, left, right) = refs
    even, _, _ = flags()
    if sweep > 0:
        for t in range(steps):
            ev = THETA * (at_step(ev_own, t) + at_step(ev_got, t))
            od = THETA * (at_step(od_own, t) + at_step(od_got, t))
            at_left = jnp.where(even, od, ev)
            at_right = jnp.where(even, ev, od)
            g_left[t * BLOCK : (t + 1) * BLOCK, :] = at_left
            g_right[t * BLOCK : (t + 1) * BLOCK, :] = at_right
            put_face(left, t, edge_ref[0] * at_left)
            put_face(right, t, edge_ref[1] * at_right)
    start = tuple(start_ref[r, e] / scale_ref[r, e] for e in range(2) for r in range(BLOCK))
    final = march(start, c_ref, r_ref, wave_ref, left, right, first, last, steps)
    for e in range(2):
        for r in range(BLOCK):
            ends[r, e] = final[e * BLOCK + r] * scale_ref[r, e]
    for t in range(steps):
        to_left = edge_ref[2] * at_step(first, t)
        to_right = edge_ref[3] * at_step(last, t)
        if sweep > 0:
            to_left = to_left - at_step(g_left, t)
            to_right = to_right - at_step(g_right, t)
        to_left = edge_ref[0] * to_left
        to_right = edge_ref[1] * to_right
        ev_out[t * BLOCK : (t + 1) * BLOCK, :] = jnp.where(even, to_right, to_left)
        od_out[t * BLOCK : (t + 1) * BLOCK, :] = jnp.where(even, to_left, to_right)


def neumann_kernel(sweep, steps, *refs):
    if sweep + 1 < SWEEPS:
        (c_ref, r_ref, edge_ref, ev_own, od_own, ev_got, od_got, ev_out, od_out, first, last, left, right) = refs
    else:
        (c_ref, r_ref, edge_ref, ev_own, od_own, ev_got, od_got, g_right, mine_out, first_out,
         first, last, left, right, s0, s1) = refs
    even, _, _ = flags()
    for t in range(steps):
        ev = at_step(ev_own, t) + at_step(ev_got, t)
        od = at_step(od_own, t) + at_step(od_got, t)
        put_face(left, t, jnp.where(even, od, ev))
        put_face(right, t, jnp.where(even, ev, od))
    zero = jnp.zeros((SUB, LANES), F32)
    march((zero,) * (2 * BLOCK), c_ref, r_ref, None, left, right, first, last, steps)
    if sweep + 1 < SWEEPS:
        for t in range(steps):
            to_left = edge_ref[2] * at_step(first, t)
            to_right = edge_ref[3] * at_step(last, t)
            ev_out[t * BLOCK : (t + 1) * BLOCK, :] = jnp.where(even, to_right, to_left)
            od_out[t * BLOCK : (t + 1) * BLOCK, :] = jnp.where(even, to_left, to_right)
    else:
        for t in range(steps):
            s0[t * BLOCK : (t + 1) * BLOCK, :] = THETA * (edge_ref[2] * at_step(first, t))
            s1[t * BLOCK : (t + 1) * BLOCK, :] = at_step(g_right, t) + THETA * (edge_ref[3] * at_step(last, t))
        for scratch, out in ((s0, first_out), (s1, mine_out)):
            for half in range(steps // SUB):
                base = half * SUB * BLOCK
                tiles = from_blocks([scratch[pl.ds(base + r, SUB, stride=BLOCK), :] for r in range(BLOCK)])
                for j in range(BLOCK):
                    out[half * SUB : (half + 1) * SUB, j * LANES : (j + 1) * LANES] = tiles[j]


def natural_kernel(ends_ref, out, scratch):
    for e in range(2):
        tiles = from_blocks([ends_ref[r, e] for r in range(BLOCK)])
        for j in range(BLOCK):
            scratch[pl.ds(16 * j + e, SUB, stride=2), :] = tiles[j]
    for j in range(BLOCK):
        out[0, :, LANES * j : LANES * j + LANES] = scratch[16 * j : 16 * j + 16, :]


def join_kernel(mine_ref, got_ref, out):
    _, _, has_right = flags()
    out[...] = jnp.where(has_right, mine_ref[...] + got_ref[...], 0.0)


def call(kernel, name, inputs, outputs, scratch=(), smem=()):
    specs = [
        pl.BlockSpec(memory_space=pltpu.SMEM if i in smem else pltpu.VMEM)
        for i in range(len(inputs))
    ]
    single = not isinstance(outputs, list)
    shapes = [jax.ShapeDtypeStruct(s, F32) for s in ([outputs] if single else outputs)]
    result = pl.pallas_call(
        kernel,
        out_shape=shapes,
        in_specs=specs,
        out_specs=[pl.BlockSpec(memory_space=pltpu.VMEM)] * len(shapes),
        scratch_shapes=[pltpu.VMEM(s, F32) for s in scratch],
        compiler_params=pltpu.CompilerParams(vmem_limit_bytes=6 << 20),
        name=name,
    )(*inputs)
    return result[0] if single else result


def body(start_states, sigma, labels, nu_table, coil, waveform):
    steps = waveform.shape[0]
    columns, rows = sigma.shape
    count = lax.axis_size("space")
    windows = lax.axis_size("tm")
    even_faces = [(i, i ^ 1) for i in range(count)]
    odd_faces = [(i, i + 1 if i % 2 else i - 1) for i in range(1, count - 1)] + [(0, 0), (count - 1, count - 1)]
    field = (BLOCK, 2, SUB, LANES)
    series = (steps * BLOCK, LANES)
    wide = (3 * steps * BLOCK, LANES)
    nu, sig, cur, state = call(
        plain_kernel, "plain", [labels, nu_table, sigma, coil, start_states], [field] * 4, [(128, LANES)] * 4, smem=(1,)
    )
    shapes = [(ROWS, 7, SUB, LANES), (ROWS, 6, SUB, LANES), field, (4, BLOCK, LANES)]
    c_dir, r_dir, scale_dir, edge_dir = call(functools.partial(coef_kernel, False), "coef_dir", [nu, sig, cur], shapes)
    c_neu, r_neu, _, edge_neu = call(functools.partial(coef_kernel, True), "coef_neu", [nu, sig, cur], shapes)

    def swapped(ev, od):
        return lax.ppermute(ev, "space", even_faces), lax.ppermute(od, "space", odd_faces)

    ends, ev, od = call(
        functools.partial(dirichlet_kernel, 0, steps), "dir0",
        [state, c_dir, r_dir, scale_dir, edge_dir, waveform], [field, series, series], [series] * 2, smem=(5,),
    )
    state = lax.ppermute(ends, "tm", [(i, (i + 1) % windows) for i in range(windows)])
    ev_got, od_got = swapped(ev, od)
    ev, od = call(
        functools.partial(neumann_kernel, 0, steps), "neu0",
        [c_neu, r_neu, edge_neu, ev, od, ev_got, od_got], [series] * 2, [series] * 2 + [wide] * 2,
    )
    ev_got, od_got = swapped(ev, od)
    ends, ev, od, _, g_right = call(
        functools.partial(dirichlet_kernel, 1, steps), "dir1",
        [state, c_dir, r_dir, scale_dir, edge_dir, waveform, ev, od, ev_got, od_got],
        [field, series, series, series, series], [series] * 2 + [wide] * 2, smem=(5,),
    )
    ev_got, od_got = swapped(ev, od)
    end_states = call(natural_kernel, "natural", [ends], (1, columns, rows), [(128, LANES)])
    mine, first = call(
        functools.partial(neumann_kernel, 1, steps), "neu1",
        [c_neu, r_neu, edge_neu, ev, od, ev_got, od_got, g_right],
        [(steps, rows)] * 2, [series] * 2 + [wide] * 2 + [series] * 2,
    )
    got = lax.ppermute(first, "space", [(i, i - 1) for i in range(1, count)])
    traces = call(join_kernel, "join", [mine, got], (steps, rows))
    return end_states, traces


def solution(mesh):
    placed = (
        P("tm", "space", None),
        P("space", None),
        P("space", None),
        P(),
        P("space", None),
        P("tm"),
    )
    return jax.shard_map(
        body,
        mesh=mesh,
        in_specs=placed,
        out_specs=(P("tm", "space", None), P("tm", "space")),
        check_vma=False,
    )
```

```python
import functools

import jax
import jax.numpy as jnp
from jax import lax
from jax.experimental import pallas as pl
from jax.experimental.pallas import tpu as pltpu
from jax.sharding import PartitionSpec as P

JACOBI = 8
SWEEPS = 2
THETA = 0.25

BLOCK = 8
SUB = 8
LANES = 128
DEPTH = 4
LOW = -(DEPTH - 1)
HIGH = BLOCK + DEPTH - 1
ROWS = HIGH - LOW
Q_E, P_O, Q_O, UP_O, DN_O, UP_E, DN_E = range(7)
SIG_E, SIG_O, COIL_E, COIL_O, FACE_E, FACE_O = range(6)
F32 = jnp.float32


def tile_index(axis):
    return lax.broadcasted_iota(jnp.int32, (SUB, LANES), axis)


def next_lane(tile):
    return pltpu.roll(tile, LANES - 1, 1)


def prev_lane(tile):
    return pltpu.roll(tile, 1, 1)


def next_sub(tile):
    return pltpu.roll(tile, SUB - 1, 0)


def prev_sub(tile):
    return pltpu.roll(tile, 1, 0)


def to_blocks(tiles):
    lane = tile_index(1)
    out = []
    for r in range(BLOCK):
        order = 8 * (lane % 16) + r
        tile = jnp.take_along_axis(tiles[0], order, axis=1)
        for j in range(1, BLOCK):
            tile = jnp.where(lane // 16 == j, jnp.take_along_axis(tiles[j], order, axis=1), tile)
        out.append(tile)
    return out


def from_blocks(tiles):
    lane = tile_index(1)
    out = []
    for j in range(BLOCK):
        order = 16 * j + lane // 8
        tile = jnp.take_along_axis(tiles[0], order, axis=1)
        for r in range(1, BLOCK):
            tile = jnp.where(lane % 8 == r, jnp.take_along_axis(tiles[r], order, axis=1), tile)
        out.append(tile)
    return out


def put_field(value, scratch, out):
    for j in range(BLOCK):
        scratch[16 * j : 16 * j + 16, :] = value[:, LANES * j : LANES * j + LANES]
    for e in range(2):
        tiles = to_blocks([scratch[pl.ds(16 * j + e, SUB, stride=2), :] for j in range(BLOCK)])
        for r in range(BLOCK):
            out[r, e] = tiles[r]


def harmonic(first_nu, second_nu):
    return 2.0 * first_nu * second_nu / (first_nu + second_nu)


def spread(tiles):
    rows = {}
    for r in range(LOW, HIGH):
        if r < 0:
            rows[r] = prev_lane(tiles[r + BLOCK])
        elif r >= BLOCK:
            rows[r] = next_lane(tiles[r - BLOCK])
        else:
            rows[r] = tiles[r]
    return rows


def flags():
    place = lax.axis_index("space")
    count = lax.axis_size("space")
    return place % 2 == 0, place > 0, place < count - 1


def first_kernel(
    labels_hbm, table_hbm, sigma_hbm, coil_hbm, start_hbm, wave_hbm,
    nu_out, sigma_out, start_out, c_out, r_out, edge_out, scale_out, wave_out,
    labels_ref, table_ref, sigma_ref, coil_ref, start_ref, wave_ref, cur_ref, s0, s1, s2, s3, sems,
):
    copies = [
        pltpu.make_async_copy(source, target, sems.at[i])
        for i, (source, target) in enumerate((
            (table_hbm, table_ref), (labels_hbm, labels_ref), (sigma_hbm, sigma_ref),
            (coil_hbm, coil_ref), (start_hbm, start_ref), (wave_hbm, wave_ref),
        ))
    ]
    for copy in copies:
        copy.start()
    copies[0].wait()
    copies[1].wait()
    labels = labels_ref[...]
    nu = jnp.zeros(labels.shape, F32)
    for material in range(table_ref.shape[0]):
        nu = nu + jnp.where(labels == material, table_ref[material], 0.0)
    put_field(nu, s0, nu_out)
    copies[2].wait()
    put_field(sigma_ref[...], s1, sigma_out)
    copies[3].wait()
    put_field(coil_ref[...], s2, cur_ref)
    copies[4].wait()
    put_field(start_ref[0], s3, start_out)
    copies[5].wait()
    for t in range(wave_ref.shape[0]):
        wave_out[t : t + 1, :] = jnp.full((1, LANES), wave_ref[t], F32)
    coef_kernel(False, nu_out, sigma_out, cur_ref, c_out, r_out, edge_out, scale_out)


def unit_up(r):
    return r % BLOCK in (0, 2, 4, 6)


def unit_down(r):
    return r % BLOCK in (2, 4, 6)


def coef_kernel(neumann, nu_ref, sigma_ref, coil_ref, c_out, r_out, edge_out, scale_out):
    _, has_left, has_right = flags()
    sub = tile_index(0)
    lane = tile_index(1)
    nu_e = [nu_ref[r, 0] for r in range(BLOCK)]
    nu_o = [nu_ref[r, 1] for r in range(BLOCK)]
    pair = [harmonic(nu_e[r], nu_o[r]) for r in range(BLOCK)]
    cross_o = [jnp.where(sub == SUB - 1, 0.0, harmonic(nu_o[r], next_sub(nu_e[r]))) for r in range(BLOCK)]
    cross_e = [prev_sub(cross_o[r]) for r in range(BLOCK)]

    def upward(nu):
        ups = [harmonic(nu[r], nu[r + 1]) for r in range(BLOCK - 1)]
        ups.append(jnp.where(lane == LANES - 1, 0.0, harmonic(nu[BLOCK - 1], next_lane(nu[0]))))
        downs = [prev_lane(ups[BLOCK - 1])] + ups[:-1]
        return ups, downs

    up_e, dn_e = upward(nu_e)
    up_o, dn_o = upward(nu_o)
    left_kept = jnp.logical_not(has_left) if neumann else True
    right_kept = jnp.logical_not(has_right) if neumann else True
    inv_e, inv_o, sig_e, sig_o = [], [], [], []
    for r in range(BLOCK):
        d_e = sigma_ref[r, 0] + pair[r] + cross_e[r] + up_e[r] + dn_e[r]
        d_o = sigma_ref[r, 1] + pair[r] + cross_o[r] + up_o[r] + dn_o[r]
        if r in (0, BLOCK - 1):
            on_edge = lane == (0 if r == 0 else LANES - 1)
            d_e = d_e + jnp.where(on_edge, 2.0 * nu_e[r], 0.0)
            d_o = d_o + jnp.where(on_edge, 2.0 * nu_o[r], 0.0)
        d_e = d_e + jnp.where((sub == 0) & left_kept, 2.0 * nu_e[r], 0.0)
        d_o = d_o + jnp.where((sub == SUB - 1) & right_kept, 2.0 * nu_o[r], 0.0)
        inv_e.append(1.0 / d_e)
        inv_o.append(1.0 / d_o)
    scale_e, scale_o = [jnp.ones((SUB, LANES), F32)], []
    for r in range(1, BLOCK):
        if unit_down(r):
            scale_e.append(scale_e[r - 1] * (dn_e[r] * inv_e[r]))
        else:
            scale_e.append(scale_e[r - 1] / (up_e[r - 1] * inv_e[r - 1]))
    for r in range(BLOCK):
        scale_o.append(scale_e[r] / (pair[r] * inv_e[r]))
    rec_e = [inv_e[r] / scale_e[r] for r in range(BLOCK)]
    rec_o = [inv_o[r] / scale_o[r] for r in range(BLOCK)]
    around_e = [prev_lane(scale_e[BLOCK - 1])] + scale_e + [next_lane(scale_e[0])]
    around_o = [prev_lane(scale_o[BLOCK - 1])] + scale_o + [next_lane(scale_o[0])]

    def put(out, slot, tiles, needed=lambda r: True):
        rows = spread(tiles)
        for r in range(LOW, HIGH):
            if needed(r):
                out[r - LOW, slot] = rows[r]

    span = range(BLOCK)
    put(c_out, Q_E, [cross_e[r] * prev_sub(scale_o[r]) * rec_e[r] for r in span])
    put(c_out, P_O, [pair[r] * scale_e[r] * rec_o[r] for r in span])
    put(c_out, Q_O, [cross_o[r] * next_sub(scale_e[r]) * rec_o[r] for r in span])
    put(c_out, UP_O, [up_o[r] * around_o[r + 2] * rec_o[r] for r in span])
    put(c_out, DN_O, [dn_o[r] * around_o[r] * rec_o[r] for r in span])
    put(c_out, UP_E, [up_e[r] * around_e[r + 2] * rec_e[r] for r in span], lambda r: not unit_up(r))
    put(c_out, DN_E, [dn_e[r] * around_e[r] * rec_e[r] for r in span], lambda r: not unit_down(r))
    put(r_out, SIG_E, [sigma_ref[r, 0] * inv_e[r] for r in span])
    put(r_out, SIG_O, [sigma_ref[r, 1] * inv_o[r] for r in span])
    if not neumann:
        put(r_out, COIL_E, [coil_ref[r, 0] * rec_e[r] for r in span])
        put(r_out, COIL_O, [coil_ref[r, 1] * rec_o[r] for r in span])
    put(r_out, FACE_E, [jnp.where((sub == 0) & has_left, rec_e[r], 0.0) for r in span])
    put(r_out, FACE_O, [jnp.where((sub == SUB - 1) & has_right, rec_o[r], 0.0) for r in span])
    for r in range(BLOCK):
        if not neumann:
            scale_out[r, 0] = scale_e[r]
            scale_out[r, 1] = scale_o[r]
        edge_out[0, r : r + 1] = 2.0 * nu_e[r][0:1]
        edge_out[1, r : r + 1] = 2.0 * nu_o[r][SUB - 1 : SUB]
        edge_out[2, r : r + 1] = scale_e[r][0:1]
        edge_out[3, r : r + 1] = scale_o[r][SUB - 1 : SUB]


def neumann_coef_kernel(nu_ref, sigma_ref, c_out, r_out, edge_out):
    coef_kernel(True, nu_ref, sigma_ref, None, c_out, r_out, edge_out, None)


def advance(field_e, field_o, rhs, c_ref):
    for turn in range(JACOBI // DEPTH):
        if turn == 0:
            now_e, now_o = field_e, field_o
        else:
            now_e, now_o = haloed(now_e), haloed(now_o)
        for k in range(1, DEPTH + 1):
            new_e, new_o = {}, {}
            for r in range(k - DEPTH, BLOCK + DEPTH - k):
                i = r - LOW
                up = now_e[r + 1] if unit_up(r) else c_ref[i, UP_E] * now_e[r + 1]
                down = now_e[r - 1] if unit_down(r) else c_ref[i, DN_E] * now_e[r - 1]
                new_e[r] = (rhs[r][0] + now_o[r]) + (up + down) + c_ref[i, Q_E] * prev_sub(now_o[r])
                new_o[r] = (
                    (rhs[r][1] + c_ref[i, P_O] * now_e[r])
                    + (c_ref[i, UP_O] * now_o[r + 1] + c_ref[i, DN_O] * now_o[r - 1])
                    + c_ref[i, Q_O] * next_sub(now_e[r])
                )
            now_e, now_o = new_e, new_o
    return now_e, now_o


def haloed(rows):
    out = {r: rows[r] for r in range(BLOCK)}
    for j in range(DEPTH):
        out[j - DEPTH] = prev_lane(rows[BLOCK - DEPTH + j])
        out[BLOCK + j] = next_lane(rows[j])
    return out


def march(start, c_ref, r_ref, wave_ref, left, right, first, last, steps):
    def step(t, carry):
        now_e = haloed(dict(enumerate(carry[:BLOCK])))
        now_o = haloed(dict(enumerate(carry[BLOCK:])))
        rhs = {}
        for r in range(LOW, HIGH):
            i = r - LOW
            b_e = r_ref[i, SIG_E] * now_e[r]
            b_o = r_ref[i, SIG_O] * now_o[r]
            if wave_ref is not None:
                wave = wave_ref[pl.ds(t, 1), :]
                b_e = b_e + r_ref[i, COIL_E] * wave
                b_o = b_o + r_ref[i, COIL_O] * wave
            if left is not None:
                at = pl.ds(t * 3 * BLOCK + BLOCK + r, 1)
                b_e = b_e + r_ref[i, FACE_E] * left[at, :]
                b_o = b_o + r_ref[i, FACE_O] * right[at, :]
            rhs[r] = (b_e, b_o)
        now_e, now_o = advance(now_e, now_o, rhs, c_ref)
        for r in range(BLOCK):
            first[pl.ds(t * BLOCK + r, 1), :] = now_e[r][0:1]
            last[pl.ds(t * BLOCK + r, 1), :] = now_o[r][SUB - 1 : SUB]
        return tuple(now_e[r] for r in range(BLOCK)) + tuple(now_o[r] for r in range(BLOCK))

    return lax.fori_loop(0, steps, step, start, unroll=2)


def put_face(ref, t, tile):
    base = t * 3 * BLOCK
    ref[base : base + BLOCK, :] = prev_lane(tile)
    ref[base + BLOCK : base + 2 * BLOCK, :] = tile
    ref[base + 2 * BLOCK : base + 3 * BLOCK, :] = next_lane(tile)


def at_step(ref, t):
    return ref[t * BLOCK : (t + 1) * BLOCK, :]


def dirichlet_kernel(sweep, steps, *refs):
    if sweep == 0:
        (start_ref, c_ref, r_ref, scale_ref, edge_ref, wave_ref, ends, ev_out, od_out, first, last) = refs
        left = right = None
    else:
        (start_ref, c_ref, r_ref, scale_ref, edge_ref, wave_ref, ev_own, od_own, ev_got, od_got,
         ends, ev_out, od_out, g_right, first, last, left, right, g_left) = refs
    even, _, _ = flags()
    if sweep > 0:
        for t in range(steps):
            ev = THETA * (at_step(ev_own, t) + at_step(ev_got, t))
            od = THETA * (at_step(od_own, t) + at_step(od_got, t))
            at_left = jnp.where(even, od, ev)
            at_right = jnp.where(even, ev, od)
            g_left[t * BLOCK : (t + 1) * BLOCK, :] = at_left
            g_right[t * BLOCK : (t + 1) * BLOCK, :] = at_right
            put_face(left, t, edge_ref[0] * at_left)
            put_face(right, t, edge_ref[1] * at_right)
    start = tuple(start_ref[r, e] / scale_ref[r, e] for e in range(2) for r in range(BLOCK))
    final = march(start, c_ref, r_ref, wave_ref, left, right, first, last, steps)
    for e in range(2):
        for r in range(BLOCK):
            ends[r, e] = final[e * BLOCK + r] * scale_ref[r, e]
    for t in range(steps):
        to_left = edge_ref[2] * at_step(first, t)
        to_right = edge_ref[3] * at_step(last, t)
        if sweep > 0:
            to_left = to_left - at_step(g_left, t)
            to_right = to_right - at_step(g_right, t)
        to_left = edge_ref[0] * to_left
        to_right = edge_ref[1] * to_right
        ev_out[t * BLOCK : (t + 1) * BLOCK, :] = jnp.where(even, to_right, to_left)
        od_out[t * BLOCK : (t + 1) * BLOCK, :] = jnp.where(even, to_left, to_right)


def neumann_kernel(sweep, steps, *refs):
    if sweep + 1 < SWEEPS:
        (c_ref, r_ref, edge_ref, ev_own, od_own, ev_got, od_got, ev_out, od_out, first, last, left, right) = refs
    else:
        (c_ref, r_ref, edge_ref, ev_own, od_own, ev_got, od_got, g_right, mine_out, first_out,
         first, last, left, right, s0, s1) = refs
    even, _, _ = flags()
    for t in range(steps):
        ev = at_step(ev_own, t) + at_step(ev_got, t)
        od = at_step(od_own, t) + at_step(od_got, t)
        put_face(left, t, jnp.where(even, od, ev))
        put_face(right, t, jnp.where(even, ev, od))
    zero = jnp.zeros((SUB, LANES), F32)
    march((zero,) * (2 * BLOCK), c_ref, r_ref, None, left, right, first, last, steps)
    if sweep + 1 < SWEEPS:
        for t in range(steps):
            to_left = edge_ref[2] * at_step(first, t)
            to_right = edge_ref[3] * at_step(last, t)
            ev_out[t * BLOCK : (t + 1) * BLOCK, :] = jnp.where(even, to_right, to_left)
            od_out[t * BLOCK : (t + 1) * BLOCK, :] = jnp.where(even, to_left, to_right)
    else:
        for t in range(steps):
            s0[t * BLOCK : (t + 1) * BLOCK, :] = THETA * (edge_ref[2] * at_step(first, t))
            s1[t * BLOCK : (t + 1) * BLOCK, :] = at_step(g_right, t) + THETA * (edge_ref[3] * at_step(last, t))
        for scratch, out in ((s0, first_out), (s1, mine_out)):
            for half in range(steps // SUB):
                base = half * SUB * BLOCK
                tiles = from_blocks([scratch[pl.ds(base + r, SUB, stride=BLOCK), :] for r in range(BLOCK)])
                for j in range(BLOCK):
                    out[half * SUB : (half + 1) * SUB, j * LANES : (j + 1) * LANES] = tiles[j]


def natural_kernel(ends_ref, out, scratch):
    for e in range(2):
        tiles = from_blocks([ends_ref[r, e] for r in range(BLOCK)])
        for j in range(BLOCK):
            scratch[pl.ds(16 * j + e, SUB, stride=2), :] = tiles[j]
    for j in range(BLOCK):
        out[0, :, LANES * j : LANES * j + LANES] = scratch[16 * j : 16 * j + 16, :]


def join_kernel(mine_ref, got_ref, out):
    _, _, has_right = flags()
    out[...] = jnp.where(has_right, mine_ref[...] + got_ref[...], 0.0)


def call(kernel, name, inputs, outputs, scratch=(), space=pltpu.VMEM):
    single = not isinstance(outputs, list)
    shapes = [jax.ShapeDtypeStruct(s, F32) for s in ([outputs] if single else outputs)]
    result = pl.pallas_call(
        kernel,
        out_shape=shapes,
        in_specs=[pl.BlockSpec(memory_space=space)] * len(inputs),
        out_specs=[pl.BlockSpec(memory_space=pltpu.VMEM)] * len(shapes),
        scratch_shapes=[pltpu.VMEM(s, F32) if isinstance(s, tuple) else s for s in scratch],
        compiler_params=pltpu.CompilerParams(vmem_limit_bytes=6 << 20),
        name=name,
    )(*inputs)
    return result[0] if single else result


def body(start_states, sigma, labels, nu_table, coil, waveform):
    steps = waveform.shape[0]
    columns, rows = sigma.shape
    count = lax.axis_size("space")
    windows = lax.axis_size("tm")
    even_faces = [(i, i ^ 1) for i in range(count)]
    odd_faces = [(i, i + 1 if i % 2 else i - 1) for i in range(1, count - 1)] + [(0, 0), (count - 1, count - 1)]
    field = (BLOCK, 2, SUB, LANES)
    series = (steps * BLOCK, LANES)
    wide = (3 * steps * BLOCK, LANES)
    coefs = [(ROWS, 7, SUB, LANES), (ROWS, 6, SUB, LANES), (4, BLOCK, LANES)]
    nu, sig, state, c_dir, r_dir, edge_dir, scale_dir, wave = call(
        first_kernel, "first", [labels, nu_table, sigma, coil, start_states, waveform],
        [field, field, field, coefs[0], coefs[1], coefs[2], field, (steps, LANES)],
        [
            pltpu.VMEM(labels.shape, jnp.int32), pltpu.SMEM(nu_table.shape, F32), sigma.shape, coil.shape,
            start_states.shape, pltpu.SMEM(waveform.shape, F32), field,
        ] + [(128, LANES)] * 4 + [pltpu.SemaphoreType.DMA((6,))],
        space=pltpu.HBM,
    )
    c_neu, r_neu, edge_neu = call(neumann_coef_kernel, "coef_neu", [nu, sig], coefs)

    def swapped(ev, od):
        return lax.ppermute(ev, "space", even_faces), lax.ppermute(od, "space", odd_faces)

    ends, ev, od = call(
        functools.partial(dirichlet_kernel, 0, steps), "dir0",
        [state, c_dir, r_dir, scale_dir, edge_dir, wave], [field, series, series], [series] * 2,
    )
    state = lax.ppermute(ends, "tm", [(i, (i + 1) % windows) for i in range(windows)])
    ev_got, od_got = swapped(ev, od)
    ev, od = call(
        functools.partial(neumann_kernel, 0, steps), "neu0",
        [c_neu, r_neu, edge_neu, ev, od, ev_got, od_got], [series] * 2, [series] * 2 + [wide] * 2,
    )
    ev_got, od_got = swapped(ev, od)
    ends, ev, od, g_right = call(
        functools.partial(dirichlet_kernel, 1, steps), "dir1",
        [state, c_dir, r_dir, scale_dir, edge_dir, wave, ev, od, ev_got, od_got],
        [field, series, series, series], [series] * 2 + [wide] * 2 + [series],
    )
    ev_got, od_got = swapped(ev, od)
    end_states = call(natural_kernel, "natural", [ends], (1, columns, rows), [(128, LANES)])
    mine, first = call(
        functools.partial(neumann_kernel, 1, steps), "neu1",
        [c_neu, r_neu, edge_neu, ev, od, ev_got, od_got, g_right],
        [(steps, rows)] * 2, [series] * 2 + [wide] * 2 + [series] * 2,
    )
    got = lax.ppermute(first, "space", [(i, i - 1) for i in range(1, count)])
    traces = call(join_kernel, "join", [mine, got], (steps, rows))
    return end_states, traces


def solution(mesh):
    placed = (
        P("tm", "space", None),
        P("space", None),
        P("space", None),
        P(),
        P("space", None),
        P("tm"),
    )
    return jax.shard_map(
        body,
        mesh=mesh,
        in_specs=placed,
        out_specs=(P("tm", "space", None), P("tm", "space")),
        check_vma=False,
    )
```

```python
import functools

import jax
import jax.numpy as jnp
from jax import lax
from jax.experimental import pallas as pl
from jax.experimental.pallas import tpu as pltpu
from jax.sharding import PartitionSpec as P

JACOBI = 8
SWEEPS = 2
THETA = 0.25

BLOCK = 8
SUB = 8
LANES = 128
DEPTH = 4
LOW = -(DEPTH - 1)
HIGH = BLOCK + DEPTH - 1
ROWS = HIGH - LOW
Q_E, P_O, Q_O, UP_O, DN_O, UP_E, DN_E = range(7)
SIG_E, SIG_O, COIL_E, COIL_O, FACE_E, FACE_O = range(6)
F32 = jnp.float32


def tile_index(axis):
    return lax.broadcasted_iota(jnp.int32, (SUB, LANES), axis)


def next_lane(tile):
    return pltpu.roll(tile, LANES - 1, 1)


def prev_lane(tile):
    return pltpu.roll(tile, 1, 1)


def next_sub(tile):
    return pltpu.roll(tile, SUB - 1, 0)


def prev_sub(tile):
    return pltpu.roll(tile, 1, 0)


def to_blocks(tiles):
    lane = tile_index(1)
    out = []
    for r in range(BLOCK):
        order = 8 * (lane % 16) + r
        tile = jnp.take_along_axis(tiles[0], order, axis=1)
        for j in range(1, BLOCK):
            tile = jnp.where(lane // 16 == j, jnp.take_along_axis(tiles[j], order, axis=1), tile)
        out.append(tile)
    return out


def from_blocks(tiles):
    lane = tile_index(1)
    out = []
    for j in range(BLOCK):
        order = 16 * j + lane // 8
        tile = jnp.take_along_axis(tiles[0], order, axis=1)
        for r in range(1, BLOCK):
            tile = jnp.where(lane % 8 == r, jnp.take_along_axis(tiles[r], order, axis=1), tile)
        out.append(tile)
    return out


def put_field(value, scratch, out):
    for j in range(BLOCK):
        scratch[16 * j : 16 * j + 16, :] = value[:, LANES * j : LANES * j + LANES]
    for e in range(2):
        tiles = to_blocks([scratch[pl.ds(16 * j + e, SUB, stride=2), :] for j in range(BLOCK)])
        for r in range(BLOCK):
            out[r, e] = tiles[r]


def harmonic(first_nu, second_nu):
    return 2.0 * first_nu * second_nu / (first_nu + second_nu)


def spread(tiles):
    rows = {}
    for r in range(LOW, HIGH):
        if r < 0:
            rows[r] = prev_lane(tiles[r + BLOCK])
        elif r >= BLOCK:
            rows[r] = next_lane(tiles[r - BLOCK])
        else:
            rows[r] = tiles[r]
    return rows


def flags():
    place = lax.axis_index("space")
    count = lax.axis_size("space")
    return place % 2 == 0, place > 0, place < count - 1


def first_kernel(
    labels_hbm, table_hbm, sigma_hbm, coil_hbm, start_hbm, wave_hbm,
    nu_out, sigma_out, start_out, c_out, r_out, edge_out, scale_out, wave_out,
    labels_ref, table_ref, sigma_ref, coil_ref, start_ref, wave_ref, cur_ref, s0, s1, s2, s3, sems,
):
    copies = [
        pltpu.make_async_copy(source, target, sems.at[i])
        for i, (source, target) in enumerate((
            (table_hbm, table_ref), (labels_hbm, labels_ref), (sigma_hbm, sigma_ref),
            (coil_hbm, coil_ref), (start_hbm, start_ref), (wave_hbm, wave_ref),
        ))
    ]
    for copy in copies:
        copy.start()
    copies[0].wait()
    copies[1].wait()
    labels = labels_ref[...]
    nu = jnp.zeros(labels.shape, F32)
    for material in range(table_ref.shape[0]):
        nu = nu + jnp.where(labels == material, table_ref[material], 0.0)
    put_field(nu, s0, nu_out)
    copies[2].wait()
    put_field(sigma_ref[...], s1, sigma_out)
    copies[3].wait()
    put_field(coil_ref[...], s2, cur_ref)
    copies[4].wait()
    put_field(start_ref[0], s3, start_out)
    copies[5].wait()
    for t in range(wave_ref.shape[0]):
        wave_out[t : t + 1, :] = jnp.full((1, LANES), wave_ref[t], F32)
    coef_kernel(False, nu_out, sigma_out, cur_ref, c_out, r_out, edge_out, scale_out)


def unit_up(r):
    return r % BLOCK in (0, 2, 4, 6)


def unit_down(r):
    return r % BLOCK in (2, 4, 6)


def coef_kernel(neumann, nu_ref, sigma_ref, coil_ref, c_out, r_out, edge_out, scale_out):
    _, has_left, has_right = flags()
    sub = tile_index(0)
    lane = tile_index(1)
    nu_e = [nu_ref[r, 0] for r in range(BLOCK)]
    nu_o = [nu_ref[r, 1] for r in range(BLOCK)]
    pair = [harmonic(nu_e[r], nu_o[r]) for r in range(BLOCK)]
    cross_o = [jnp.where(sub == SUB - 1, 0.0, harmonic(nu_o[r], next_sub(nu_e[r]))) for r in range(BLOCK)]
    cross_e = [prev_sub(cross_o[r]) for r in range(BLOCK)]

    def upward(nu):
        ups = [harmonic(nu[r], nu[r + 1]) for r in range(BLOCK - 1)]
        ups.append(jnp.where(lane == LANES - 1, 0.0, harmonic(nu[BLOCK - 1], next_lane(nu[0]))))
        downs = [prev_lane(ups[BLOCK - 1])] + ups[:-1]
        return ups, downs

    up_e, dn_e = upward(nu_e)
    up_o, dn_o = upward(nu_o)
    left_kept = jnp.logical_not(has_left) if neumann else True
    right_kept = jnp.logical_not(has_right) if neumann else True
    inv_e, inv_o, sig_e, sig_o = [], [], [], []
    for r in range(BLOCK):
        d_e = sigma_ref[r, 0] + pair[r] + cross_e[r] + up_e[r] + dn_e[r]
        d_o = sigma_ref[r, 1] + pair[r] + cross_o[r] + up_o[r] + dn_o[r]
        if r in (0, BLOCK - 1):
            on_edge = lane == (0 if r == 0 else LANES - 1)
            d_e = d_e + jnp.where(on_edge, 2.0 * nu_e[r], 0.0)
            d_o = d_o + jnp.where(on_edge, 2.0 * nu_o[r], 0.0)
        d_e = d_e + jnp.where((sub == 0) & left_kept, 2.0 * nu_e[r], 0.0)
        d_o = d_o + jnp.where((sub == SUB - 1) & right_kept, 2.0 * nu_o[r], 0.0)
        inv_e.append(1.0 / d_e)
        inv_o.append(1.0 / d_o)
    scale_e, scale_o = [jnp.ones((SUB, LANES), F32)], []
    for r in range(1, BLOCK):
        if unit_down(r):
            scale_e.append(scale_e[r - 1] * (dn_e[r] * inv_e[r]))
        else:
            scale_e.append(scale_e[r - 1] / (up_e[r - 1] * inv_e[r - 1]))
    for r in range(BLOCK):
        scale_o.append(scale_e[r] / (pair[r] * inv_e[r]))
    rec_e = [inv_e[r] / scale_e[r] for r in range(BLOCK)]
    rec_o = [inv_o[r] / scale_o[r] for r in range(BLOCK)]
    around_e = [prev_lane(scale_e[BLOCK - 1])] + scale_e + [next_lane(scale_e[0])]
    around_o = [prev_lane(scale_o[BLOCK - 1])] + scale_o + [next_lane(scale_o[0])]

    def put(out, slot, tiles, needed=lambda r: True):
        rows = spread(tiles)
        for r in range(LOW, HIGH):
            if needed(r):
                out[r - LOW, slot] = rows[r]

    span = range(BLOCK)
    put(c_out, Q_E, [cross_e[r] * prev_sub(scale_o[r]) * rec_e[r] for r in span])
    put(c_out, P_O, [pair[r] * scale_e[r] * rec_o[r] for r in span])
    put(c_out, Q_O, [cross_o[r] * next_sub(scale_e[r]) * rec_o[r] for r in span])
    put(c_out, UP_O, [up_o[r] * around_o[r + 2] * rec_o[r] for r in span])
    put(c_out, DN_O, [dn_o[r] * around_o[r] * rec_o[r] for r in span])
    put(c_out, UP_E, [up_e[r] * around_e[r + 2] * rec_e[r] for r in span], lambda r: not unit_up(r))
    put(c_out, DN_E, [dn_e[r] * around_e[r] * rec_e[r] for r in span], lambda r: not unit_down(r))
    put(r_out, SIG_E, [sigma_ref[r, 0] * inv_e[r] for r in span])
    put(r_out, SIG_O, [sigma_ref[r, 1] * inv_o[r] for r in span])
    if not neumann:
        put(r_out, COIL_E, [coil_ref[r, 0] * rec_e[r] for r in span])
        put(r_out, COIL_O, [coil_ref[r, 1] * rec_o[r] for r in span])
    put(r_out, FACE_E, [jnp.where((sub == 0) & has_left, rec_e[r], 0.0) for r in span])
    put(r_out, FACE_O, [jnp.where((sub == SUB - 1) & has_right, rec_o[r], 0.0) for r in span])
    for r in range(BLOCK):
        if not neumann:
            scale_out[r, 0] = scale_e[r]
            scale_out[r, 1] = scale_o[r]
        edge_out[0, r : r + 1] = 2.0 * nu_e[r][0:1]
        edge_out[1, r : r + 1] = 2.0 * nu_o[r][SUB - 1 : SUB]
        edge_out[2, r : r + 1] = scale_e[r][0:1]
        edge_out[3, r : r + 1] = scale_o[r][SUB - 1 : SUB]


def neumann_coef_kernel(nu_ref, sigma_ref, c_out, r_out, edge_out):
    coef_kernel(True, nu_ref, sigma_ref, None, c_out, r_out, edge_out, None)


def advance(field_e, field_o, rhs, c_ref):
    for turn in range(JACOBI // DEPTH):
        if turn == 0:
            now_e, now_o = field_e, field_o
        else:
            now_e, now_o = haloed(now_e), haloed(now_o)
        for k in range(1, DEPTH + 1):
            new_e, new_o = {}, {}
            for r in range(k - DEPTH, BLOCK + DEPTH - k):
                i = r - LOW
                up = now_e[r + 1] if unit_up(r) else c_ref[i, UP_E] * now_e[r + 1]
                down = now_e[r - 1] if unit_down(r) else c_ref[i, DN_E] * now_e[r - 1]
                new_e[r] = (rhs[r][0] + now_o[r]) + (up + down) + c_ref[i, Q_E] * prev_sub(now_o[r])
                new_o[r] = (
                    (rhs[r][1] + c_ref[i, P_O] * now_e[r])
                    + (c_ref[i, UP_O] * now_o[r + 1] + c_ref[i, DN_O] * now_o[r - 1])
                    + c_ref[i, Q_O] * next_sub(now_e[r])
                )
            now_e, now_o = new_e, new_o
    return now_e, now_o


def haloed(rows):
    out = {r: rows[r] for r in range(BLOCK)}
    for j in range(DEPTH):
        out[j - DEPTH] = prev_lane(rows[BLOCK - DEPTH + j])
        out[BLOCK + j] = next_lane(rows[j])
    return out


def march(start, c_ref, r_ref, wave_ref, left, right, first, last, steps):
    def step(t, carry):
        now_e = haloed(dict(enumerate(carry[:BLOCK])))
        now_o = haloed(dict(enumerate(carry[BLOCK:])))
        rhs = {}
        for r in range(LOW, HIGH):
            i = r - LOW
            b_e = r_ref[i, SIG_E] * now_e[r]
            b_o = r_ref[i, SIG_O] * now_o[r]
            if wave_ref is not None:
                wave = wave_ref[pl.ds(t, 1), :]
                b_e = b_e + r_ref[i, COIL_E] * wave
                b_o = b_o + r_ref[i, COIL_O] * wave
            if left is not None:
                at = pl.ds(t * 3 * BLOCK + BLOCK + r, 1)
                b_e = b_e + r_ref[i, FACE_E] * left[at, :]
                b_o = b_o + r_ref[i, FACE_O] * right[at, :]
            rhs[r] = (b_e, b_o)
        now_e, now_o = advance(now_e, now_o, rhs, c_ref)
        for r in range(BLOCK):
            first[pl.ds(t * BLOCK + r, 1), :] = now_e[r][0:1]
            last[pl.ds(t * BLOCK + r, 1), :] = now_o[r][SUB - 1 : SUB]
        return tuple(now_e[r] for r in range(BLOCK)) + tuple(now_o[r] for r in range(BLOCK))

    return lax.fori_loop(0, steps, step, start, unroll=2)


def put_face(ref, t, tile):
    base = t * 3 * BLOCK
    ref[base : base + BLOCK, :] = prev_lane(tile)
    ref[base + BLOCK : base + 2 * BLOCK, :] = tile
    ref[base + 2 * BLOCK : base + 3 * BLOCK, :] = next_lane(tile)


def at_step(ref, t):
    return ref[t * BLOCK : (t + 1) * BLOCK, :]


def dirichlet_kernel(sweep, steps, *refs):
    if sweep == 0:
        (start_ref, c_ref, r_ref, scale_ref, edge_ref, wave_ref, ends, ev_out, od_out, first, last) = refs
        left = right = None
    else:
        (start_ref, c_ref, r_ref, scale_ref, edge_ref, wave_ref, ev_own, od_own, ev_got, od_got,
         ends, ev_out, od_out, g_right, first, last, left, right, g_left) = refs
    even, _, _ = flags()
    if sweep > 0:
        for t in range(steps):
            ev = THETA * (at_step(ev_own, t) + at_step(ev_got, t))
            od = THETA * (at_step(od_own, t) + at_step(od_got, t))
            at_left = jnp.where(even, od, ev)
            at_right = jnp.where(even, ev, od)
            g_left[t * BLOCK : (t + 1) * BLOCK, :] = at_left
            g_right[t * BLOCK : (t + 1) * BLOCK, :] = at_right
            put_face(left, t, edge_ref[0] * at_left)
            put_face(right, t, edge_ref[1] * at_right)
    start = tuple(start_ref[r, e] / scale_ref[r, e] for e in range(2) for r in range(BLOCK))
    final = march(start, c_ref, r_ref, wave_ref, left, right, first, last, steps)
    for e in range(2):
        for r in range(BLOCK):
            ends[r, e] = final[e * BLOCK + r] * scale_ref[r, e]
    for t in range(steps):
        to_left = edge_ref[2] * at_step(first, t)
        to_right = edge_ref[3] * at_step(last, t)
        if sweep > 0:
            to_left = to_left - at_step(g_left, t)
            to_right = to_right - at_step(g_right, t)
        to_left = edge_ref[0] * to_left
        to_right = edge_ref[1] * to_right
        ev_out[t * BLOCK : (t + 1) * BLOCK, :] = jnp.where(even, to_right, to_left)
        od_out[t * BLOCK : (t + 1) * BLOCK, :] = jnp.where(even, to_left, to_right)


def neumann_kernel(sweep, steps, *refs):
    if sweep + 1 < SWEEPS:
        (c_ref, r_ref, edge_ref, ev_own, od_own, ev_got, od_got, ev_out, od_out, first, last, left, right) = refs
    else:
        (c_ref, r_ref, edge_ref, ev_own, od_own, ev_got, od_got, g_right, mine_out, first_out,
         first, last, left, right, s0, s1) = refs
    even, _, _ = flags()
    for t in range(steps):
        ev = at_step(ev_own, t) + at_step(ev_got, t)
        od = at_step(od_own, t) + at_step(od_got, t)
        put_face(left, t, jnp.where(even, od, ev))
        put_face(right, t, jnp.where(even, ev, od))
    zero = jnp.zeros((SUB, LANES), F32)
    march((zero,) * (2 * BLOCK), c_ref, r_ref, None, left, right, first, last, steps)
    if sweep + 1 < SWEEPS:
        for t in range(steps):
            to_left = edge_ref[2] * at_step(first, t)
            to_right = edge_ref[3] * at_step(last, t)
            ev_out[t * BLOCK : (t + 1) * BLOCK, :] = jnp.where(even, to_right, to_left)
            od_out[t * BLOCK : (t + 1) * BLOCK, :] = jnp.where(even, to_left, to_right)
    else:
        for t in range(steps):
            s0[t * BLOCK : (t + 1) * BLOCK, :] = THETA * (edge_ref[2] * at_step(first, t))
            s1[t * BLOCK : (t + 1) * BLOCK, :] = at_step(g_right, t) + THETA * (edge_ref[3] * at_step(last, t))
        for scratch, out in ((s0, first_out), (s1, mine_out)):
            for half in range(steps // SUB):
                base = half * SUB * BLOCK
                tiles = from_blocks([scratch[pl.ds(base + r, SUB, stride=BLOCK), :] for r in range(BLOCK)])
                for j in range(BLOCK):
                    out[half * SUB : (half + 1) * SUB, j * LANES : (j + 1) * LANES] = tiles[j]


def natural_kernel(ends_ref, out, scratch):
    for e in range(2):
        tiles = from_blocks([ends_ref[r, e] for r in range(BLOCK)])
        for j in range(BLOCK):
            scratch[pl.ds(16 * j + e, SUB, stride=2), :] = tiles[j]
    for j in range(BLOCK):
        out[0, :, LANES * j : LANES * j + LANES] = scratch[16 * j : 16 * j + 16, :]


def join_kernel(mine_ref, got_ref, out):
    _, _, has_right = flags()
    out[...] = jnp.where(has_right, mine_ref[...] + got_ref[...], 0.0)


def call(kernel, name, inputs, outputs, scratch=(), space=pltpu.VMEM):
    single = not isinstance(outputs, list)
    shapes = [jax.ShapeDtypeStruct(s, F32) for s in ([outputs] if single else outputs)]
    result = pl.pallas_call(
        kernel,
        out_shape=shapes,
        in_specs=[pl.BlockSpec(memory_space=space)] * len(inputs),
        out_specs=[pl.BlockSpec(memory_space=pltpu.VMEM)] * len(shapes),
        scratch_shapes=[pltpu.VMEM(s, F32) if isinstance(s, tuple) else s for s in scratch],
        compiler_params=pltpu.CompilerParams(vmem_limit_bytes=6 << 20),
        name=name,
    )(*inputs)
    return result[0] if single else result


def body(start_states, sigma, labels, nu_table, coil, waveform):
    steps = waveform.shape[0]
    columns, rows = sigma.shape
    count = lax.axis_size("space")
    windows = lax.axis_size("tm")
    even_faces = [(i, i ^ 1) for i in range(count)]
    odd_faces = [(i, i + 1 if i % 2 else i - 1) for i in range(1, count - 1)] + [(0, 0), (count - 1, count - 1)]
    field = (BLOCK, 2, SUB, LANES)
    series = (steps * BLOCK, LANES)
    wide = (3 * steps * BLOCK, LANES)
    coefs = [(ROWS, 7, SUB, LANES), (ROWS, 6, SUB, LANES), (4, BLOCK, LANES)]
    nu, sig, state, c_dir, r_dir, edge_dir, scale_dir, wave = call(
        first_kernel, "first",
        [
            pltpu.with_memory_space_constraint(array, pltpu.HBM)
            for array in (labels, nu_table, sigma, coil, start_states, waveform)
        ],
        [field, field, field, coefs[0], coefs[1], coefs[2], field, (steps, LANES)],
        [
            pltpu.VMEM(labels.shape, jnp.int32), pltpu.SMEM(nu_table.shape, F32), sigma.shape, coil.shape,
            start_states.shape, pltpu.SMEM(waveform.shape, F32), field,
        ] + [(128, LANES)] * 4 + [pltpu.SemaphoreType.DMA((6,))],
        space=pltpu.HBM,
    )
    c_neu, r_neu, edge_neu = call(neumann_coef_kernel, "coef_neu", [nu, sig], coefs)

    def swapped(ev, od):
        return lax.ppermute(ev, "space", even_faces), lax.ppermute(od, "space", odd_faces)

    ends, ev, od = call(
        functools.partial(dirichlet_kernel, 0, steps), "dir0",
        [state, c_dir, r_dir, scale_dir, edge_dir, wave], [field, series, series], [series] * 2,
    )
    state = lax.ppermute(ends, "tm", [(i, (i + 1) % windows) for i in range(windows)])
    ev_got, od_got = swapped(ev, od)
    ev, od = call(
        functools.partial(neumann_kernel, 0, steps), "neu0",
        [c_neu, r_neu, edge_neu, ev, od, ev_got, od_got], [series] * 2, [series] * 2 + [wide] * 2,
    )
    ev_got, od_got = swapped(ev, od)
    ends, ev, od, g_right = call(
        functools.partial(dirichlet_kernel, 1, steps), "dir1",
        [state, c_dir, r_dir, scale_dir, edge_dir, wave, ev, od, ev_got, od_got],
        [field, series, series, series], [series] * 2 + [wide] * 2 + [series],
    )
    ev_got, od_got = swapped(ev, od)
    end_states = call(natural_kernel, "natural", [ends], (1, columns, rows), [(128, LANES)])
    mine, first = call(
        functools.partial(neumann_kernel, 1, steps), "neu1",
        [c_neu, r_neu, edge_neu, ev, od, ev_got, od_got, g_right],
        [(steps, rows)] * 2, [series] * 2 + [wide] * 2 + [series] * 2,
    )
    got = lax.ppermute(first, "space", [(i, i - 1) for i in range(1, count)])
    traces = call(join_kernel, "join", [mine, got], (steps, rows))
    return end_states, traces


def solution(mesh):
    placed = (
        P("tm", "space", None),
        P("space", None),
        P("space", None),
        P(),
        P("space", None),
        P("tm"),
    )
    return jax.shard_map(
        body,
        mesh=mesh,
        in_specs=placed,
        out_specs=(P("tm", "space", None), P("tm", "space")),
        check_vma=False,
    )
```

```python
import functools

import jax
import jax.numpy as jnp
from jax import lax
from jax.experimental import pallas as pl
from jax.experimental.pallas import tpu as pltpu
from jax.sharding import PartitionSpec as P

JACOBI = 8
SWEEPS = 2
THETA = 0.25

BLOCK = 8
SUB = 8
LANES = 128
DEPTH = 4
LOW = -(DEPTH - 1)
HIGH = BLOCK + DEPTH - 1
ROWS = HIGH - LOW
Q_E, P_O, Q_O, UP_O, DN_O, UP_E, DN_E = range(7)
SIG_E, SIG_O, COIL_E, COIL_O, FACE_E, FACE_O = range(6)
F32 = jnp.float32


def tile_index(axis):
    return lax.broadcasted_iota(jnp.int32, (SUB, LANES), axis)


def next_lane(tile):
    return pltpu.roll(tile, LANES - 1, 1)


def prev_lane(tile):
    return pltpu.roll(tile, 1, 1)


def next_sub(tile):
    return pltpu.roll(tile, SUB - 1, 0)


def prev_sub(tile):
    return pltpu.roll(tile, 1, 0)


def to_blocks(tiles):
    lane = tile_index(1)
    out = []
    for r in range(BLOCK):
        order = 8 * (lane % 16) + r
        tile = jnp.take_along_axis(tiles[0], order, axis=1)
        for j in range(1, BLOCK):
            tile = jnp.where(lane // 16 == j, jnp.take_along_axis(tiles[j], order, axis=1), tile)
        out.append(tile)
    return out


def from_blocks(tiles):
    lane = tile_index(1)
    out = []
    for j in range(BLOCK):
        order = 16 * j + lane // 8
        tile = jnp.take_along_axis(tiles[0], order, axis=1)
        for r in range(1, BLOCK):
            tile = jnp.where(lane % 8 == r, jnp.take_along_axis(tiles[r], order, axis=1), tile)
        out.append(tile)
    return out


def put_field(value, scratch, out):
    for j in range(BLOCK):
        scratch[16 * j : 16 * j + 16, :] = value[:, LANES * j : LANES * j + LANES]
    for e in range(2):
        tiles = to_blocks([scratch[pl.ds(16 * j + e, SUB, stride=2), :] for j in range(BLOCK)])
        for r in range(BLOCK):
            out[r, e] = tiles[r]


def harmonic(first_nu, second_nu):
    return 2.0 * first_nu * second_nu / (first_nu + second_nu)


def spread(tiles):
    rows = {}
    for r in range(LOW, HIGH):
        if r < 0:
            rows[r] = prev_lane(tiles[r + BLOCK])
        elif r >= BLOCK:
            rows[r] = next_lane(tiles[r - BLOCK])
        else:
            rows[r] = tiles[r]
    return rows


def flags():
    place = lax.axis_index("space")
    count = lax.axis_size("space")
    return place % 2 == 0, place > 0, place < count - 1


def first_kernel(
    labels_hbm, table_hbm, sigma_hbm, coil_hbm, start_hbm, wave_hbm,
    nu_out, sigma_out, start_out, c_out, r_out, edge_out, scale_out, wave_out,
    labels_ref, table_ref, sigma_ref, coil_ref, start_ref, wave_ref, cur_ref, s0, s1, s2, s3, sems,
):
    copies = [
        pltpu.make_async_copy(source, target, sems.at[i])
        for i, (source, target) in enumerate((
            (table_hbm, table_ref), (labels_hbm, labels_ref), (sigma_hbm, sigma_ref),
            (coil_hbm, coil_ref), (start_hbm, start_ref), (wave_hbm, wave_ref),
        ))
    ]
    for copy in copies:
        copy.start()
    copies[0].wait()
    copies[1].wait()
    labels = labels_ref[...]
    nu = jnp.zeros(labels.shape, F32)
    for material in range(table_ref.shape[0]):
        nu = nu + jnp.where(labels == material, table_ref[material], 0.0)
    put_field(nu, s0, nu_out)
    copies[2].wait()
    put_field(sigma_ref[...], s1, sigma_out)
    copies[3].wait()
    put_field(coil_ref[...], s2, cur_ref)
    copies[4].wait()
    put_field(start_ref[0], s3, start_out)
    copies[5].wait()
    for t in range(wave_ref.shape[0]):
        wave_out[t : t + 1, :] = jnp.full((1, LANES), wave_ref[t], F32)
    coef_kernel(False, nu_out, sigma_out, cur_ref, c_out, r_out, edge_out, scale_out)


def unit_up(r):
    return r % BLOCK in (0, 2, 4, 6)


def unit_down(r):
    return r % BLOCK in (2, 4, 6)


def coef_kernel(neumann, nu_ref, sigma_ref, coil_ref, c_out, r_out, edge_out, scale_out):
    _, has_left, has_right = flags()
    sub = tile_index(0)
    lane = tile_index(1)
    nu_e = [nu_ref[r, 0] for r in range(BLOCK)]
    nu_o = [nu_ref[r, 1] for r in range(BLOCK)]
    pair = [harmonic(nu_e[r], nu_o[r]) for r in range(BLOCK)]
    cross_o = [jnp.where(sub == SUB - 1, 0.0, harmonic(nu_o[r], next_sub(nu_e[r]))) for r in range(BLOCK)]
    cross_e = [prev_sub(cross_o[r]) for r in range(BLOCK)]

    def upward(nu):
        ups = [harmonic(nu[r], nu[r + 1]) for r in range(BLOCK - 1)]
        ups.append(jnp.where(lane == LANES - 1, 0.0, harmonic(nu[BLOCK - 1], next_lane(nu[0]))))
        downs = [prev_lane(ups[BLOCK - 1])] + ups[:-1]
        return ups, downs

    up_e, dn_e = upward(nu_e)
    up_o, dn_o = upward(nu_o)
    left_kept = jnp.logical_not(has_left) if neumann else True
    right_kept = jnp.logical_not(has_right) if neumann else True
    inv_e, inv_o, sig_e, sig_o = [], [], [], []
    for r in range(BLOCK):
        d_e = sigma_ref[r, 0] + pair[r] + cross_e[r] + up_e[r] + dn_e[r]
        d_o = sigma_ref[r, 1] + pair[r] + cross_o[r] + up_o[r] + dn_o[r]
        if r in (0, BLOCK - 1):
            on_edge = lane == (0 if r == 0 else LANES - 1)
            d_e = d_e + jnp.where(on_edge, 2.0 * nu_e[r], 0.0)
            d_o = d_o + jnp.where(on_edge, 2.0 * nu_o[r], 0.0)
        d_e = d_e + jnp.where((sub == 0) & left_kept, 2.0 * nu_e[r], 0.0)
        d_o = d_o + jnp.where((sub == SUB - 1) & right_kept, 2.0 * nu_o[r], 0.0)
        inv_e.append(1.0 / d_e)
        inv_o.append(1.0 / d_o)
    scale_e, scale_o = [jnp.ones((SUB, LANES), F32)], []
    for r in range(1, BLOCK):
        if unit_down(r):
            scale_e.append(scale_e[r - 1] * (dn_e[r] * inv_e[r]))
        else:
            scale_e.append(scale_e[r - 1] / (up_e[r - 1] * inv_e[r - 1]))
    for r in range(BLOCK):
        scale_o.append(scale_e[r] / (pair[r] * inv_e[r]))
    rec_e = [inv_e[r] / scale_e[r] for r in range(BLOCK)]
    rec_o = [inv_o[r] / scale_o[r] for r in range(BLOCK)]
    around_e = [prev_lane(scale_e[BLOCK - 1])] + scale_e + [next_lane(scale_e[0])]
    around_o = [prev_lane(scale_o[BLOCK - 1])] + scale_o + [next_lane(scale_o[0])]

    def put(out, slot, tiles, needed=lambda r: True):
        rows = spread(tiles)
        for r in range(LOW, HIGH):
            if needed(r):
                out[r - LOW, slot] = rows[r]

    span = range(BLOCK)
    put(c_out, Q_E, [cross_e[r] * prev_sub(scale_o[r]) * rec_e[r] for r in span])
    put(c_out, P_O, [pair[r] * scale_e[r] * rec_o[r] for r in span])
    put(c_out, Q_O, [cross_o[r] * next_sub(scale_e[r]) * rec_o[r] for r in span])
    put(c_out, UP_O, [up_o[r] * around_o[r + 2] * rec_o[r] for r in span])
    put(c_out, DN_O, [dn_o[r] * around_o[r] * rec_o[r] for r in span])
    put(c_out, UP_E, [up_e[r] * around_e[r + 2] * rec_e[r] for r in span], lambda r: not unit_up(r))
    put(c_out, DN_E, [dn_e[r] * around_e[r] * rec_e[r] for r in span], lambda r: not unit_down(r))
    put(r_out, SIG_E, [sigma_ref[r, 0] * inv_e[r] for r in span])
    put(r_out, SIG_O, [sigma_ref[r, 1] * inv_o[r] for r in span])
    if not neumann:
        put(r_out, COIL_E, [coil_ref[r, 0] * rec_e[r] for r in span])
        put(r_out, COIL_O, [coil_ref[r, 1] * rec_o[r] for r in span])
    put(r_out, FACE_E, [jnp.where((sub == 0) & has_left, rec_e[r], 0.0) for r in span])
    put(r_out, FACE_O, [jnp.where((sub == SUB - 1) & has_right, rec_o[r], 0.0) for r in span])
    for r in range(BLOCK):
        if not neumann:
            scale_out[r, 0] = scale_e[r]
            scale_out[r, 1] = scale_o[r]
        edge_out[0, r : r + 1] = 2.0 * nu_e[r][0:1]
        edge_out[1, r : r + 1] = 2.0 * nu_o[r][SUB - 1 : SUB]
        edge_out[2, r : r + 1] = scale_e[r][0:1]
        edge_out[3, r : r + 1] = scale_o[r][SUB - 1 : SUB]


def neumann_coef_kernel(nu_ref, sigma_ref, c_out, r_out, edge_out):
    coef_kernel(True, nu_ref, sigma_ref, None, c_out, r_out, edge_out, None)


def advance(field_e, field_o, rhs, c_ref):
    for turn in range(JACOBI // DEPTH):
        if turn == 0:
            now_e, now_o = field_e, field_o
        else:
            now_e, now_o = haloed(now_e), haloed(now_o)
        for k in range(1, DEPTH + 1):
            new_e, new_o = {}, {}
            for r in range(k - DEPTH, BLOCK + DEPTH - k):
                i = r - LOW
                up = now_e[r + 1] if unit_up(r) else c_ref[i, UP_E] * now_e[r + 1]
                down = now_e[r - 1] if unit_down(r) else c_ref[i, DN_E] * now_e[r - 1]
                new_e[r] = (rhs[r][0] + now_o[r]) + (up + down) + c_ref[i, Q_E] * prev_sub(now_o[r])
                new_o[r] = (
                    (rhs[r][1] + c_ref[i, P_O] * now_e[r])
                    + (c_ref[i, UP_O] * now_o[r + 1] + c_ref[i, DN_O] * now_o[r - 1])
                    + c_ref[i, Q_O] * next_sub(now_e[r])
                )
            now_e, now_o = new_e, new_o
    return now_e, now_o


def haloed(rows):
    out = {r: rows[r] for r in range(BLOCK)}
    for j in range(DEPTH):
        out[j - DEPTH] = prev_lane(rows[BLOCK - DEPTH + j])
        out[BLOCK + j] = next_lane(rows[j])
    return out


def march(start, c_ref, r_ref, wave_ref, left, right, first, last, steps):
    def step(t, carry):
        now_e = haloed(dict(enumerate(carry[:BLOCK])))
        now_o = haloed(dict(enumerate(carry[BLOCK:])))
        rhs = {}
        for r in range(LOW, HIGH):
            i = r - LOW
            b_e = r_ref[i, SIG_E] * now_e[r]
            b_o = r_ref[i, SIG_O] * now_o[r]
            if wave_ref is not None:
                wave = wave_ref[pl.ds(t, 1), :]
                b_e = b_e + r_ref[i, COIL_E] * wave
                b_o = b_o + r_ref[i, COIL_O] * wave
            if left is not None:
                at = pl.ds(t * 3 * BLOCK + BLOCK + r, 1)
                b_e = b_e + r_ref[i, FACE_E] * left[at, :]
                b_o = b_o + r_ref[i, FACE_O] * right[at, :]
            rhs[r] = (b_e, b_o)
        now_e, now_o = advance(now_e, now_o, rhs, c_ref)
        for r in range(BLOCK):
            first[pl.ds(t * BLOCK + r, 1), :] = now_e[r][0:1]
            last[pl.ds(t * BLOCK + r, 1), :] = now_o[r][SUB - 1 : SUB]
        return tuple(now_e[r] for r in range(BLOCK)) + tuple(now_o[r] for r in range(BLOCK))

    return lax.fori_loop(0, steps, step, start, unroll=2)


def put_face(ref, t, tile):
    base = t * 3 * BLOCK
    ref[base : base + BLOCK, :] = prev_lane(tile)
    ref[base + BLOCK : base + 2 * BLOCK, :] = tile
    ref[base + 2 * BLOCK : base + 3 * BLOCK, :] = next_lane(tile)


def at_step(ref, t):
    return ref[t * BLOCK : (t + 1) * BLOCK, :]


def dirichlet_kernel(sweep, steps, *refs):
    if sweep == 0:
        (start_ref, c_ref, r_ref, scale_ref, edge_ref, wave_ref, ends, ev_out, od_out, first, last) = refs
        left = right = None
    else:
        (start_ref, c_ref, r_ref, scale_ref, edge_ref, wave_ref, ev_own, od_own, ev_got, od_got,
         ends, ev_out, od_out, g_right, first, last, left, right, g_left) = refs
    even, _, _ = flags()
    if sweep > 0:
        for t in range(steps):
            ev = THETA * (at_step(ev_own, t) + at_step(ev_got, t))
            od = THETA * (at_step(od_own, t) + at_step(od_got, t))
            at_left = jnp.where(even, od, ev)
            at_right = jnp.where(even, ev, od)
            g_left[t * BLOCK : (t + 1) * BLOCK, :] = at_left
            g_right[t * BLOCK : (t + 1) * BLOCK, :] = at_right
            put_face(left, t, edge_ref[0] * at_left)
            put_face(right, t, edge_ref[1] * at_right)
    start = tuple(start_ref[r, e] / scale_ref[r, e] for e in range(2) for r in range(BLOCK))
    final = march(start, c_ref, r_ref, wave_ref, left, right, first, last, steps)
    for e in range(2):
        for r in range(BLOCK):
            ends[r, e] = final[e * BLOCK + r] * scale_ref[r, e]
    for t in range(steps):
        to_left = edge_ref[2] * at_step(first, t)
        to_right = edge_ref[3] * at_step(last, t)
        if sweep > 0:
            to_left = to_left - at_step(g_left, t)
            to_right = to_right - at_step(g_right, t)
        to_left = edge_ref[0] * to_left
        to_right = edge_ref[1] * to_right
        ev_out[t * BLOCK : (t + 1) * BLOCK, :] = jnp.where(even, to_right, to_left)
        od_out[t * BLOCK : (t + 1) * BLOCK, :] = jnp.where(even, to_left, to_right)


def neumann_kernel(sweep, steps, *refs):
    if sweep + 1 < SWEEPS:
        (c_ref, r_ref, edge_ref, ev_own, od_own, ev_got, od_got, ev_out, od_out, first, last, left, right) = refs
    else:
        (c_ref, r_ref, edge_ref, ev_own, od_own, ev_got, od_got, g_right, mine_out, first_out,
         first, last, left, right, s0, s1) = refs
    even, _, _ = flags()
    for t in range(steps):
        ev = at_step(ev_own, t) + at_step(ev_got, t)
        od = at_step(od_own, t) + at_step(od_got, t)
        put_face(left, t, jnp.where(even, od, ev))
        put_face(right, t, jnp.where(even, ev, od))
    zero = jnp.zeros((SUB, LANES), F32)
    march((zero,) * (2 * BLOCK), c_ref, r_ref, None, left, right, first, last, steps)
    if sweep + 1 < SWEEPS:
        for t in range(steps):
            to_left = edge_ref[2] * at_step(first, t)
            to_right = edge_ref[3] * at_step(last, t)
            ev_out[t * BLOCK : (t + 1) * BLOCK, :] = jnp.where(even, to_right, to_left)
            od_out[t * BLOCK : (t + 1) * BLOCK, :] = jnp.where(even, to_left, to_right)
    else:
        for t in range(steps):
            s0[t * BLOCK : (t + 1) * BLOCK, :] = THETA * (edge_ref[2] * at_step(first, t))
            s1[t * BLOCK : (t + 1) * BLOCK, :] = at_step(g_right, t) + THETA * (edge_ref[3] * at_step(last, t))
        for scratch, out in ((s0, first_out), (s1, mine_out)):
            for half in range(steps // SUB):
                base = half * SUB * BLOCK
                tiles = from_blocks([scratch[pl.ds(base + r, SUB, stride=BLOCK), :] for r in range(BLOCK)])
                for j in range(BLOCK):
                    out[half * SUB : (half + 1) * SUB, j * LANES : (j + 1) * LANES] = tiles[j]


def natural_kernel(ends_ref, out, scratch):
    for e in range(2):
        tiles = from_blocks([ends_ref[r, e] for r in range(BLOCK)])
        for j in range(BLOCK):
            scratch[pl.ds(16 * j + e, SUB, stride=2), :] = tiles[j]
    for j in range(BLOCK):
        out[0, :, LANES * j : LANES * j + LANES] = scratch[16 * j : 16 * j + 16, :]


def join_kernel(mine_ref, ev_ref, od_ref, out):
    even, _, has_right = flags()
    out[...] = jnp.where(has_right, mine_ref[...] + jnp.where(even, ev_ref[...], od_ref[...]), 0.0)


def call(kernel, name, inputs, outputs, scratch=(), space=pltpu.VMEM):
    single = not isinstance(outputs, list)
    shapes = [jax.ShapeDtypeStruct(s, F32) for s in ([outputs] if single else outputs)]
    result = pl.pallas_call(
        kernel,
        out_shape=shapes,
        in_specs=[pl.BlockSpec(memory_space=space)] * len(inputs),
        out_specs=[pl.BlockSpec(memory_space=pltpu.VMEM)] * len(shapes),
        scratch_shapes=[pltpu.VMEM(s, F32) if isinstance(s, tuple) else s for s in scratch],
        compiler_params=pltpu.CompilerParams(vmem_limit_bytes=6 << 20),
        name=name,
    )(*inputs)
    return result[0] if single else result


def body(start_states, sigma, labels, nu_table, coil, waveform):
    steps = waveform.shape[0]
    columns, rows = sigma.shape
    count = lax.axis_size("space")
    windows = lax.axis_size("tm")
    even_faces = [(i, i ^ 1) for i in range(count)]
    odd_faces = []
    for w in range(windows):
        for i in range(count):
            inner = 0 < i < count - 1
            partner = (w, i + 1 if i % 2 else i - 1) if inner else (w ^ 1, i)
            odd_faces.append((w * count + i, partner[0] * count + partner[1]))
    field = (BLOCK, 2, SUB, LANES)
    series = (steps * BLOCK, LANES)
    wide = (3 * steps * BLOCK, LANES)
    coefs = [(ROWS, 7, SUB, LANES), (ROWS, 6, SUB, LANES), (4, BLOCK, LANES)]
    nu, sig, state, c_dir, r_dir, edge_dir, scale_dir, wave = call(
        first_kernel, "first",
        [
            pltpu.with_memory_space_constraint(array, pltpu.HBM)
            for array in (labels, nu_table, sigma, coil, start_states, waveform)
        ],
        [field, field, field, coefs[0], coefs[1], coefs[2], field, (steps, LANES)],
        [
            pltpu.VMEM(labels.shape, jnp.int32), pltpu.SMEM(nu_table.shape, F32), sigma.shape, coil.shape,
            start_states.shape, pltpu.SMEM(waveform.shape, F32), field,
        ] + [(128, LANES)] * 4 + [pltpu.SemaphoreType.DMA((6,))],
        space=pltpu.HBM,
    )
    c_neu, r_neu, edge_neu = call(neumann_coef_kernel, "coef_neu", [nu, sig], coefs)

    def swapped(ev, od):
        return lax.ppermute(ev, "space", even_faces), lax.ppermute(od, ("tm", "space"), odd_faces)

    ends, ev, od = call(
        functools.partial(dirichlet_kernel, 0, steps), "dir0",
        [state, c_dir, r_dir, scale_dir, edge_dir, wave], [field, series, series], [series] * 2,
    )
    state = lax.ppermute(ends, "tm", [(i, (i + 1) % windows) for i in range(windows)])
    ev_got, od_got = swapped(ev, od)
    ev, od = call(
        functools.partial(neumann_kernel, 0, steps), "neu0",
        [c_neu, r_neu, edge_neu, ev, od, ev_got, od_got], [series] * 2, [series] * 2 + [wide] * 2,
    )
    ev_got, od_got = swapped(ev, od)
    ends, ev, od, g_right = call(
        functools.partial(dirichlet_kernel, 1, steps), "dir1",
        [state, c_dir, r_dir, scale_dir, edge_dir, wave, ev, od, ev_got, od_got],
        [field, series, series, series], [series] * 2 + [wide] * 2 + [series],
    )
    ev_got, od_got = swapped(ev, od)
    end_states = call(natural_kernel, "natural", [ends], (1, columns, rows), [(128, LANES)])
    mine, first = call(
        functools.partial(neumann_kernel, 1, steps), "neu1",
        [c_neu, r_neu, edge_neu, ev, od, ev_got, od_got, g_right],
        [(steps, rows)] * 2, [series] * 2 + [wide] * 2 + [series] * 2,
    )
    ev_got, od_got = swapped(first, first)
    traces = call(join_kernel, "join", [mine, ev_got, od_got], (steps, rows))
    return end_states, traces


def solution(mesh):
    placed = (
        P("tm", "space", None),
        P("space", None),
        P("space", None),
        P(),
        P("space", None),
        P("tm"),
    )
    return jax.shard_map(
        body,
        mesh=mesh,
        in_specs=placed,
        out_specs=(P("tm", "space", None), P("tm", "space")),
        check_vma=False,
    )
```

```python
import functools

import jax
import jax.numpy as jnp
from jax import lax
from jax.experimental import pallas as pl
from jax.experimental.pallas import tpu as pltpu
from jax.sharding import PartitionSpec as P

JACOBI = 8
SWEEPS = 2
THETA = 0.25

BLOCK = 8
SUB = 8
LANES = 128
DEPTH = 4
LOW = -(DEPTH - 1)
HIGH = BLOCK + DEPTH - 1
ROWS = HIGH - LOW
Q_E, P_O, Q_O, UP_O, DN_O, UP_E, DN_E = range(7)
SIG_E, SIG_O, COIL_E, COIL_O, FACE_E, FACE_O = range(6)
F32 = jnp.float32


def tile_index(axis):
    return lax.broadcasted_iota(jnp.int32, (SUB, LANES), axis)


def next_lane(tile):
    return pltpu.roll(tile, LANES - 1, 1)


def prev_lane(tile):
    return pltpu.roll(tile, 1, 1)


def next_sub(tile):
    return pltpu.roll(tile, SUB - 1, 0)


def prev_sub(tile):
    return pltpu.roll(tile, 1, 0)


def swap_groups(tiles):
    group = tile_index(1) // 16
    for bit in (1, 2, 4):
        low = (group & bit) == 0
        new = []
        for j, tile in enumerate(tiles):
            other = tiles[j ^ bit]
            if j & bit:
                new.append(jnp.where(low, pltpu.roll(other, LANES - 16 * bit, 1), tile))
            else:
                new.append(jnp.where(low, tile, pltpu.roll(other, 16 * bit, 1)))
        tiles = new
    return tiles


def to_blocks(tiles):
    lane = tile_index(1)
    order = 8 * (lane % 16) + lane // 16
    return swap_groups([jnp.take_along_axis(tile, order, axis=1) for tile in tiles])


def from_blocks(tiles):
    lane = tile_index(1)
    order = 16 * (lane % 8) + lane // 8
    return [jnp.take_along_axis(tile, order, axis=1) for tile in swap_groups(tiles)]


def put_field(value, scratch, out):
    for j in range(BLOCK):
        scratch[16 * j : 16 * j + 16, :] = value[:, LANES * j : LANES * j + LANES]
    for e in range(2):
        tiles = to_blocks([scratch[pl.ds(16 * j + e, SUB, stride=2), :] for j in range(BLOCK)])
        for r in range(BLOCK):
            out[r, e] = tiles[r]


def harmonic(first_nu, second_nu):
    return 2.0 * first_nu * second_nu / (first_nu + second_nu)


def spread(tiles):
    rows = {}
    for r in range(LOW, HIGH):
        if r < 0:
            rows[r] = prev_lane(tiles[r + BLOCK])
        elif r >= BLOCK:
            rows[r] = next_lane(tiles[r - BLOCK])
        else:
            rows[r] = tiles[r]
    return rows


def flags():
    place = lax.axis_index("space")
    count = lax.axis_size("space")
    return place % 2 == 0, place > 0, place < count - 1


def first_kernel(
    labels_hbm, table_hbm, sigma_hbm, coil_hbm, start_hbm, wave_hbm,
    nu_out, sigma_out, start_out, c_out, r_out, edge_out, scale_out, wave_out,
    labels_ref, table_ref, sigma_ref, coil_ref, start_ref, wave_ref, cur_ref, s0, s1, s2, s3, sems,
):
    copies = [
        pltpu.make_async_copy(source, target, sems.at[i])
        for i, (source, target) in enumerate((
            (table_hbm, table_ref), (labels_hbm, labels_ref), (sigma_hbm, sigma_ref),
            (coil_hbm, coil_ref), (start_hbm, start_ref), (wave_hbm, wave_ref),
        ))
    ]
    for copy in copies:
        copy.start()
    for copy in copies:
        copy.wait()
    labels = labels_ref[...]
    nu = jnp.zeros(labels.shape, F32)
    for material in range(table_ref.shape[0]):
        nu = nu + jnp.where(labels == material, table_ref[material], 0.0)
    put_field(nu, s0, nu_out)
    put_field(sigma_ref[...], s1, sigma_out)
    put_field(coil_ref[...], s2, cur_ref)
    put_field(start_ref[0], s3, start_out)
    for t in range(wave_ref.shape[0]):
        wave_out[t : t + 1, :] = jnp.full((1, LANES), wave_ref[t], F32)
    coef_kernel(False, nu_out, sigma_out, cur_ref, c_out, r_out, edge_out, scale_out)


def unit_up(r):
    return r % BLOCK in (0, 2, 4, 6)


def unit_down(r):
    return r % BLOCK in (2, 4, 6)


def coef_kernel(neumann, nu_ref, sigma_ref, coil_ref, c_out, r_out, edge_out, scale_out):
    _, has_left, has_right = flags()
    sub = tile_index(0)
    lane = tile_index(1)
    nu_e = [nu_ref[r, 0] for r in range(BLOCK)]
    nu_o = [nu_ref[r, 1] for r in range(BLOCK)]
    pair = [harmonic(nu_e[r], nu_o[r]) for r in range(BLOCK)]
    cross_o = [jnp.where(sub == SUB - 1, 0.0, harmonic(nu_o[r], next_sub(nu_e[r]))) for r in range(BLOCK)]
    cross_e = [prev_sub(cross_o[r]) for r in range(BLOCK)]

    def upward(nu):
        ups = [harmonic(nu[r], nu[r + 1]) for r in range(BLOCK - 1)]
        ups.append(jnp.where(lane == LANES - 1, 0.0, harmonic(nu[BLOCK - 1], next_lane(nu[0]))))
        downs = [prev_lane(ups[BLOCK - 1])] + ups[:-1]
        return ups, downs

    up_e, dn_e = upward(nu_e)
    up_o, dn_o = upward(nu_o)
    left_kept = jnp.logical_not(has_left) if neumann else True
    right_kept = jnp.logical_not(has_right) if neumann else True
    inv_e, inv_o, sig_e, sig_o = [], [], [], []
    for r in range(BLOCK):
        d_e = sigma_ref[r, 0] + pair[r] + cross_e[r] + up_e[r] + dn_e[r]
        d_o = sigma_ref[r, 1] + pair[r] + cross_o[r] + up_o[r] + dn_o[r]
        if r in (0, BLOCK - 1):
            on_edge = lane == (0 if r == 0 else LANES - 1)
            d_e = d_e + jnp.where(on_edge, 2.0 * nu_e[r], 0.0)
            d_o = d_o + jnp.where(on_edge, 2.0 * nu_o[r], 0.0)
        d_e = d_e + jnp.where((sub == 0) & left_kept, 2.0 * nu_e[r], 0.0)
        d_o = d_o + jnp.where((sub == SUB - 1) & right_kept, 2.0 * nu_o[r], 0.0)
        inv_e.append(1.0 / d_e)
        inv_o.append(1.0 / d_o)
    scale_e, scale_o = [jnp.ones((SUB, LANES), F32)], []
    for r in range(1, BLOCK):
        if unit_down(r):
            scale_e.append(scale_e[r - 1] * (dn_e[r] * inv_e[r]))
        else:
            scale_e.append(scale_e[r - 1] / (up_e[r - 1] * inv_e[r - 1]))
    for r in range(BLOCK):
        scale_o.append(scale_e[r] / (pair[r] * inv_e[r]))
    rec_e = [inv_e[r] / scale_e[r] for r in range(BLOCK)]
    rec_o = [inv_o[r] / scale_o[r] for r in range(BLOCK)]
    around_e = [prev_lane(scale_e[BLOCK - 1])] + scale_e + [next_lane(scale_e[0])]
    around_o = [prev_lane(scale_o[BLOCK - 1])] + scale_o + [next_lane(scale_o[0])]

    def put(out, slot, tiles, needed=lambda r: True):
        rows = spread(tiles)
        for r in range(LOW, HIGH):
            if needed(r):
                out[r - LOW, slot] = rows[r]

    span = range(BLOCK)
    put(c_out, Q_E, [cross_e[r] * prev_sub(scale_o[r]) * rec_e[r] for r in span])
    put(c_out, P_O, [pair[r] * scale_e[r] * rec_o[r] for r in span])
    put(c_out, Q_O, [cross_o[r] * next_sub(scale_e[r]) * rec_o[r] for r in span])
    put(c_out, UP_O, [up_o[r] * around_o[r + 2] * rec_o[r] for r in span])
    put(c_out, DN_O, [dn_o[r] * around_o[r] * rec_o[r] for r in span])
    put(c_out, UP_E, [up_e[r] * around_e[r + 2] * rec_e[r] for r in span], lambda r: not unit_up(r))
    put(c_out, DN_E, [dn_e[r] * around_e[r] * rec_e[r] for r in span], lambda r: not unit_down(r))
    def keep(slot, tiles):
        for r in range(BLOCK):
            r_out[r, slot] = tiles[r]

    keep(SIG_E, [sigma_ref[r, 0] * inv_e[r] for r in span])
    keep(SIG_O, [sigma_ref[r, 1] * inv_o[r] for r in span])
    if not neumann:
        keep(COIL_E, [coil_ref[r, 0] * rec_e[r] for r in span])
        keep(COIL_O, [coil_ref[r, 1] * rec_o[r] for r in span])
    keep(FACE_E, [jnp.where((sub == 0) & has_left, rec_e[r], 0.0) for r in span])
    keep(FACE_O, [jnp.where((sub == SUB - 1) & has_right, rec_o[r], 0.0) for r in span])
    for r in range(BLOCK):
        if not neumann:
            scale_out[r, 0] = scale_e[r]
            scale_out[r, 1] = scale_o[r]
        edge_out[0, r : r + 1] = 2.0 * nu_e[r][0:1]
        edge_out[1, r : r + 1] = 2.0 * nu_o[r][SUB - 1 : SUB]
        edge_out[2, r : r + 1] = scale_e[r][0:1]
        edge_out[3, r : r + 1] = scale_o[r][SUB - 1 : SUB]


def neumann_coef_kernel(nu_ref, sigma_ref, c_out, r_out, edge_out):
    coef_kernel(True, nu_ref, sigma_ref, None, c_out, r_out, edge_out, None)


def advance(field_e, field_o, rhs, c_ref):
    for turn in range(JACOBI // DEPTH):
        if turn == 0:
            now_e, now_o = field_e, field_o
        else:
            now_e, now_o = haloed(now_e), haloed(now_o)
        for k in range(1, DEPTH + 1):
            new_e, new_o = {}, {}
            for r in range(k - DEPTH, BLOCK + DEPTH - k):
                i = r - LOW
                up = now_e[r + 1] if unit_up(r) else c_ref[i, UP_E] * now_e[r + 1]
                down = now_e[r - 1] if unit_down(r) else c_ref[i, DN_E] * now_e[r - 1]
                new_e[r] = (rhs[r][0] + now_o[r]) + (up + down) + c_ref[i, Q_E] * prev_sub(now_o[r])
                new_o[r] = (
                    (rhs[r][1] + c_ref[i, P_O] * now_e[r])
                    + (c_ref[i, UP_O] * now_o[r + 1] + c_ref[i, DN_O] * now_o[r - 1])
                    + c_ref[i, Q_O] * next_sub(now_e[r])
                )
            now_e, now_o = new_e, new_o
    return now_e, now_o


def haloed(rows):
    out = {r: rows[r] for r in range(BLOCK)}
    for j in range(DEPTH):
        out[j - DEPTH] = prev_lane(rows[BLOCK - DEPTH + j])
        out[BLOCK + j] = next_lane(rows[j])
    return out


def march(start, c_ref, r_ref, wave_ref, left, right, first, last, steps):
    def step(t, carry):
        now_e = haloed(dict(enumerate(carry[:BLOCK])))
        now_o = haloed(dict(enumerate(carry[BLOCK:])))
        own = []
        for r in range(BLOCK):
            b_e = r_ref[r, SIG_E] * now_e[r]
            b_o = r_ref[r, SIG_O] * now_o[r]
            if wave_ref is not None:
                wave = wave_ref[pl.ds(t, 1), :]
                b_e = b_e + r_ref[r, COIL_E] * wave
                b_o = b_o + r_ref[r, COIL_O] * wave
            if left is not None:
                at = pl.ds(t * BLOCK + r, 1)
                b_e = b_e + r_ref[r, FACE_E] * left[at, :]
                b_o = b_o + r_ref[r, FACE_O] * right[at, :]
            own.append((b_e, b_o))
        rhs_e = spread([pair[0] for pair in own])
        rhs_o = spread([pair[1] for pair in own])
        rhs = {r: (rhs_e[r], rhs_o[r]) for r in range(LOW, HIGH)}
        now_e, now_o = advance(now_e, now_o, rhs, c_ref)
        for r in range(BLOCK):
            first[pl.ds(t * BLOCK + r, 1), :] = now_e[r][0:1]
            last[pl.ds(t * BLOCK + r, 1), :] = now_o[r][SUB - 1 : SUB]
        return tuple(now_e[r] for r in range(BLOCK)) + tuple(now_o[r] for r in range(BLOCK))

    return lax.fori_loop(0, steps, step, start, unroll=2)


def at_step(ref, t):
    return ref[t * BLOCK : (t + 1) * BLOCK, :]


def dirichlet_kernel(sweep, steps, *refs):
    if sweep == 0:
        (start_ref, c_ref, r_ref, scale_ref, edge_ref, wave_ref, ends, ev_out, od_out, first, last) = refs
        left = right = None
    else:
        (start_ref, c_ref, r_ref, scale_ref, edge_ref, wave_ref, ev_own, od_own, ev_got, od_got,
         ends, ev_out, od_out, g_right, first, last, left, right, g_left) = refs
    even, _, _ = flags()
    if sweep > 0:
        for t in range(steps):
            ev = THETA * (at_step(ev_own, t) + at_step(ev_got, t))
            od = THETA * (at_step(od_own, t) + at_step(od_got, t))
            at_left = jnp.where(even, od, ev)
            at_right = jnp.where(even, ev, od)
            g_left[t * BLOCK : (t + 1) * BLOCK, :] = at_left
            g_right[t * BLOCK : (t + 1) * BLOCK, :] = at_right
            left[t * BLOCK : (t + 1) * BLOCK, :] = edge_ref[0] * at_left
            right[t * BLOCK : (t + 1) * BLOCK, :] = edge_ref[1] * at_right
    start = tuple(start_ref[r, e] / scale_ref[r, e] for e in range(2) for r in range(BLOCK))
    final = march(start, c_ref, r_ref, wave_ref, left, right, first, last, steps)
    for e in range(2):
        for r in range(BLOCK):
            ends[r, e] = final[e * BLOCK + r] * scale_ref[r, e]
    for t in range(steps):
        to_left = edge_ref[2] * at_step(first, t)
        to_right = edge_ref[3] * at_step(last, t)
        if sweep > 0:
            to_left = to_left - at_step(g_left, t)
            to_right = to_right - at_step(g_right, t)
        to_left = edge_ref[0] * to_left
        to_right = edge_ref[1] * to_right
        ev_out[t * BLOCK : (t + 1) * BLOCK, :] = jnp.where(even, to_right, to_left)
        od_out[t * BLOCK : (t + 1) * BLOCK, :] = jnp.where(even, to_left, to_right)


def neumann_kernel(sweep, steps, *refs):
    if sweep + 1 < SWEEPS:
        (c_ref, r_ref, edge_ref, ev_own, od_own, ev_got, od_got, ev_out, od_out, first, last, left, right) = refs
    else:
        (c_ref, r_ref, edge_ref, ev_own, od_own, ev_got, od_got, g_right, mine_out, first_out,
         first, last, left, right, s0, s1) = refs
    even, _, _ = flags()
    for t in range(steps):
        ev = at_step(ev_own, t) + at_step(ev_got, t)
        od = at_step(od_own, t) + at_step(od_got, t)
        left[t * BLOCK : (t + 1) * BLOCK, :] = jnp.where(even, od, ev)
        right[t * BLOCK : (t + 1) * BLOCK, :] = jnp.where(even, ev, od)
    zero = jnp.zeros((SUB, LANES), F32)
    march((zero,) * (2 * BLOCK), c_ref, r_ref, None, left, right, first, last, steps)
    if sweep + 1 < SWEEPS:
        for t in range(steps):
            to_left = edge_ref[2] * at_step(first, t)
            to_right = edge_ref[3] * at_step(last, t)
            ev_out[t * BLOCK : (t + 1) * BLOCK, :] = jnp.where(even, to_right, to_left)
            od_out[t * BLOCK : (t + 1) * BLOCK, :] = jnp.where(even, to_left, to_right)
    else:
        for t in range(steps):
            s0[t * BLOCK : (t + 1) * BLOCK, :] = THETA * (edge_ref[2] * at_step(first, t))
            s1[t * BLOCK : (t + 1) * BLOCK, :] = at_step(g_right, t) + THETA * (edge_ref[3] * at_step(last, t))
        for scratch, out in ((s0, first_out), (s1, mine_out)):
            for half in range(steps // SUB):
                base = half * SUB * BLOCK
                tiles = from_blocks([scratch[pl.ds(base + r, SUB, stride=BLOCK), :] for r in range(BLOCK)])
                for j in range(BLOCK):
                    out[half * SUB : (half + 1) * SUB, j * LANES : (j + 1) * LANES] = tiles[j]


def natural_kernel(ends_ref, out, scratch):
    for e in range(2):
        tiles = from_blocks([ends_ref[r, e] for r in range(BLOCK)])
        for j in range(BLOCK):
            scratch[pl.ds(16 * j + e, SUB, stride=2), :] = tiles[j]
    for j in range(BLOCK):
        out[0, :, LANES * j : LANES * j + LANES] = scratch[16 * j : 16 * j + 16, :]


def join_kernel(mine_ref, ev_ref, od_ref, out):
    even, _, has_right = flags()
    out[...] = jnp.where(has_right, mine_ref[...] + jnp.where(even, ev_ref[...], od_ref[...]), 0.0)


def call(kernel, name, inputs, outputs, scratch=(), space=pltpu.VMEM):
    single = not isinstance(outputs, list)
    shapes = [jax.ShapeDtypeStruct(s, F32) for s in ([outputs] if single else outputs)]
    result = pl.pallas_call(
        kernel,
        out_shape=shapes,
        in_specs=[pl.BlockSpec(memory_space=space)] * len(inputs),
        out_specs=[pl.BlockSpec(memory_space=pltpu.VMEM)] * len(shapes),
        scratch_shapes=[pltpu.VMEM(s, F32) if isinstance(s, tuple) else s for s in scratch],
        compiler_params=pltpu.CompilerParams(vmem_limit_bytes=6 << 20),
        name=name,
    )(*inputs)
    return result[0] if single else result


def body(start_states, sigma, labels, nu_table, coil, waveform):
    steps = waveform.shape[0]
    columns, rows = sigma.shape
    count = lax.axis_size("space")
    windows = lax.axis_size("tm")
    even_faces = [(i, i ^ 1) for i in range(count)]
    odd_faces = []
    for w in range(windows):
        for i in range(count):
            inner = 0 < i < count - 1
            partner = (w, i + 1 if i % 2 else i - 1) if inner else (w ^ 1, i)
            odd_faces.append((w * count + i, partner[0] * count + partner[1]))
    field = (BLOCK, 2, SUB, LANES)
    series = (steps * BLOCK, LANES)
    coefs = [(ROWS, 7, SUB, LANES), (BLOCK, 6, SUB, LANES), (4, BLOCK, LANES)]
    nu, sig, state, c_dir, r_dir, edge_dir, scale_dir, wave = call(
        first_kernel, "first",
        [
            pltpu.with_memory_space_constraint(array, pltpu.HBM)
            for array in (labels, nu_table, sigma, coil, start_states, waveform)
        ],
        [field, field, field, coefs[0], coefs[1], coefs[2], field, (steps, LANES)],
        [
            pltpu.VMEM(labels.shape, jnp.int32), pltpu.SMEM(nu_table.shape, F32), sigma.shape, coil.shape,
            start_states.shape, pltpu.SMEM(waveform.shape, F32), field,
        ] + [(128, LANES)] * 4 + [pltpu.SemaphoreType.DMA((6,))],
        space=pltpu.HBM,
    )
    c_neu, r_neu, edge_neu = call(neumann_coef_kernel, "coef_neu", [nu, sig], coefs)

    def swapped(ev, od):
        return lax.ppermute(ev, "space", even_faces), lax.ppermute(od, ("tm", "space"), odd_faces)

    ends, ev, od = call(
        functools.partial(dirichlet_kernel, 0, steps), "dir0",
        [state, c_dir, r_dir, scale_dir, edge_dir, wave], [field, series, series], [series] * 2,
    )
    state = lax.ppermute(ends, "tm", [(i, (i + 1) % windows) for i in range(windows)])
    ev_got, od_got = swapped(ev, od)
    ev, od = call(
        functools.partial(neumann_kernel, 0, steps), "neu0",
        [c_neu, r_neu, edge_neu, ev, od, ev_got, od_got], [series] * 2, [series] * 2 + [series] * 2,
    )
    ev_got, od_got = swapped(ev, od)
    ends, ev, od, g_right = call(
        functools.partial(dirichlet_kernel, 1, steps), "dir1",
        [state, c_dir, r_dir, scale_dir, edge_dir, wave, ev, od, ev_got, od_got],
        [field, series, series, series], [series] * 2 + [series] * 2 + [series],
    )
    ev_got, od_got = swapped(ev, od)
    end_states = call(natural_kernel, "natural", [ends], (1, columns, rows), [(128, LANES)])
    mine, first = call(
        functools.partial(neumann_kernel, 1, steps), "neu1",
        [c_neu, r_neu, edge_neu, ev, od, ev_got, od_got, g_right],
        [(steps, rows)] * 2, [series] * 2 + [series] * 2 + [series] * 2,
    )
    ev_got, od_got = swapped(first, first)
    traces = call(join_kernel, "join", [mine, ev_got, od_got], (steps, rows))
    return end_states, traces


def solution(mesh):
    placed = (
        P("tm", "space", None),
        P("space", None),
        P("space", None),
        P(),
        P("space", None),
        P("tm"),
    )
    return jax.shard_map(
        body,
        mesh=mesh,
        in_specs=placed,
        out_specs=(P("tm", "space", None), P("tm", "space")),
        check_vma=False,
    )
```

```python
import functools

import jax
import jax.numpy as jnp
from jax import lax
from jax.experimental import pallas as pl
from jax.experimental.pallas import tpu as pltpu
from jax.sharding import PartitionSpec as P

JACOBI = 8
SWEEPS = 2
THETA = 0.25

BLOCK = 8
SUB = 8
LANES = 128
DEPTH = 4
LOW = -(DEPTH - 1)
HIGH = BLOCK + DEPTH - 1
ROWS = HIGH - LOW
Q_E, P_O, Q_O, UP_O, DN_O, UP_E, DN_E = range(7)
COIL_E, COIL_O, FACE_E, FACE_O = range(4)
F32 = jnp.float32
UNROLL = 4


def tile_index(axis):
    return lax.broadcasted_iota(jnp.int32, (SUB, LANES), axis)


def next_lane(tile):
    return pltpu.roll(tile, LANES - 1, 1)


def prev_lane(tile):
    return pltpu.roll(tile, 1, 1)


def next_sub(tile):
    return pltpu.roll(tile, SUB - 1, 0)


def prev_sub(tile):
    return pltpu.roll(tile, 1, 0)


def swap_groups(tiles):
    group = tile_index(1) // 16
    for bit in (1, 2, 4):
        low = (group & bit) == 0
        new = []
        for j, tile in enumerate(tiles):
            other = tiles[j ^ bit]
            if j & bit:
                new.append(jnp.where(low, pltpu.roll(other, LANES - 16 * bit, 1), tile))
            else:
                new.append(jnp.where(low, tile, pltpu.roll(other, 16 * bit, 1)))
        tiles = new
    return tiles


def to_blocks(tiles):
    lane = tile_index(1)
    order = 8 * (lane % 16) + lane // 16
    return swap_groups([jnp.take_along_axis(tile, order, axis=1) for tile in tiles])


def from_blocks(tiles):
    lane = tile_index(1)
    order = 16 * (lane % 8) + lane // 8
    return [jnp.take_along_axis(tile, order, axis=1) for tile in swap_groups(tiles)]


def put_field(value, scratch, out):
    for j in range(BLOCK):
        scratch[16 * j : 16 * j + 16, :] = value[:, LANES * j : LANES * j + LANES]
    for e in range(2):
        tiles = to_blocks([scratch[pl.ds(16 * j + e, SUB, stride=2), :] for j in range(BLOCK)])
        for r in range(BLOCK):
            out[r, e] = tiles[r]


def harmonic(first_nu, second_nu):
    return 2.0 * first_nu * second_nu / (first_nu + second_nu)


def spread(tiles):
    rows = {}
    for r in range(LOW, HIGH):
        if r < 0:
            rows[r] = prev_lane(tiles[r + BLOCK])
        elif r >= BLOCK:
            rows[r] = next_lane(tiles[r - BLOCK])
        else:
            rows[r] = tiles[r]
    return rows


def flags():
    place = lax.axis_index("space")
    count = lax.axis_size("space")
    return place % 2 == 0, place > 0, place < count - 1


def first_kernel(
    labels_hbm, table_hbm, sigma_hbm, coil_hbm, start_hbm, wave_hbm,
    nu_out, sigma_out, start_out, c_out, s_out, r_out, edge_out, scale_out, wave_out,
    labels_ref, table_ref, sigma_ref, coil_ref, start_ref, wave_ref, cur_ref, s0, s1, s2, s3, sems,
):
    copies = [
        pltpu.make_async_copy(source, target, sems.at[i])
        for i, (source, target) in enumerate((
            (table_hbm, table_ref), (labels_hbm, labels_ref), (sigma_hbm, sigma_ref),
            (coil_hbm, coil_ref), (start_hbm, start_ref), (wave_hbm, wave_ref),
        ))
    ]
    for copy in copies:
        copy.start()
    for copy in copies:
        copy.wait()
    labels = labels_ref[...]
    nu = jnp.zeros(labels.shape, F32)
    for material in range(table_ref.shape[0]):
        nu = nu + jnp.where(labels == material, table_ref[material], 0.0)
    put_field(nu, s0, nu_out)
    put_field(sigma_ref[...], s1, sigma_out)
    put_field(coil_ref[...], s2, cur_ref)
    put_field(start_ref[0], s3, start_out)
    for t in range(wave_ref.shape[0]):
        wave_out[t : t + 1, :] = jnp.full((1, LANES), wave_ref[t], F32)
    coef_kernel(False, nu_out, sigma_out, cur_ref, c_out, s_out, r_out, edge_out, scale_out)


def unit_up(r):
    return r % BLOCK in (0, 2, 4, 6)


def unit_down(r):
    return r % BLOCK in (2, 4, 6)


def coef_kernel(neumann, nu_ref, sigma_ref, coil_ref, c_out, s_out, r_out, edge_out, scale_out):
    _, has_left, has_right = flags()
    sub = tile_index(0)
    lane = tile_index(1)
    nu_e = [nu_ref[r, 0] for r in range(BLOCK)]
    nu_o = [nu_ref[r, 1] for r in range(BLOCK)]
    pair = [harmonic(nu_e[r], nu_o[r]) for r in range(BLOCK)]
    cross_o = [jnp.where(sub == SUB - 1, 0.0, harmonic(nu_o[r], next_sub(nu_e[r]))) for r in range(BLOCK)]
    cross_e = [prev_sub(cross_o[r]) for r in range(BLOCK)]

    def upward(nu):
        ups = [harmonic(nu[r], nu[r + 1]) for r in range(BLOCK - 1)]
        ups.append(jnp.where(lane == LANES - 1, 0.0, harmonic(nu[BLOCK - 1], next_lane(nu[0]))))
        downs = [prev_lane(ups[BLOCK - 1])] + ups[:-1]
        return ups, downs

    up_e, dn_e = upward(nu_e)
    up_o, dn_o = upward(nu_o)
    left_kept = jnp.logical_not(has_left) if neumann else True
    right_kept = jnp.logical_not(has_right) if neumann else True
    inv_e, inv_o, sig_e, sig_o = [], [], [], []
    for r in range(BLOCK):
        d_e = sigma_ref[r, 0] + pair[r] + cross_e[r] + up_e[r] + dn_e[r]
        d_o = sigma_ref[r, 1] + pair[r] + cross_o[r] + up_o[r] + dn_o[r]
        if r in (0, BLOCK - 1):
            on_edge = lane == (0 if r == 0 else LANES - 1)
            d_e = d_e + jnp.where(on_edge, 2.0 * nu_e[r], 0.0)
            d_o = d_o + jnp.where(on_edge, 2.0 * nu_o[r], 0.0)
        d_e = d_e + jnp.where((sub == 0) & left_kept, 2.0 * nu_e[r], 0.0)
        d_o = d_o + jnp.where((sub == SUB - 1) & right_kept, 2.0 * nu_o[r], 0.0)
        inv_e.append(1.0 / d_e)
        inv_o.append(1.0 / d_o)
    scale_e, scale_o = [jnp.ones((SUB, LANES), F32)], []
    for r in range(1, BLOCK):
        if unit_down(r):
            scale_e.append(scale_e[r - 1] * (dn_e[r] * inv_e[r]))
        else:
            scale_e.append(scale_e[r - 1] / (up_e[r - 1] * inv_e[r - 1]))
    for r in range(BLOCK):
        scale_o.append(scale_e[r] / (pair[r] * inv_e[r]))
    rec_e = [inv_e[r] / scale_e[r] for r in range(BLOCK)]
    rec_o = [inv_o[r] / scale_o[r] for r in range(BLOCK)]
    around_e = [prev_lane(scale_e[BLOCK - 1])] + scale_e + [next_lane(scale_e[0])]
    around_o = [prev_lane(scale_o[BLOCK - 1])] + scale_o + [next_lane(scale_o[0])]

    def put(out, slot, tiles, needed=lambda r: True):
        rows = spread(tiles)
        for r in range(LOW, HIGH):
            if needed(r):
                out[r - LOW, slot] = rows[r]

    span = range(BLOCK)
    put(c_out, Q_E, [cross_e[r] * prev_sub(scale_o[r]) * rec_e[r] for r in span])
    put(c_out, P_O, [pair[r] * scale_e[r] * rec_o[r] for r in span])
    put(c_out, Q_O, [cross_o[r] * next_sub(scale_e[r]) * rec_o[r] for r in span])
    put(c_out, UP_O, [up_o[r] * around_o[r + 2] * rec_o[r] for r in span])
    put(c_out, DN_O, [dn_o[r] * around_o[r] * rec_o[r] for r in span])
    put(c_out, UP_E, [up_e[r] * around_e[r + 2] * rec_e[r] for r in span], lambda r: not unit_up(r))
    put(c_out, DN_E, [dn_e[r] * around_e[r] * rec_e[r] for r in span], lambda r: not unit_down(r))
    put(s_out, 0, [sigma_ref[r, 0] * inv_e[r] for r in span])
    put(s_out, 1, [sigma_ref[r, 1] * inv_o[r] for r in span])
    if not neumann:
        put(r_out, COIL_E, [coil_ref[r, 0] * rec_e[r] for r in span])
        put(r_out, COIL_O, [coil_ref[r, 1] * rec_o[r] for r in span])
    put(r_out, FACE_E, [jnp.where((sub == 0) & has_left, rec_e[r], 0.0) for r in span])
    put(r_out, FACE_O, [jnp.where((sub == SUB - 1) & has_right, rec_o[r], 0.0) for r in span])
    for r in range(BLOCK):
        if not neumann:
            scale_out[r, 0] = scale_e[r]
            scale_out[r, 1] = scale_o[r]
        edge_out[0, r : r + 1] = 2.0 * nu_e[r][0:1]
        edge_out[1, r : r + 1] = 2.0 * nu_o[r][SUB - 1 : SUB]
        edge_out[2, r : r + 1] = scale_e[r][0:1]
        edge_out[3, r : r + 1] = scale_o[r][SUB - 1 : SUB]


def neumann_coef_kernel(nu_ref, sigma_ref, c_out, s_out, r_out, edge_out):
    coef_kernel(True, nu_ref, sigma_ref, None, c_out, s_out, r_out, edge_out, None)


def advance(field_e, field_o, rhs, c_ref):
    for turn in range(JACOBI // DEPTH):
        if turn == 0:
            now_e, now_o = field_e, field_o
        else:
            now_e, now_o = haloed(now_e), haloed(now_o)
        for k in range(1, DEPTH + 1):
            new_e, new_o = {}, {}
            for r in range(k - DEPTH, BLOCK + DEPTH - k):
                i = r - LOW
                up_e = now_e[r + 1] if unit_up(r) else c_ref[i, UP_E] * now_e[r + 1]
                dn_e = now_e[r - 1] if unit_down(r) else c_ref[i, DN_E] * now_e[r - 1]
                up_o = c_ref[i, UP_O] * now_o[r + 1]
                dn_o = c_ref[i, DN_O] * now_o[r - 1]
                soon_e, late_e = (dn_e, up_e) if 2 * r >= BLOCK else (up_e, dn_e)
                soon_o, late_o = (dn_o, up_o) if 2 * r >= BLOCK else (up_o, dn_o)
                beside_e = now_o[r] + c_ref[i, Q_E] * prev_sub(now_o[r])
                beside_o = c_ref[i, P_O] * now_e[r] + c_ref[i, Q_O] * next_sub(now_e[r])
                new_e[r] = ((rhs[r][0] + soon_e) + beside_e) + late_e
                new_o[r] = ((rhs[r][1] + soon_o) + beside_o) + late_o
            now_e, now_o = new_e, new_o
    return now_e, now_o


def haloed(rows):
    out = {r: rows[r] for r in range(BLOCK)}
    for j in range(DEPTH):
        out[j - DEPTH] = prev_lane(rows[BLOCK - DEPTH + j])
        out[BLOCK + j] = next_lane(rows[j])
    return out


def march(start, c_ref, s_ref, r_ref, wave_ref, left, right, first, last, halo, steps):
    def given_at(t, r):
        f_e = f_o = None
        if wave_ref is not None:
            wave = wave_ref[pl.ds(t, 1), :]
            f_e = r_ref[r - LOW, COIL_E] * wave
            f_o = r_ref[r - LOW, COIL_O] * wave
        if left is not None:
            at = pl.ds(t * BLOCK + r, 1)
            from_left = r_ref[r - LOW, FACE_E] * left[at, :]
            from_right = r_ref[r - LOW, FACE_O] * right[at, :]
            f_e = from_left if f_e is None else f_e + from_left
            f_o = from_right if f_o is None else f_o + from_right
        return f_e, f_o

    halo_rows = [r for r in range(LOW, HIGH) if not 0 <= r < BLOCK]

    def put_halo(t, slot):
        for n, r in enumerate(halo_rows if halo is not None else ()):
            shift = prev_lane if r < 0 else next_lane
            for e, tile in enumerate(given_at(t, r % BLOCK)):
                halo[slot, n, e] = shift(tile)

    def step(t, slot, carry):
        now_e = haloed(dict(enumerate(carry[:BLOCK])))
        now_o = haloed(dict(enumerate(carry[BLOCK:])))
        given = {r: given_at(t, r) for r in range(BLOCK)}
        for n, r in enumerate(halo_rows):
            if halo is not None:
                given[r] = halo[slot, n, 0], halo[slot, n, 1]
            elif left is None:
                given[r] = given_at(t, r)
        rhs = {
            r: (s_ref[r - LOW, 0] * now_e[r] + f_e, s_ref[r - LOW, 1] * now_o[r] + f_o)
            for r, (f_e, f_o) in given.items()
        }
        for r in halo_rows:
            if r not in rhs:
                shift = prev_lane if r < 0 else next_lane
                rhs[r] = shift(rhs[r % BLOCK][0]), shift(rhs[r % BLOCK][1])
        now_e, now_o = advance(now_e, now_o, rhs, c_ref)
        put_halo(jnp.minimum(t + 1, steps - 1), 1 - slot)
        for r in range(BLOCK):
            first[pl.ds(t * BLOCK + r, 1), :] = now_e[r][0:1]
            last[pl.ds(t * BLOCK + r, 1), :] = now_o[r][SUB - 1 : SUB]
        return tuple(now_e[r] for r in range(BLOCK)) + tuple(now_o[r] for r in range(BLOCK))

    def some_steps(i, carry):
        for j in range(UNROLL):
            carry = step(UNROLL * i + j, j % 2, carry)
        return carry

    put_halo(0, 0)
    return lax.fori_loop(0, steps // UNROLL, some_steps, start)


def at_step(ref, t):
    return ref[t * BLOCK : (t + 1) * BLOCK, :]


def dirichlet_kernel(sweep, steps, *refs):
    if sweep == 0:
        (start_ref, c_ref, s_ref, r_ref, scale_ref, edge_ref, wave_ref, ends, ev_out, od_out, first, last) = refs
        halo = None
        left = right = None
    else:
        (start_ref, c_ref, s_ref, r_ref, scale_ref, edge_ref, wave_ref, ev_own, od_own, ev_got, od_got,
         ends, ev_out, od_out, g_right, first, last, left, right, g_left, halo) = refs
    even, _, _ = flags()
    if sweep > 0:
        for t in range(steps):
            ev = THETA * (at_step(ev_own, t) + at_step(ev_got, t))
            od = THETA * (at_step(od_own, t) + at_step(od_got, t))
            at_left = jnp.where(even, od, ev)
            at_right = jnp.where(even, ev, od)
            g_left[t * BLOCK : (t + 1) * BLOCK, :] = at_left
            g_right[t * BLOCK : (t + 1) * BLOCK, :] = at_right
            left[t * BLOCK : (t + 1) * BLOCK, :] = edge_ref[0] * at_left
            right[t * BLOCK : (t + 1) * BLOCK, :] = edge_ref[1] * at_right
    start = tuple(start_ref[r, e] / scale_ref[r, e] for e in range(2) for r in range(BLOCK))
    final = march(start, c_ref, s_ref, r_ref, wave_ref, left, right, first, last, halo, steps)
    for e in range(2):
        for r in range(BLOCK):
            ends[r, e] = final[e * BLOCK + r] * scale_ref[r, e]
    for t in range(steps):
        to_left = edge_ref[2] * at_step(first, t)
        to_right = edge_ref[3] * at_step(last, t)
        if sweep > 0:
            to_left = to_left - at_step(g_left, t)
            to_right = to_right - at_step(g_right, t)
        to_left = edge_ref[0] * to_left
        to_right = edge_ref[1] * to_right
        ev_out[t * BLOCK : (t + 1) * BLOCK, :] = jnp.where(even, to_right, to_left)
        od_out[t * BLOCK : (t + 1) * BLOCK, :] = jnp.where(even, to_left, to_right)


def neumann_kernel(sweep, steps, *refs):
    if sweep + 1 < SWEEPS:
        (c_ref, s_ref, r_ref, edge_ref, ev_own, od_own, ev_got, od_got, ev_out, od_out,
         first, last, left, right) = refs
    else:
        (c_ref, s_ref, r_ref, edge_ref, ev_own, od_own, ev_got, od_got, g_right, mine_out, ev_out, od_out,
         first, last, left, right, s0, s1) = refs
    even, _, _ = flags()
    for t in range(steps):
        ev = at_step(ev_own, t) + at_step(ev_got, t)
        od = at_step(od_own, t) + at_step(od_got, t)
        left[t * BLOCK : (t + 1) * BLOCK, :] = jnp.where(even, od, ev)
        right[t * BLOCK : (t + 1) * BLOCK, :] = jnp.where(even, ev, od)
    zero = jnp.zeros((SUB, LANES), F32)
    march((zero,) * (2 * BLOCK), c_ref, s_ref, r_ref, None, left, right, first, last, None, steps)
    if sweep + 1 < SWEEPS:
        for t in range(steps):
            to_left = edge_ref[2] * at_step(first, t)
            to_right = edge_ref[3] * at_step(last, t)
            ev_out[t * BLOCK : (t + 1) * BLOCK, :] = jnp.where(even, to_right, to_left)
            od_out[t * BLOCK : (t + 1) * BLOCK, :] = jnp.where(even, to_left, to_right)
    else:
        for t in range(steps):
            s0[t * BLOCK : (t + 1) * BLOCK, :] = THETA * (edge_ref[2] * at_step(first, t))
            s1[t * BLOCK : (t + 1) * BLOCK, :] = at_step(g_right, t) + THETA * (edge_ref[3] * at_step(last, t))
        for scratch, outs in ((s0, (ev_out, od_out)), (s1, (mine_out,))):
            for half in range(steps // SUB):
                base = half * SUB * BLOCK
                tiles = from_blocks([scratch[pl.ds(base + r, SUB, stride=BLOCK), :] for r in range(BLOCK)])
                for j in range(BLOCK):
                    for out in outs:
                        out[half * SUB : (half + 1) * SUB, j * LANES : (j + 1) * LANES] = tiles[j]


def natural_kernel(ends_ref, out, scratch):
    for e in range(2):
        tiles = from_blocks([ends_ref[r, e] for r in range(BLOCK)])
        for j in range(BLOCK):
            scratch[pl.ds(16 * j + e, SUB, stride=2), :] = tiles[j]
    for j in range(BLOCK):
        out[0, :, LANES * j : LANES * j + LANES] = scratch[16 * j : 16 * j + 16, :]


def join_kernel(mine_ref, ev_ref, od_ref, out):
    even, _, has_right = flags()
    out[...] = jnp.where(has_right, mine_ref[...] + jnp.where(even, ev_ref[...], od_ref[...]), 0.0)


def call(kernel, name, inputs, outputs, scratch=(), space=pltpu.VMEM):
    single = not isinstance(outputs, list)
    shapes = [jax.ShapeDtypeStruct(s, F32) for s in ([outputs] if single else outputs)]
    result = pl.pallas_call(
        kernel,
        out_shape=shapes,
        in_specs=[pl.BlockSpec(memory_space=space)] * len(inputs),
        out_specs=[pl.BlockSpec(memory_space=pltpu.VMEM)] * len(shapes),
        scratch_shapes=[pltpu.VMEM(s, F32) if isinstance(s, tuple) else s for s in scratch],
        compiler_params=pltpu.CompilerParams(vmem_limit_bytes=6 << 20),
        name=name,
    )(*inputs)
    return result[0] if single else result


def body(start_states, sigma, labels, nu_table, coil, waveform):
    steps = waveform.shape[0]
    columns, rows = sigma.shape
    count = lax.axis_size("space")
    windows = lax.axis_size("tm")
    even_faces = [(i, i ^ 1) for i in range(count)]
    odd_faces = []
    for w in range(windows):
        for i in range(count):
            inner = 0 < i < count - 1
            partner = (w, i + 1 if i % 2 else i - 1) if inner else (w ^ 1, i)
            odd_faces.append((w * count + i, partner[0] * count + partner[1]))
    field = (BLOCK, 2, SUB, LANES)
    series = (steps * BLOCK, LANES)
    halo = (2, ROWS - BLOCK, 2, SUB, LANES)
    coefs = [(ROWS, 7, SUB, LANES), (ROWS, 2, SUB, LANES), (ROWS, 4, SUB, LANES), (4, BLOCK, LANES)]
    nu, sig, state, c_dir, s_dir, r_dir, edge_dir, scale_dir, wave = call(
        first_kernel, "first",
        [
            pltpu.with_memory_space_constraint(array, pltpu.HBM)
            for array in (labels, nu_table, sigma, coil, start_states, waveform)
        ],
        [field, field, field] + coefs + [field, (steps, LANES)],
        [
            pltpu.VMEM(labels.shape, jnp.int32), pltpu.SMEM(nu_table.shape, F32), sigma.shape, coil.shape,
            start_states.shape, pltpu.SMEM(waveform.shape, F32), field,
        ] + [(128, LANES)] * 4 + [pltpu.SemaphoreType.DMA((6,))],
        space=pltpu.HBM,
    )
    c_neu, s_neu, r_neu, edge_neu = call(neumann_coef_kernel, "coef_neu", [nu, sig], coefs)

    def swapped(ev, od):
        return lax.ppermute(ev, "space", even_faces), lax.ppermute(od, ("tm", "space"), odd_faces)

    ends, ev, od = call(
        functools.partial(dirichlet_kernel, 0, steps), "dir0",
        [state, c_dir, s_dir, r_dir, scale_dir, edge_dir, wave], [field, series, series], [series] * 2,
    )
    state = lax.ppermute(ends, "tm", [(i, (i + 1) % windows) for i in range(windows)])
    ev_got, od_got = swapped(ev, od)
    ev, od = call(
        functools.partial(neumann_kernel, 0, steps), "neu0",
        [c_neu, s_neu, r_neu, edge_neu, ev, od, ev_got, od_got], [series] * 2, [series] * 4,
    )
    ev_got, od_got = swapped(ev, od)
    ends, ev, od, g_right = call(
        functools.partial(dirichlet_kernel, 1, steps), "dir1",
        [state, c_dir, s_dir, r_dir, scale_dir, edge_dir, wave, ev, od, ev_got, od_got],
        [field, series, series, series], [series] * 5 + [halo],
    )
    ev_got, od_got = swapped(ev, od)
    end_states = call(natural_kernel, "natural", [ends], (1, columns, rows), [(128, LANES)])
    mine, ev, od = call(
        functools.partial(neumann_kernel, 1, steps), "neu1",
        [c_neu, s_neu, r_neu, edge_neu, ev, od, ev_got, od_got, g_right],
        [(steps, rows)] * 3, [series] * 6,
    )
    ev_got, od_got = swapped(ev, od)
    traces = call(join_kernel, "join", [mine, ev_got, od_got], (steps, rows))
    return end_states, traces


def solution(mesh):
    placed = (
        P("tm", "space", None),
        P("space", None),
        P("space", None),
        P(),
        P("space", None),
        P("tm"),
    )
    return jax.shard_map(
        body,
        mesh=mesh,
        in_specs=placed,
        out_specs=(P("tm", "space", None), P("tm", "space")),
        check_vma=False,
    )
```

```python
import functools

import jax
import jax.numpy as jnp
from jax import lax
from jax.experimental import pallas as pl
from jax.experimental.pallas import tpu as pltpu
from jax.sharding import PartitionSpec as P

JACOBI = 8
SWEEPS = 2
THETA = 0.25

BLOCK = 8
SUB = 8
LANES = 128
DEPTH = 4
LOW = -(DEPTH - 1)
HIGH = BLOCK + DEPTH - 1
ROWS = HIGH - LOW
Q_E, P_O, Q_O, UP_O, DN_O, UP_E, DN_E = range(7)
COIL_E, COIL_O, FACE_E, FACE_O = range(4)
F32 = jnp.float32
UNROLL = 4


def tile_index(axis):
    return lax.broadcasted_iota(jnp.int32, (SUB, LANES), axis)


def next_lane(tile):
    return pltpu.roll(tile, LANES - 1, 1)


def prev_lane(tile):
    return pltpu.roll(tile, 1, 1)


def next_sub(tile):
    return pltpu.roll(tile, SUB - 1, 0)


def prev_sub(tile):
    return pltpu.roll(tile, 1, 0)


def swap_groups(tiles):
    group = tile_index(1) // 16
    for bit in (1, 2, 4):
        low = (group & bit) == 0
        new = []
        for j, tile in enumerate(tiles):
            other = tiles[j ^ bit]
            if j & bit:
                new.append(jnp.where(low, pltpu.roll(other, LANES - 16 * bit, 1), tile))
            else:
                new.append(jnp.where(low, tile, pltpu.roll(other, 16 * bit, 1)))
        tiles = new
    return tiles


def to_blocks(tiles):
    lane = tile_index(1)
    order = 8 * (lane % 16) + lane // 16
    return swap_groups([jnp.take_along_axis(tile, order, axis=1) for tile in tiles])


def from_blocks(tiles):
    lane = tile_index(1)
    order = 16 * (lane % 8) + lane // 8
    return [jnp.take_along_axis(tile, order, axis=1) for tile in swap_groups(tiles)]


def put_field(value, scratch, out):
    for j in range(BLOCK):
        scratch[16 * j : 16 * j + 16, :] = value[:, LANES * j : LANES * j + LANES]
    for e in range(2):
        tiles = to_blocks([scratch[pl.ds(16 * j + e, SUB, stride=2), :] for j in range(BLOCK)])
        for r in range(BLOCK):
            out[r, e] = tiles[r]


def harmonic(first_nu, second_nu):
    return 2.0 * first_nu * second_nu / (first_nu + second_nu)


def spread(tiles):
    rows = {}
    for r in range(LOW, HIGH):
        if r < 0:
            rows[r] = prev_lane(tiles[r + BLOCK])
        elif r >= BLOCK:
            rows[r] = next_lane(tiles[r - BLOCK])
        else:
            rows[r] = tiles[r]
    return rows


def flags():
    place = lax.axis_index("space")
    count = lax.axis_size("space")
    return place % 2 == 0, place > 0, place < count - 1


def first_kernel(
    labels_hbm, table_hbm, sigma_hbm, coil_hbm, start_hbm, wave_hbm,
    nu_out, sigma_out, start_out, c_out, s_out, r_out, edge_out, scale_out, wave_out,
    labels_ref, table_ref, sigma_ref, coil_ref, start_ref, wave_ref, cur_ref, s0, s1, s2, s3, sems,
):
    copies = [
        pltpu.make_async_copy(source, target, sems.at[i])
        for i, (source, target) in enumerate((
            (table_hbm, table_ref), (labels_hbm, labels_ref), (sigma_hbm, sigma_ref),
            (coil_hbm, coil_ref), (start_hbm, start_ref), (wave_hbm, wave_ref),
        ))
    ]
    for copy in copies:
        copy.start()
    for copy in copies:
        copy.wait()
    labels = labels_ref[...]
    nu = jnp.zeros(labels.shape, F32)
    for material in range(table_ref.shape[0]):
        nu = nu + jnp.where(labels == material, table_ref[material], 0.0)
    put_field(nu, s0, nu_out)
    put_field(sigma_ref[...], s1, sigma_out)
    put_field(coil_ref[...], s2, cur_ref)
    put_field(start_ref[0], s3, start_out)
    for t in range(wave_ref.shape[0]):
        wave_out[t : t + 1, :] = jnp.full((1, LANES), wave_ref[t], F32)
    coef_kernel(False, nu_out, sigma_out, cur_ref, c_out, s_out, r_out, edge_out, scale_out)


def unit_up(r):
    return r % BLOCK in (0, 2, 4, 6)


def unit_down(r):
    return r % BLOCK in (2, 4, 6)


def coef_kernel(neumann, nu_ref, sigma_ref, coil_ref, c_out, s_out, r_out, edge_out, scale_out):
    _, has_left, has_right = flags()
    sub = tile_index(0)
    lane = tile_index(1)
    nu_e = [nu_ref[r, 0] for r in range(BLOCK)]
    nu_o = [nu_ref[r, 1] for r in range(BLOCK)]
    pair = [harmonic(nu_e[r], nu_o[r]) for r in range(BLOCK)]
    cross_o = [jnp.where(sub == SUB - 1, 0.0, harmonic(nu_o[r], next_sub(nu_e[r]))) for r in range(BLOCK)]
    cross_e = [prev_sub(cross_o[r]) for r in range(BLOCK)]

    def upward(nu):
        ups = [harmonic(nu[r], nu[r + 1]) for r in range(BLOCK - 1)]
        ups.append(jnp.where(lane == LANES - 1, 0.0, harmonic(nu[BLOCK - 1], next_lane(nu[0]))))
        downs = [jnp.where(lane == 0, 0.0, harmonic(prev_lane(nu[BLOCK - 1]), nu[0]))] + ups[:-1]
        return ups, downs

    up_e, dn_e = upward(nu_e)
    up_o, dn_o = upward(nu_o)
    left_kept = jnp.logical_not(has_left) if neumann else True
    right_kept = jnp.logical_not(has_right) if neumann else True
    all_e, all_o = [], []
    for r in range(BLOCK):
        d_e = sigma_ref[r, 0] + pair[r] + cross_e[r] + up_e[r] + dn_e[r]
        d_o = sigma_ref[r, 1] + pair[r] + cross_o[r] + up_o[r] + dn_o[r]
        if r in (0, BLOCK - 1):
            on_edge = lane == (0 if r == 0 else LANES - 1)
            d_e = d_e + jnp.where(on_edge, 2.0 * nu_e[r], 0.0)
            d_o = d_o + jnp.where(on_edge, 2.0 * nu_o[r], 0.0)
        all_e.append(d_e + jnp.where((sub == 0) & left_kept, 2.0 * nu_e[r], 0.0))
        all_o.append(d_o + jnp.where((sub == SUB - 1) & right_kept, 2.0 * nu_o[r], 0.0))
    inv_e = [1.0 / d for d in all_e]
    inv_o = [1.0 / d for d in all_o]
    scale_e, over_e = [jnp.ones((SUB, LANES), F32)], [jnp.ones((SUB, LANES), F32)]
    for r in range(1, BLOCK):
        link = up_e[r - 1]
        even = r if r % 2 == 0 else r - 1
        there, back = link * inv_e[even], all_e[even] / link
        if even == r:
            there, back = back, there
        scale_e.append(scale_e[r - 1] * back)
        over_e.append(over_e[r - 1] * there)
    scale_o = [scale_e[r] * (all_e[r] / pair[r]) for r in range(BLOCK)]
    rec_e = [inv_e[r] * over_e[r] for r in range(BLOCK)]
    rec_o = [inv_o[r] * (over_e[r] * (pair[r] * inv_e[r])) for r in range(BLOCK)]
    around_e = [prev_lane(scale_e[BLOCK - 1])] + scale_e + [next_lane(scale_e[0])]
    around_o = [prev_lane(scale_o[BLOCK - 1])] + scale_o + [next_lane(scale_o[0])]

    def put(out, slot, tiles, needed=lambda r: True):
        rows = spread(tiles)
        for r in range(LOW, HIGH):
            if needed(r):
                out[r - LOW, slot] = rows[r]

    span = range(BLOCK)
    put(c_out, Q_E, [cross_e[r] * prev_sub(scale_o[r]) * rec_e[r] for r in span])
    put(c_out, P_O, [pair[r] * scale_e[r] * rec_o[r] for r in span])
    put(c_out, Q_O, [cross_o[r] * next_sub(scale_e[r]) * rec_o[r] for r in span])
    put(c_out, UP_O, [up_o[r] * around_o[r + 2] * rec_o[r] for r in span])
    put(c_out, DN_O, [dn_o[r] * around_o[r] * rec_o[r] for r in span])
    put(c_out, UP_E, [up_e[r] * around_e[r + 2] * rec_e[r] for r in span], lambda r: not unit_up(r))
    put(c_out, DN_E, [dn_e[r] * around_e[r] * rec_e[r] for r in span], lambda r: not unit_down(r))
    put(s_out, 0, [sigma_ref[r, 0] * inv_e[r] for r in span])
    put(s_out, 1, [sigma_ref[r, 1] * inv_o[r] for r in span])
    if not neumann:
        put(r_out, COIL_E, [coil_ref[r, 0] * rec_e[r] for r in span])
        put(r_out, COIL_O, [coil_ref[r, 1] * rec_o[r] for r in span])
    put(r_out, FACE_E, [jnp.where((sub == 0) & has_left, rec_e[r], 0.0) for r in span])
    put(r_out, FACE_O, [jnp.where((sub == SUB - 1) & has_right, rec_o[r], 0.0) for r in span])
    for r in range(BLOCK):
        if not neumann:
            scale_out[r, 0] = scale_e[r]
            scale_out[r, 1] = scale_o[r]
        edge_out[0, r : r + 1] = 2.0 * nu_e[r][0:1]
        edge_out[1, r : r + 1] = 2.0 * nu_o[r][SUB - 1 : SUB]
        edge_out[2, r : r + 1] = scale_e[r][0:1]
        edge_out[3, r : r + 1] = scale_o[r][SUB - 1 : SUB]


def neumann_coef_kernel(nu_ref, sigma_ref, c_out, s_out, r_out, edge_out):
    coef_kernel(True, nu_ref, sigma_ref, None, c_out, s_out, r_out, edge_out, None)


def advance(field_e, field_o, rhs, c_ref):
    for turn in range(JACOBI // DEPTH):
        if turn == 0:
            now_e, now_o = field_e, field_o
        else:
            now_e, now_o = haloed(now_e), haloed(now_o)
        for k in range(1, DEPTH + 1):
            new_e, new_o = {}, {}
            for r in range(k - DEPTH, BLOCK + DEPTH - k):
                i = r - LOW
                up_e = now_e[r + 1] if unit_up(r) else c_ref[i, UP_E] * now_e[r + 1]
                dn_e = now_e[r - 1] if unit_down(r) else c_ref[i, DN_E] * now_e[r - 1]
                up_o = c_ref[i, UP_O] * now_o[r + 1]
                dn_o = c_ref[i, DN_O] * now_o[r - 1]
                soon_e, late_e = (dn_e, up_e) if 2 * r >= BLOCK else (up_e, dn_e)
                soon_o, late_o = (dn_o, up_o) if 2 * r >= BLOCK else (up_o, dn_o)
                beside_e = now_o[r] + c_ref[i, Q_E] * prev_sub(now_o[r])
                beside_o = c_ref[i, P_O] * now_e[r] + c_ref[i, Q_O] * next_sub(now_e[r])
                new_e[r] = ((rhs[r][0] + soon_e) + beside_e) + late_e
                new_o[r] = ((rhs[r][1] + soon_o) + beside_o) + late_o
            now_e, now_o = new_e, new_o
    return now_e, now_o


def haloed(rows):
    out = {r: rows[r] for r in range(BLOCK)}
    for j in range(DEPTH):
        out[j - DEPTH] = prev_lane(rows[BLOCK - DEPTH + j])
        out[BLOCK + j] = next_lane(rows[j])
    return out


def march(start, c_ref, s_ref, r_ref, wave_ref, left, right, first, last, halo, steps):
    def given_at(t, r):
        f_e = f_o = None
        if wave_ref is not None:
            wave = wave_ref[pl.ds(t, 1), :]
            f_e = r_ref[r - LOW, COIL_E] * wave
            f_o = r_ref[r - LOW, COIL_O] * wave
        if left is not None:
            at = pl.ds(t * BLOCK + r, 1)
            from_left = r_ref[r - LOW, FACE_E] * left[at, :]
            from_right = r_ref[r - LOW, FACE_O] * right[at, :]
            f_e = from_left if f_e is None else f_e + from_left
            f_o = from_right if f_o is None else f_o + from_right
        return f_e, f_o

    halo_rows = [r for r in range(LOW, HIGH) if not 0 <= r < BLOCK]

    def put_halo(t, slot):
        for n, r in enumerate(halo_rows if halo is not None else ()):
            shift = prev_lane if r < 0 else next_lane
            for e, tile in enumerate(given_at(t, r % BLOCK)):
                halo[slot, n, e] = shift(tile)

    def step(t, slot, carry):
        now_e = haloed(dict(enumerate(carry[:BLOCK])))
        now_o = haloed(dict(enumerate(carry[BLOCK:])))
        given = {r: given_at(t, r) for r in range(BLOCK)}
        for n, r in enumerate(halo_rows):
            if halo is not None:
                given[r] = halo[slot, n, 0], halo[slot, n, 1]
            elif left is None:
                given[r] = given_at(t, r)
        rhs = {
            r: (s_ref[r - LOW, 0] * now_e[r] + f_e, s_ref[r - LOW, 1] * now_o[r] + f_o)
            for r, (f_e, f_o) in given.items()
        }
        for r in halo_rows:
            if r not in rhs:
                shift = prev_lane if r < 0 else next_lane
                rhs[r] = shift(rhs[r % BLOCK][0]), shift(rhs[r % BLOCK][1])
        now_e, now_o = advance(now_e, now_o, rhs, c_ref)
        put_halo(jnp.minimum(t + 1, steps - 1), 1 - slot)
        for r in range(BLOCK):
            first[pl.ds(t * BLOCK + r, 1), :] = now_e[r][0:1]
            last[pl.ds(t * BLOCK + r, 1), :] = now_o[r][SUB - 1 : SUB]
        return tuple(now_e[r] for r in range(BLOCK)) + tuple(now_o[r] for r in range(BLOCK))

    def some_steps(i, carry):
        for j in range(UNROLL):
            carry = step(UNROLL * i + j, j % 2, carry)
        return carry

    put_halo(0, 0)
    return lax.fori_loop(0, steps // UNROLL, some_steps, start)


def at_step(ref, t):
    return ref[t * BLOCK : (t + 1) * BLOCK, :]


def dirichlet_kernel(sweep, steps, *refs):
    if sweep == 0:
        (start_ref, c_ref, s_ref, r_ref, scale_ref, edge_ref, wave_ref, ends, ev_out, od_out, first, last) = refs
        halo = None
        left = right = None
    else:
        (start_ref, c_ref, s_ref, r_ref, scale_ref, edge_ref, wave_ref, ev_own, od_own, ev_got, od_got,
         ends, ev_out, od_out, g_right, first, last, left, right, g_left, halo) = refs
    even, _, _ = flags()
    if sweep > 0:
        for t in range(steps):
            ev = THETA * (at_step(ev_own, t) + at_step(ev_got, t))
            od = THETA * (at_step(od_own, t) + at_step(od_got, t))
            at_left = jnp.where(even, od, ev)
            at_right = jnp.where(even, ev, od)
            g_left[t * BLOCK : (t + 1) * BLOCK, :] = at_left
            g_right[t * BLOCK : (t + 1) * BLOCK, :] = at_right
            left[t * BLOCK : (t + 1) * BLOCK, :] = edge_ref[0] * at_left
            right[t * BLOCK : (t + 1) * BLOCK, :] = edge_ref[1] * at_right
    start = tuple(start_ref[r, e] / scale_ref[r, e] for e in range(2) for r in range(BLOCK))
    final = march(start, c_ref, s_ref, r_ref, wave_ref, left, right, first, last, halo, steps)
    for e in range(2):
        for r in range(BLOCK):
            ends[r, e] = final[e * BLOCK + r] * scale_ref[r, e]
    for t in range(steps):
        to_left = edge_ref[2] * at_step(first, t)
        to_right = edge_ref[3] * at_step(last, t)
        if sweep > 0:
            to_left = to_left - at_step(g_left, t)
            to_right = to_right - at_step(g_right, t)
        to_left = edge_ref[0] * to_left
        to_right = edge_ref[1] * to_right
        ev_out[t * BLOCK : (t + 1) * BLOCK, :] = jnp.where(even, to_right, to_left)
        od_out[t * BLOCK : (t + 1) * BLOCK, :] = jnp.where(even, to_left, to_right)


def neumann_kernel(
    steps, c_ref, s_ref, r_ref, edge_ref, ev_own, od_own, ev_got, od_got, ev_out, od_out, first, last, left, right
):
    even, _, _ = flags()
    for t in range(steps):
        ev = at_step(ev_own, t) + at_step(ev_got, t)
        od = at_step(od_own, t) + at_step(od_got, t)
        left[t * BLOCK : (t + 1) * BLOCK, :] = jnp.where(even, od, ev)
        right[t * BLOCK : (t + 1) * BLOCK, :] = jnp.where(even, ev, od)
    zero = jnp.zeros((SUB, LANES), F32)
    march((zero,) * (2 * BLOCK), c_ref, s_ref, r_ref, None, left, right, first, last, None, steps)
    for t in range(steps):
        to_left = edge_ref[2] * at_step(first, t)
        to_right = edge_ref[3] * at_step(last, t)
        ev_out[t * BLOCK : (t + 1) * BLOCK, :] = jnp.where(even, to_right, to_left)
        od_out[t * BLOCK : (t + 1) * BLOCK, :] = jnp.where(even, to_left, to_right)


def natural_kernel(ends_ref, out, scratch):
    for e in range(2):
        tiles = from_blocks([ends_ref[r, e] for r in range(BLOCK)])
        for j in range(BLOCK):
            scratch[pl.ds(16 * j + e, SUB, stride=2), :] = tiles[j]
    for j in range(BLOCK):
        out[0, :, LANES * j : LANES * j + LANES] = scratch[16 * j : 16 * j + 16, :]


def join_kernel(steps, g_right, ev_own, od_own, ev_got, od_got, out, scratch):
    even, _, has_right = flags()
    for t in range(steps):
        ev = at_step(ev_own, t) + at_step(ev_got, t)
        od = at_step(od_own, t) + at_step(od_got, t)
        total = at_step(g_right, t) + THETA * jnp.where(even, ev, od)
        scratch[t * BLOCK : (t + 1) * BLOCK, :] = jnp.where(has_right, total, 0.0)
    for half in range(steps // SUB):
        base = half * SUB * BLOCK
        tiles = from_blocks([scratch[pl.ds(base + r, SUB, stride=BLOCK), :] for r in range(BLOCK)])
        for j in range(BLOCK):
            out[half * SUB : (half + 1) * SUB, j * LANES : (j + 1) * LANES] = tiles[j]


def call(kernel, name, inputs, outputs, scratch=(), space=pltpu.VMEM):
    single = not isinstance(outputs, list)
    shapes = [jax.ShapeDtypeStruct(s, F32) for s in ([outputs] if single else outputs)]
    result = pl.pallas_call(
        kernel,
        out_shape=shapes,
        in_specs=[pl.BlockSpec(memory_space=space)] * len(inputs),
        out_specs=[pl.BlockSpec(memory_space=pltpu.VMEM)] * len(shapes),
        scratch_shapes=[pltpu.VMEM(s, F32) if isinstance(s, tuple) else s for s in scratch],
        compiler_params=pltpu.CompilerParams(vmem_limit_bytes=6 << 20),
        name=name,
    )(*inputs)
    return result[0] if single else result


def body(start_states, sigma, labels, nu_table, coil, waveform):
    steps = waveform.shape[0]
    columns, rows = sigma.shape
    count = lax.axis_size("space")
    windows = lax.axis_size("tm")
    even_faces = [(i, i ^ 1) for i in range(count)]
    odd_faces = []
    for w in range(windows):
        for i in range(count):
            inner = 0 < i < count - 1
            partner = (w, i + 1 if i % 2 else i - 1) if inner else (w ^ 1, i)
            odd_faces.append((w * count + i, partner[0] * count + partner[1]))
    field = (BLOCK, 2, SUB, LANES)
    series = (steps * BLOCK, LANES)
    halo = (2, ROWS - BLOCK, 2, SUB, LANES)
    coefs = [(ROWS, 7, SUB, LANES), (ROWS, 2, SUB, LANES), (ROWS, 4, SUB, LANES), (4, BLOCK, LANES)]
    nu, sig, state, c_dir, s_dir, r_dir, edge_dir, scale_dir, wave = call(
        first_kernel, "first",
        [
            pltpu.with_memory_space_constraint(array, pltpu.HBM)
            for array in (labels, nu_table, sigma, coil, start_states, waveform)
        ],
        [field, field, field] + coefs + [field, (steps, LANES)],
        [
            pltpu.VMEM(labels.shape, jnp.int32), pltpu.SMEM(nu_table.shape, F32), sigma.shape, coil.shape,
            start_states.shape, pltpu.SMEM(waveform.shape, F32), field,
        ] + [(128, LANES)] * 4 + [pltpu.SemaphoreType.DMA((6,))],
        space=pltpu.HBM,
    )
    c_neu, s_neu, r_neu, edge_neu = call(neumann_coef_kernel, "coef_neu", [nu, sig], coefs)

    def swapped(ev, od):
        return lax.ppermute(ev, "space", even_faces), lax.ppermute(od, ("tm", "space"), odd_faces)

    ends, ev, od = call(
        functools.partial(dirichlet_kernel, 0, steps), "dir0",
        [state, c_dir, s_dir, r_dir, scale_dir, edge_dir, wave], [field, series, series], [series] * 2,
    )
    state = lax.ppermute(ends, "tm", [(i, (i + 1) % windows) for i in range(windows)])
    ev_got, od_got = swapped(ev, od)
    def neumann(*series_pairs):
        return call(
            functools.partial(neumann_kernel, steps), "neu",
            [c_neu, s_neu, r_neu, edge_neu, *series_pairs], [series] * 2, [series] * 4,
        )

    ev, od = neumann(ev, od, ev_got, od_got)
    ev_got, od_got = swapped(ev, od)
    ends, ev, od, g_right = call(
        functools.partial(dirichlet_kernel, 1, steps), "dir1",
        [state, c_dir, s_dir, r_dir, scale_dir, edge_dir, wave, ev, od, ev_got, od_got],
        [field, series, series, series], [series] * 5 + [halo],
    )
    ev_got, od_got = swapped(ev, od)
    end_states = call(natural_kernel, "natural", [ends], (1, columns, rows), [(128, LANES)])
    ev, od = neumann(ev, od, ev_got, od_got)
    ev_got, od_got = swapped(ev, od)
    traces = call(
        functools.partial(join_kernel, steps), "join", [g_right, ev, od, ev_got, od_got], (steps, rows), [series]
    )
    return end_states, traces


def solution(mesh):
    placed = (
        P("tm", "space", None),
        P("space", None),
        P("space", None),
        P(),
        P("space", None),
        P("tm"),
    )
    return jax.shard_map(
        body,
        mesh=mesh,
        in_specs=placed,
        out_specs=(P("tm", "space", None), P("tm", "space")),
        check_vma=False,
    )
```

```python
import functools

import jax
import jax.numpy as jnp
from jax import lax
from jax.experimental import pallas as pl
from jax.experimental.pallas import tpu as pltpu
from jax.sharding import PartitionSpec as P

JACOBI = 8
SWEEPS = 2
THETA = 0.25

BLOCK = 8
SUB = 8
LANES = 128
DEPTH = 4
LOW = -(DEPTH - 1)
HIGH = BLOCK + DEPTH - 1
ROWS = HIGH - LOW
Q_E, P_O, Q_O, UP_O, DN_O, UP_E, DN_E = range(7)
COIL_E, COIL_O, FACE_E, FACE_O = range(4)
F32 = jnp.float32
UNROLL = 4


def tile_index(axis):
    return lax.broadcasted_iota(jnp.int32, (SUB, LANES), axis)


def next_lane(tile):
    return pltpu.roll(tile, LANES - 1, 1)


def prev_lane(tile):
    return pltpu.roll(tile, 1, 1)


def next_sub(tile):
    return pltpu.roll(tile, SUB - 1, 0)


def prev_sub(tile):
    return pltpu.roll(tile, 1, 0)


def swap_groups(tiles):
    group = tile_index(1) // 16
    for bit in (1, 2, 4):
        low = (group & bit) == 0
        new = []
        for j, tile in enumerate(tiles):
            other = tiles[j ^ bit]
            if j & bit:
                new.append(jnp.where(low, pltpu.roll(other, LANES - 16 * bit, 1), tile))
            else:
                new.append(jnp.where(low, tile, pltpu.roll(other, 16 * bit, 1)))
        tiles = new
    return tiles


def to_blocks(tiles):
    lane = tile_index(1)
    order = 8 * (lane % 16) + lane // 16
    return swap_groups([jnp.take_along_axis(tile, order, axis=1) for tile in tiles])


def from_blocks(tiles):
    lane = tile_index(1)
    order = 16 * (lane % 8) + lane // 8
    return [jnp.take_along_axis(tile, order, axis=1) for tile in swap_groups(tiles)]


def put_field(value, scratch, out):
    for j in range(BLOCK):
        scratch[16 * j : 16 * j + 16, :] = value[:, LANES * j : LANES * j + LANES]
    for e in range(2):
        tiles = to_blocks([scratch[pl.ds(16 * j + e, SUB, stride=2), :] for j in range(BLOCK)])
        for r in range(BLOCK):
            out[r, e] = tiles[r]


def harmonic(first_nu, second_nu):
    return 2.0 * first_nu * second_nu / (first_nu + second_nu)


def spread(tiles):
    rows = {}
    for r in range(LOW, HIGH):
        if r < 0:
            rows[r] = prev_lane(tiles[r + BLOCK])
        elif r >= BLOCK:
            rows[r] = next_lane(tiles[r - BLOCK])
        else:
            rows[r] = tiles[r]
    return rows


def flags():
    place = lax.axis_index("space")
    count = lax.axis_size("space")
    return place % 2 == 0, place > 0, place < count - 1


def first_kernel(
    labels_hbm, table_hbm, sigma_hbm, coil_hbm, start_hbm, wave_hbm,
    nu_out, sigma_out, start_out, c_out, s_out, r_out, edge_out, scale_out, wave_out,
    labels_ref, table_ref, sigma_ref, coil_ref, start_ref, wave_ref, cur_ref, s0, s1, s2, s3, sems,
):
    copies = [
        pltpu.make_async_copy(source, target, sems.at[i])
        for i, (source, target) in enumerate((
            (table_hbm, table_ref), (labels_hbm, labels_ref), (sigma_hbm, sigma_ref),
            (coil_hbm, coil_ref), (start_hbm, start_ref), (wave_hbm, wave_ref),
        ))
    ]
    for copy in copies:
        copy.start()
    for copy in copies:
        copy.wait()
    labels = labels_ref[...]
    nu = jnp.zeros(labels.shape, F32)
    for material in range(table_ref.shape[0]):
        nu = nu + jnp.where(labels == material, table_ref[material], 0.0)
    put_field(nu, s0, nu_out)
    put_field(sigma_ref[...], s1, sigma_out)
    put_field(coil_ref[...], s2, cur_ref)
    put_field(start_ref[0], s3, start_out)
    for t in range(wave_ref.shape[0]):
        wave_out[t : t + 1, :] = jnp.full((1, LANES), wave_ref[t], F32)
    coef_kernel(False, nu_out, sigma_out, cur_ref, c_out, s_out, r_out, edge_out, scale_out)


def unit_up(r):
    return r % BLOCK in (0, 2, 4, 6)


def unit_down(r):
    return r % BLOCK in (2, 4, 6)


def coef_kernel(neumann, nu_ref, sigma_ref, coil_ref, c_out, s_out, r_out, edge_out, scale_out):
    _, has_left, has_right = flags()
    sub = tile_index(0)
    lane = tile_index(1)
    nu_e = [nu_ref[r, 0] for r in range(BLOCK)]
    nu_o = [nu_ref[r, 1] for r in range(BLOCK)]
    pair = [harmonic(nu_e[r], nu_o[r]) for r in range(BLOCK)]
    cross_o = [jnp.where(sub == SUB - 1, 0.0, harmonic(nu_o[r], next_sub(nu_e[r]))) for r in range(BLOCK)]
    cross_e = [prev_sub(cross_o[r]) for r in range(BLOCK)]

    def upward(nu):
        ups = [harmonic(nu[r], nu[r + 1]) for r in range(BLOCK - 1)]
        ups.append(jnp.where(lane == LANES - 1, 0.0, harmonic(nu[BLOCK - 1], next_lane(nu[0]))))
        downs = [jnp.where(lane == 0, 0.0, harmonic(prev_lane(nu[BLOCK - 1]), nu[0]))] + ups[:-1]
        return ups, downs

    up_e, dn_e = upward(nu_e)
    up_o, dn_o = upward(nu_o)
    left_kept = jnp.logical_not(has_left) if neumann else True
    right_kept = jnp.logical_not(has_right) if neumann else True
    all_e, all_o = [], []
    for r in range(BLOCK):
        d_e = sigma_ref[r, 0] + pair[r] + cross_e[r] + up_e[r] + dn_e[r]
        d_o = sigma_ref[r, 1] + pair[r] + cross_o[r] + up_o[r] + dn_o[r]
        if r in (0, BLOCK - 1):
            on_edge = lane == (0 if r == 0 else LANES - 1)
            d_e = d_e + jnp.where(on_edge, 2.0 * nu_e[r], 0.0)
            d_o = d_o + jnp.where(on_edge, 2.0 * nu_o[r], 0.0)
        all_e.append(d_e + jnp.where((sub == 0) & left_kept, 2.0 * nu_e[r], 0.0))
        all_o.append(d_o + jnp.where((sub == SUB - 1) & right_kept, 2.0 * nu_o[r], 0.0))
    inv_e = [1.0 / d for d in all_e]
    inv_o = [1.0 / d for d in all_o]
    scale_e, over_e = [jnp.ones((SUB, LANES), F32)], [jnp.ones((SUB, LANES), F32)]
    for r in range(1, BLOCK):
        link = up_e[r - 1]
        even = r if r % 2 == 0 else r - 1
        there, back = link * inv_e[even], all_e[even] / link
        if even == r:
            there, back = back, there
        scale_e.append(scale_e[r - 1] * back)
        over_e.append(over_e[r - 1] * there)
    scale_o = [scale_e[r] * (all_e[r] / pair[r]) for r in range(BLOCK)]
    rec_e = [inv_e[r] * over_e[r] for r in range(BLOCK)]
    rec_o = [inv_o[r] * (over_e[r] * (pair[r] * inv_e[r])) for r in range(BLOCK)]
    around_e = [prev_lane(scale_e[BLOCK - 1])] + scale_e + [next_lane(scale_e[0])]
    around_o = [prev_lane(scale_o[BLOCK - 1])] + scale_o + [next_lane(scale_o[0])]

    def put(out, slot, tiles, needed=lambda r: True):
        rows = spread(tiles)
        for r in range(LOW, HIGH):
            if needed(r):
                out[r - LOW, slot] = rows[r]

    span = range(BLOCK)
    put(c_out, Q_E, [cross_e[r] * prev_sub(scale_o[r]) * rec_e[r] for r in span])
    put(c_out, P_O, [pair[r] * scale_e[r] * rec_o[r] for r in span])
    put(c_out, Q_O, [cross_o[r] * next_sub(scale_e[r]) * rec_o[r] for r in span])
    put(c_out, UP_O, [up_o[r] * around_o[r + 2] * rec_o[r] for r in span])
    put(c_out, DN_O, [dn_o[r] * around_o[r] * rec_o[r] for r in span])
    put(c_out, UP_E, [up_e[r] * around_e[r + 2] * rec_e[r] for r in span], lambda r: not unit_up(r))
    put(c_out, DN_E, [dn_e[r] * around_e[r] * rec_e[r] for r in span], lambda r: not unit_down(r))
    put(s_out, 0, [sigma_ref[r, 0] * inv_e[r] for r in span])
    put(s_out, 1, [sigma_ref[r, 1] * inv_o[r] for r in span])
    if not neumann:
        put(r_out, COIL_E, [coil_ref[r, 0] * rec_e[r] for r in span])
        put(r_out, COIL_O, [coil_ref[r, 1] * rec_o[r] for r in span])
    for r in span:
        r_out[r - LOW, FACE_E] = jnp.where((sub == 0) & has_left, rec_e[r], 0.0)
        r_out[r - LOW, FACE_O] = jnp.where((sub == SUB - 1) & has_right, rec_o[r], 0.0)
    for r in range(BLOCK):
        if not neumann:
            scale_out[r, 0] = scale_e[r]
            scale_out[r, 1] = scale_o[r]
        edge_out[0, r : r + 1] = 2.0 * nu_e[r][0:1]
        edge_out[1, r : r + 1] = 2.0 * nu_o[r][SUB - 1 : SUB]
        edge_out[2, r : r + 1] = scale_e[r][0:1]
        edge_out[3, r : r + 1] = scale_o[r][SUB - 1 : SUB]


def neumann_coef_kernel(nu_ref, sigma_ref, c_out, s_out, r_out, edge_out):
    coef_kernel(True, nu_ref, sigma_ref, None, c_out, s_out, r_out, edge_out, None)


def advance(field_e, field_o, rhs, c_ref):
    def updated(now, r, e, zero=None):
        i = r - LOW
        if e == 0:
            up = now[r + 1, 0] if unit_up(r) else c_ref[i, UP_E] * now[r + 1, 0]
            dn = now[r - 1, 0] if unit_down(r) else c_ref[i, DN_E] * now[r - 1, 0]
            mid = now[r, 1]
            beside = mid + c_ref[i, Q_E] * prev_sub(mid)
        else:
            up = c_ref[i, UP_O] * now[r + 1, 1]
            dn = c_ref[i, DN_O] * now[r - 1, 1]
            mid = now[r, 0]
            beside = c_ref[i, P_O] * mid + c_ref[i, Q_O] * next_sub(mid)
        soon, late = (dn, up) if 2 * r >= BLOCK else (up, dn)
        b = rhs[r][e] if zero is None else rhs[r][e] + zero
        return ((b + soon) + beside) + late

    field = {(r, 0): v for r, v in field_e.items()}
    field.update({(r, 1): v for r, v in field_o.items()})
    chains = [{k: v for k, v in field.items() if sum(k) % 2 == c} for c in range(2)]
    for turn in range(JACOBI // DEPTH):
        for c in range(2):
            now = chains[c]
            if turn:
                wide = {}
                for (r, e), v in now.items():
                    wide[r, e] = v
                    if r >= BLOCK - DEPTH:
                        wide[r - BLOCK, e] = prev_lane(v)
                    if r < DEPTH:
                        wide[r + BLOCK, e] = next_lane(v)
                now = wide
            zero = jnp.minimum(jnp.maximum(ahead, 0.0), 0.0) if c == 1 and turn == 0 else None
            for k in range(1, DEPTH + 1):
                colour = (c + turn * DEPTH + k) % 2
                new = {}
                for r in range(k - DEPTH, BLOCK + DEPTH - k):
                    e = (r + colour) % 2
                    on_halo = k == 1 and not 0 <= r < BLOCK
                    new[r, e] = updated(now, r, e, zero if on_halo else None)
                now = new
            chains[c] = now
            ahead = next(v for (r, _), v in now.items() if r == BLOCK - 1)
    done = {**chains[0], **chains[1]}
    return {r: done[r, 0] for r in range(BLOCK)}, {r: done[r, 1] for r in range(BLOCK)}


def haloed(rows):
    out = {r: rows[r] for r in range(BLOCK)}
    for j in range(DEPTH):
        out[j - DEPTH] = prev_lane(rows[BLOCK - DEPTH + j])
        out[BLOCK + j] = next_lane(rows[j])
    return out


def march(start, c_ref, s_ref, r_ref, wave_ref, left, right, first, last, halo, steps):
    def given_at(t, r):
        f_e = f_o = None
        if wave_ref is not None:
            wave = wave_ref[pl.ds(t, 1), :]
            f_e = r_ref[r - LOW, COIL_E] * wave
            f_o = r_ref[r - LOW, COIL_O] * wave
        if left is not None:
            at = pl.ds(t * BLOCK + r, 1)
            from_left = r_ref[r - LOW, FACE_E] * left[at, :]
            from_right = r_ref[r - LOW, FACE_O] * right[at, :]
            f_e = from_left if f_e is None else f_e + from_left
            f_o = from_right if f_o is None else f_o + from_right
        return f_e, f_o

    halo_rows = [r for r in range(LOW, HIGH) if not 0 <= r < BLOCK]

    def put_halo(t, slot):
        for n, r in enumerate(halo_rows if halo is not None else ()):
            shift = prev_lane if r < 0 else next_lane
            for e, tile in enumerate(given_at(t, r % BLOCK)):
                halo[slot, n, e] = shift(tile)

    def step(t, slot, carry):
        now_e = haloed(dict(enumerate(carry[:BLOCK])))
        now_o = haloed(dict(enumerate(carry[BLOCK:])))
        given = {r: given_at(t, r) for r in range(BLOCK)}
        for n, r in enumerate(halo_rows):
            if halo is not None:
                given[r] = halo[slot, n, 0], halo[slot, n, 1]
            elif left is None:
                given[r] = given_at(t, r)
        rhs = {
            r: (s_ref[r - LOW, 0] * now_e[r] + f_e, s_ref[r - LOW, 1] * now_o[r] + f_o)
            for r, (f_e, f_o) in given.items()
        }
        for r in halo_rows:
            if r not in rhs:
                shift = prev_lane if r < 0 else next_lane
                rhs[r] = shift(rhs[r % BLOCK][0]), shift(rhs[r % BLOCK][1])
        now_e, now_o = advance(now_e, now_o, rhs, c_ref)
        put_halo(jnp.minimum(t + 1, steps - 1), 1 - slot)
        for r in range(BLOCK):
            first[pl.ds(t * BLOCK + r, 1), :] = now_e[r][0:1]
            last[pl.ds(t * BLOCK + r, 1), :] = now_o[r][SUB - 1 : SUB]
        return tuple(now_e[r] for r in range(BLOCK)) + tuple(now_o[r] for r in range(BLOCK))

    def some_steps(i, carry):
        for j in range(UNROLL):
            carry = step(UNROLL * i + j, j % 2, carry)
        return carry

    put_halo(0, 0)
    return lax.fori_loop(0, steps // UNROLL, some_steps, start)


def at_step(ref, t):
    return ref[t * BLOCK : (t + 1) * BLOCK, :]


def dirichlet_kernel(sweep, steps, *refs):
    if sweep == 0:
        (start_ref, c_ref, s_ref, r_ref, scale_ref, edge_ref, wave_ref, ends, ev_out, od_out, first, last) = refs
        halo = None
        left = right = None
    else:
        (start_ref, c_ref, s_ref, r_ref, scale_ref, edge_ref, wave_ref, ev_own, od_own, ev_got, od_got,
         ends, ev_out, od_out, g_right, first, last, left, right, g_left, halo) = refs
    even, _, _ = flags()
    if sweep > 0:
        for t in range(steps):
            ev = THETA * (at_step(ev_own, t) + at_step(ev_got, t))
            od = THETA * (at_step(od_own, t) + at_step(od_got, t))
            at_left = jnp.where(even, od, ev)
            at_right = jnp.where(even, ev, od)
            g_left[t * BLOCK : (t + 1) * BLOCK, :] = at_left
            g_right[t * BLOCK : (t + 1) * BLOCK, :] = at_right
            left[t * BLOCK : (t + 1) * BLOCK, :] = edge_ref[0] * at_left
            right[t * BLOCK : (t + 1) * BLOCK, :] = edge_ref[1] * at_right
    start = tuple(start_ref[r, e] / scale_ref[r, e] for e in range(2) for r in range(BLOCK))
    final = march(start, c_ref, s_ref, r_ref, wave_ref, left, right, first, last, halo, steps)
    for e in range(2):
        for r in range(BLOCK):
            ends[r, e] = final[e * BLOCK + r] * scale_ref[r, e]
    for t in range(steps):
        to_left = edge_ref[2] * at_step(first, t)
        to_right = edge_ref[3] * at_step(last, t)
        if sweep > 0:
            to_left = to_left - at_step(g_left, t)
            to_right = to_right - at_step(g_right, t)
        to_left = edge_ref[0] * to_left
        to_right = edge_ref[1] * to_right
        ev_out[t * BLOCK : (t + 1) * BLOCK, :] = jnp.where(even, to_right, to_left)
        od_out[t * BLOCK : (t + 1) * BLOCK, :] = jnp.where(even, to_left, to_right)


def neumann_kernel(
    steps, c_ref, s_ref, r_ref, edge_ref, ev_own, od_own, ev_got, od_got, ev_out, od_out, first, last, left, right
):
    even, _, _ = flags()
    for t in range(steps):
        ev = at_step(ev_own, t) + at_step(ev_got, t)
        od = at_step(od_own, t) + at_step(od_got, t)
        left[t * BLOCK : (t + 1) * BLOCK, :] = jnp.where(even, od, ev)
        right[t * BLOCK : (t + 1) * BLOCK, :] = jnp.where(even, ev, od)
    zero = jnp.zeros((SUB, LANES), F32)
    march((zero,) * (2 * BLOCK), c_ref, s_ref, r_ref, None, left, right, first, last, None, steps)
    for t in range(steps):
        to_left = edge_ref[2] * at_step(first, t)
        to_right = edge_ref[3] * at_step(last, t)
        ev_out[t * BLOCK : (t + 1) * BLOCK, :] = jnp.where(even, to_right, to_left)
        od_out[t * BLOCK : (t + 1) * BLOCK, :] = jnp.where(even, to_left, to_right)


def natural_kernel(ends_ref, out, scratch):
    for e in range(2):
        tiles = from_blocks([ends_ref[r, e] for r in range(BLOCK)])
        for j in range(BLOCK):
            scratch[pl.ds(16 * j + e, SUB, stride=2), :] = tiles[j]
    for j in range(BLOCK):
        out[0, :, LANES * j : LANES * j + LANES] = scratch[16 * j : 16 * j + 16, :]


def join_kernel(steps, g_right, ev_own, od_own, ev_got, od_got, out, scratch):
    even, _, has_right = flags()
    for t in range(steps):
        ev = at_step(ev_own, t) + at_step(ev_got, t)
        od = at_step(od_own, t) + at_step(od_got, t)
        total = at_step(g_right, t) + THETA * jnp.where(even, ev, od)
        scratch[t * BLOCK : (t + 1) * BLOCK, :] = jnp.where(has_right, total, 0.0)
    for half in range(steps // SUB):
        base = half * SUB * BLOCK
        tiles = from_blocks([scratch[pl.ds(base + r, SUB, stride=BLOCK), :] for r in range(BLOCK)])
        for j in range(BLOCK):
            out[half * SUB : (half + 1) * SUB, j * LANES : (j + 1) * LANES] = tiles[j]


def call(kernel, name, inputs, outputs, scratch=(), space=pltpu.VMEM):
    single = not isinstance(outputs, list)
    shapes = [jax.ShapeDtypeStruct(s, F32) for s in ([outputs] if single else outputs)]
    result = pl.pallas_call(
        kernel,
        out_shape=shapes,
        in_specs=[pl.BlockSpec(memory_space=space)] * len(inputs),
        out_specs=[pl.BlockSpec(memory_space=pltpu.VMEM)] * len(shapes),
        scratch_shapes=[pltpu.VMEM(s, F32) if isinstance(s, tuple) else s for s in scratch],
        compiler_params=pltpu.CompilerParams(vmem_limit_bytes=6 << 20),
        name=name,
    )(*inputs)
    return result[0] if single else result


def body(start_states, sigma, labels, nu_table, coil, waveform):
    steps = waveform.shape[0]
    columns, rows = sigma.shape
    count = lax.axis_size("space")
    windows = lax.axis_size("tm")
    even_faces = [(i, i ^ 1) for i in range(count)]
    odd_faces = []
    for w in range(windows):
        for i in range(count):
            inner = 0 < i < count - 1
            partner = (w, i + 1 if i % 2 else i - 1) if inner else (w ^ 1, i)
            odd_faces.append((w * count + i, partner[0] * count + partner[1]))
    field = (BLOCK, 2, SUB, LANES)
    series = (steps * BLOCK, LANES)
    halo = (2, ROWS - BLOCK, 2, SUB, LANES)
    coefs = [(ROWS, 7, SUB, LANES), (ROWS, 2, SUB, LANES), (ROWS, 4, SUB, LANES), (4, BLOCK, LANES)]
    nu, sig, state, c_dir, s_dir, r_dir, edge_dir, scale_dir, wave = call(
        first_kernel, "first",
        [
            pltpu.with_memory_space_constraint(array, pltpu.HBM)
            for array in (labels, nu_table, sigma, coil, start_states, waveform)
        ],
        [field, field, field] + coefs + [field, (steps, LANES)],
        [
            pltpu.VMEM(labels.shape, jnp.int32), pltpu.SMEM(nu_table.shape, F32), sigma.shape, coil.shape,
            start_states.shape, pltpu.SMEM(waveform.shape, F32), field,
        ] + [(128, LANES)] * 4 + [pltpu.SemaphoreType.DMA((6,))],
        space=pltpu.HBM,
    )
    c_neu, s_neu, r_neu, edge_neu = call(neumann_coef_kernel, "coef_neu", [nu, sig], coefs)

    def swapped(ev, od):
        return lax.ppermute(ev, "space", even_faces), lax.ppermute(od, ("tm", "space"), odd_faces)

    ends, ev, od = call(
        functools.partial(dirichlet_kernel, 0, steps), "dir0",
        [state, c_dir, s_dir, r_dir, scale_dir, edge_dir, wave], [field, series, series], [series] * 2,
    )
    state = lax.ppermute(ends, "tm", [(i, (i + 1) % windows) for i in range(windows)])
    ev_got, od_got = swapped(ev, od)
    def neumann(*series_pairs):
        return call(
            functools.partial(neumann_kernel, steps), "neu",
            [c_neu, s_neu, r_neu, edge_neu, *series_pairs], [series] * 2, [series] * 4,
        )

    ev, od = neumann(ev, od, ev_got, od_got)
    ev_got, od_got = swapped(ev, od)
    ends, ev, od, g_right = call(
        functools.partial(dirichlet_kernel, 1, steps), "dir1",
        [state, c_dir, s_dir, r_dir, scale_dir, edge_dir, wave, ev, od, ev_got, od_got],
        [field, series, series, series], [series] * 5 + [halo],
    )
    ev_got, od_got = swapped(ev, od)
    end_states = call(natural_kernel, "natural", [ends], (1, columns, rows), [(128, LANES)])
    ev, od = neumann(ev, od, ev_got, od_got)
    ev_got, od_got = swapped(ev, od)
    traces = call(
        functools.partial(join_kernel, steps), "join", [g_right, ev, od, ev_got, od_got], (steps, rows), [series]
    )
    return end_states, traces


def solution(mesh):
    placed = (
        P("tm", "space", None),
        P("space", None),
        P("space", None),
        P(),
        P("space", None),
        P("tm"),
    )
    return jax.shard_map(
        body,
        mesh=mesh,
        in_specs=placed,
        out_specs=(P("tm", "space", None), P("tm", "space")),
        check_vma=False,
    )
```

```python
import functools

import jax
import jax.numpy as jnp
from jax import lax
from jax.experimental import pallas as pl
from jax.experimental.pallas import tpu as pltpu
from jax.sharding import PartitionSpec as P

JACOBI = 8
SWEEPS = 2
THETA = 0.25

BLOCK = 8
SUB = 8
LANES = 128
DEPTH = 4
LOW = -(DEPTH - 1)
HIGH = BLOCK + DEPTH - 1
ROWS = HIGH - LOW
Q_E, P_O, Q_O, UP_O, DN_O, UP_E, DN_E = range(7)
COIL_E, COIL_O, FACE_E, FACE_O = range(4)
F32 = jnp.float32
UNROLL = 8


def tile_index(axis):
    return lax.broadcasted_iota(jnp.int32, (SUB, LANES), axis)


def next_lane(tile):
    return pltpu.roll(tile, LANES - 1, 1)


def prev_lane(tile):
    return pltpu.roll(tile, 1, 1)


def next_sub(tile):
    return pltpu.roll(tile, SUB - 1, 0)


def prev_sub(tile):
    return pltpu.roll(tile, 1, 0)


def swap_groups(tiles):
    group = tile_index(1) // 16
    for bit in (1, 2, 4):
        low = (group & bit) == 0
        new = []
        for j, tile in enumerate(tiles):
            other = tiles[j ^ bit]
            if j & bit:
                new.append(jnp.where(low, pltpu.roll(other, LANES - 16 * bit, 1), tile))
            else:
                new.append(jnp.where(low, tile, pltpu.roll(other, 16 * bit, 1)))
        tiles = new
    return tiles


def to_blocks(tiles):
    lane = tile_index(1)
    order = 8 * (lane % 16) + lane // 16
    return swap_groups([jnp.take_along_axis(tile, order, axis=1) for tile in tiles])


def from_blocks(tiles):
    lane = tile_index(1)
    order = 16 * (lane % 8) + lane // 8
    return [jnp.take_along_axis(tile, order, axis=1) for tile in swap_groups(tiles)]


def put_field(value, scratch, out):
    for j in range(BLOCK):
        scratch[16 * j : 16 * j + 16, :] = value[:, LANES * j : LANES * j + LANES]
    for e in range(2):
        tiles = to_blocks([scratch[pl.ds(16 * j + e, SUB, stride=2), :] for j in range(BLOCK)])
        for r in range(BLOCK):
            out[r, e] = tiles[r]


def harmonic(first_nu, second_nu):
    return 2.0 * first_nu * second_nu / (first_nu + second_nu)


def spread(tiles):
    rows = {}
    for r in range(LOW, HIGH):
        if r < 0:
            rows[r] = prev_lane(tiles[r + BLOCK])
        elif r >= BLOCK:
            rows[r] = next_lane(tiles[r - BLOCK])
        else:
            rows[r] = tiles[r]
    return rows


def flags():
    place = lax.axis_index("space")
    count = lax.axis_size("space")
    return place % 2 == 0, place > 0, place < count - 1


def first_kernel(
    labels_hbm, table_hbm, sigma_hbm, coil_hbm, start_hbm, wave_hbm,
    nu_out, sigma_out, start_out, c_out, s_out, r_out, edge_out, scale_out, wave_out,
    labels_ref, table_ref, sigma_ref, coil_ref, start_ref, wave_ref, cur_ref, s0, s1, s2, s3, sems,
):
    copies = [
        pltpu.make_async_copy(source, target, sems.at[i])
        for i, (source, target) in enumerate((
            (table_hbm, table_ref), (labels_hbm, labels_ref), (sigma_hbm, sigma_ref),
            (coil_hbm, coil_ref), (start_hbm, start_ref), (wave_hbm, wave_ref),
        ))
    ]
    for copy in copies:
        copy.start()
    for copy in copies:
        copy.wait()
    labels = labels_ref[...]
    nu = jnp.zeros(labels.shape, F32)
    for material in range(table_ref.shape[0]):
        nu = nu + jnp.where(labels == material, table_ref[material], 0.0)
    put_field(nu, s0, nu_out)
    put_field(sigma_ref[...], s1, sigma_out)
    put_field(coil_ref[...], s2, cur_ref)
    put_field(start_ref[0], s3, start_out)
    for t in range(wave_ref.shape[0]):
        wave_out[t : t + 1, :] = jnp.full((1, LANES), wave_ref[t], F32)
    coef_kernel(False, nu_out, sigma_out, cur_ref, c_out, s_out, r_out, edge_out, scale_out)


def unit_up(r):
    return r % BLOCK in (0, 2, 4, 6)


def unit_down(r):
    return r % BLOCK in (2, 4, 6)


def coef_kernel(neumann, nu_ref, sigma_ref, coil_ref, c_out, s_out, r_out, edge_out, scale_out):
    _, has_left, has_right = flags()
    sub = tile_index(0)
    lane = tile_index(1)
    nu_e = [nu_ref[r, 0] for r in range(BLOCK)]
    nu_o = [nu_ref[r, 1] for r in range(BLOCK)]
    pair = [harmonic(nu_e[r], nu_o[r]) for r in range(BLOCK)]
    cross_o = [jnp.where(sub == SUB - 1, 0.0, harmonic(nu_o[r], next_sub(nu_e[r]))) for r in range(BLOCK)]
    cross_e = [prev_sub(cross_o[r]) for r in range(BLOCK)]

    def upward(nu):
        ups = [harmonic(nu[r], nu[r + 1]) for r in range(BLOCK - 1)]
        ups.append(jnp.where(lane == LANES - 1, 0.0, harmonic(nu[BLOCK - 1], next_lane(nu[0]))))
        downs = [jnp.where(lane == 0, 0.0, harmonic(prev_lane(nu[BLOCK - 1]), nu[0]))] + ups[:-1]
        return ups, downs

    up_e, dn_e = upward(nu_e)
    up_o, dn_o = upward(nu_o)
    left_kept = jnp.logical_not(has_left) if neumann else True
    right_kept = jnp.logical_not(has_right) if neumann else True
    all_e, all_o = [], []
    for r in range(BLOCK):
        d_e = sigma_ref[r, 0] + pair[r] + cross_e[r] + up_e[r] + dn_e[r]
        d_o = sigma_ref[r, 1] + pair[r] + cross_o[r] + up_o[r] + dn_o[r]
        if r in (0, BLOCK - 1):
            on_edge = lane == (0 if r == 0 else LANES - 1)
            d_e = d_e + jnp.where(on_edge, 2.0 * nu_e[r], 0.0)
            d_o = d_o + jnp.where(on_edge, 2.0 * nu_o[r], 0.0)
        all_e.append(d_e + jnp.where((sub == 0) & left_kept, 2.0 * nu_e[r], 0.0))
        all_o.append(d_o + jnp.where((sub == SUB - 1) & right_kept, 2.0 * nu_o[r], 0.0))
    inv_e = [1.0 / d for d in all_e]
    inv_o = [1.0 / d for d in all_o]
    scale_e, over_e = [jnp.ones((SUB, LANES), F32)], [jnp.ones((SUB, LANES), F32)]
    for r in range(1, BLOCK):
        link = up_e[r - 1]
        even = r if r % 2 == 0 else r - 1
        there, back = link * inv_e[even], all_e[even] / link
        if even == r:
            there, back = back, there
        scale_e.append(scale_e[r - 1] * back)
        over_e.append(over_e[r - 1] * there)
    scale_o = [scale_e[r] * (all_e[r] / pair[r]) for r in range(BLOCK)]
    rec_e = [inv_e[r] * over_e[r] for r in range(BLOCK)]
    rec_o = [inv_o[r] * (over_e[r] * (pair[r] * inv_e[r])) for r in range(BLOCK)]
    around_e = [prev_lane(scale_e[BLOCK - 1])] + scale_e + [next_lane(scale_e[0])]
    around_o = [prev_lane(scale_o[BLOCK - 1])] + scale_o + [next_lane(scale_o[0])]

    def put(out, slot, tiles, needed=lambda r: True):
        rows = spread(tiles)
        for r in range(LOW, HIGH):
            if needed(r):
                out[r - LOW, slot] = rows[r]

    span = range(BLOCK)
    put(c_out, Q_E, [cross_e[r] * prev_sub(scale_o[r]) * rec_e[r] for r in span])
    put(c_out, P_O, [pair[r] * scale_e[r] * rec_o[r] for r in span])
    put(c_out, Q_O, [cross_o[r] * next_sub(scale_e[r]) * rec_o[r] for r in span])
    put(c_out, UP_O, [up_o[r] * around_o[r + 2] * rec_o[r] for r in span])
    put(c_out, DN_O, [dn_o[r] * around_o[r] * rec_o[r] for r in span])
    put(c_out, UP_E, [up_e[r] * around_e[r + 2] * rec_e[r] for r in span], lambda r: not unit_up(r))
    put(c_out, DN_E, [dn_e[r] * around_e[r] * rec_e[r] for r in span], lambda r: not unit_down(r))
    put(s_out, 0, [sigma_ref[r, 0] * inv_e[r] for r in span])
    put(s_out, 1, [sigma_ref[r, 1] * inv_o[r] for r in span])
    if not neumann:
        put(r_out, COIL_E, [coil_ref[r, 0] * rec_e[r] for r in span])
        put(r_out, COIL_O, [coil_ref[r, 1] * rec_o[r] for r in span])
    for r in span:
        r_out[r - LOW, FACE_E] = jnp.where((sub == 0) & has_left, rec_e[r], 0.0)
        r_out[r - LOW, FACE_O] = jnp.where((sub == SUB - 1) & has_right, rec_o[r], 0.0)
    for r in range(BLOCK):
        if not neumann:
            scale_out[r, 0] = scale_e[r]
            scale_out[r, 1] = scale_o[r]
        edge_out[0, r : r + 1] = 2.0 * nu_e[r][0:1]
        edge_out[1, r : r + 1] = 2.0 * nu_o[r][SUB - 1 : SUB]
        edge_out[2, r : r + 1] = scale_e[r][0:1]
        edge_out[3, r : r + 1] = scale_o[r][SUB - 1 : SUB]


def neumann_coef_kernel(nu_ref, sigma_ref, c_out, s_out, r_out, edge_out):
    coef_kernel(True, nu_ref, sigma_ref, None, c_out, s_out, r_out, edge_out, None)


def advance(field_e, field_o, rhs, c_ref):
    def updated(now, r, e, zero=None):
        i = r - LOW
        if e == 0:
            up = now[r + 1, 0] if unit_up(r) else c_ref[i, UP_E] * now[r + 1, 0]
            dn = now[r - 1, 0] if unit_down(r) else c_ref[i, DN_E] * now[r - 1, 0]
            mid = now[r, 1]
            beside = mid + c_ref[i, Q_E] * prev_sub(mid)
        else:
            up = c_ref[i, UP_O] * now[r + 1, 1]
            dn = c_ref[i, DN_O] * now[r - 1, 1]
            mid = now[r, 0]
            beside = c_ref[i, P_O] * mid + c_ref[i, Q_O] * next_sub(mid)
        soon, late = (dn, up) if 2 * r >= BLOCK else (up, dn)
        b = rhs[r][e] if zero is None else rhs[r][e] + zero
        return ((b + soon) + beside) + late

    field = {(r, 0): v for r, v in field_e.items()}
    field.update({(r, 1): v for r, v in field_o.items()})
    chains = [{k: v for k, v in field.items() if sum(k) % 2 == c} for c in range(2)]
    for turn in range(JACOBI // DEPTH):
        for c in range(2):
            now = chains[c]
            if turn:
                wide = {}
                for (r, e), v in now.items():
                    wide[r, e] = v
                    if r >= BLOCK - DEPTH:
                        wide[r - BLOCK, e] = prev_lane(v)
                    if r < DEPTH:
                        wide[r + BLOCK, e] = next_lane(v)
                now = wide
            zero = jnp.minimum(jnp.maximum(ahead, 0.0), 0.0) if c == 1 and turn == 0 else None
            for k in range(1, DEPTH + 1):
                colour = (c + turn * DEPTH + k) % 2
                new = {}
                for r in range(k - DEPTH, BLOCK + DEPTH - k):
                    e = (r + colour) % 2
                    on_halo = k == 1 and not 0 <= r < BLOCK
                    new[r, e] = updated(now, r, e, zero if on_halo else None)
                now = new
            chains[c] = now
            ahead = next(v for (r, _), v in now.items() if r == BLOCK - 1)
    done = {**chains[0], **chains[1]}
    return {r: done[r, 0] for r in range(BLOCK)}, {r: done[r, 1] for r in range(BLOCK)}


def haloed(rows):
    out = {r: rows[r] for r in range(BLOCK)}
    for j in range(DEPTH):
        out[j - DEPTH] = prev_lane(rows[BLOCK - DEPTH + j])
        out[BLOCK + j] = next_lane(rows[j])
    return out


def march(start, c_ref, s_ref, r_ref, wave_ref, left, right, first, last, halo, steps):
    def given_at(t, r):
        f_e = f_o = None
        if wave_ref is not None:
            wave = wave_ref[pl.ds(t, 1), :]
            f_e = r_ref[r - LOW, COIL_E] * wave
            f_o = r_ref[r - LOW, COIL_O] * wave
        if left is not None:
            at = pl.ds(t * BLOCK + r, 1)
            from_left = r_ref[r - LOW, FACE_E] * left[at, :]
            from_right = r_ref[r - LOW, FACE_O] * right[at, :]
            f_e = from_left if f_e is None else f_e + from_left
            f_o = from_right if f_o is None else f_o + from_right
        return f_e, f_o

    halo_rows = [r for r in range(LOW, HIGH) if not 0 <= r < BLOCK]

    def put_halo(t, slot):
        for n, r in enumerate(halo_rows if halo is not None else ()):
            shift = prev_lane if r < 0 else next_lane
            for e, tile in enumerate(given_at(t, r % BLOCK)):
                halo[slot, n, e] = shift(tile)

    def step(t, slot, carry):
        now_e = haloed(dict(enumerate(carry[:BLOCK])))
        now_o = haloed(dict(enumerate(carry[BLOCK:])))
        given = {r: given_at(t, r) for r in range(BLOCK)}
        for n, r in enumerate(halo_rows):
            if halo is not None:
                given[r] = halo[slot, n, 0], halo[slot, n, 1]
            elif left is None:
                given[r] = given_at(t, r)
        rhs = {
            r: (s_ref[r - LOW, 0] * now_e[r] + f_e, s_ref[r - LOW, 1] * now_o[r] + f_o)
            for r, (f_e, f_o) in given.items()
        }
        for r in halo_rows:
            if r not in rhs:
                shift = prev_lane if r < 0 else next_lane
                rhs[r] = shift(rhs[r % BLOCK][0]), shift(rhs[r % BLOCK][1])
        now_e, now_o = advance(now_e, now_o, rhs, c_ref)
        put_halo(jnp.minimum(t + 1, steps - 1), 1 - slot)
        for r in range(BLOCK):
            first[pl.ds(t * BLOCK + r, 1), :] = now_e[r][0:1]
            last[pl.ds(t * BLOCK + r, 1), :] = now_o[r][SUB - 1 : SUB]
        return tuple(now_e[r] for r in range(BLOCK)) + tuple(now_o[r] for r in range(BLOCK))

    def some_steps(i, carry):
        for j in range(UNROLL):
            carry = step(UNROLL * i + j, j % 2, carry)
        return carry

    put_halo(0, 0)
    return lax.fori_loop(0, steps // UNROLL, some_steps, start)


def at_step(ref, t):
    return ref[t * BLOCK : (t + 1) * BLOCK, :]


def dirichlet_kernel(sweep, steps, *refs):
    if sweep == 0:
        (start_ref, c_ref, s_ref, r_ref, scale_ref, edge_ref, wave_ref, ends, ev_out, od_out, first, last) = refs
        halo = None
        left = right = None
    else:
        (start_ref, c_ref, s_ref, r_ref, scale_ref, edge_ref, wave_ref, ev_own, od_own, ev_got, od_got,
         ends, ev_out, od_out, g_right, first, last, left, right, g_left, halo) = refs
    even, _, _ = flags()
    if sweep > 0:
        for t in range(steps):
            ev = THETA * (at_step(ev_own, t) + at_step(ev_got, t))
            od = THETA * (at_step(od_own, t) + at_step(od_got, t))
            at_left = jnp.where(even, od, ev)
            at_right = jnp.where(even, ev, od)
            g_left[t * BLOCK : (t + 1) * BLOCK, :] = at_left
            g_right[t * BLOCK : (t + 1) * BLOCK, :] = at_right
            left[t * BLOCK : (t + 1) * BLOCK, :] = edge_ref[0] * at_left
            right[t * BLOCK : (t + 1) * BLOCK, :] = edge_ref[1] * at_right
    start = tuple(start_ref[r, e] / scale_ref[r, e] for e in range(2) for r in range(BLOCK))
    final = march(start, c_ref, s_ref, r_ref, wave_ref, left, right, first, last, halo, steps)
    for e in range(2):
        for r in range(BLOCK):
            ends[r, e] = final[e * BLOCK + r] * scale_ref[r, e]
    for t in range(steps):
        to_left = edge_ref[2] * at_step(first, t)
        to_right = edge_ref[3] * at_step(last, t)
        if sweep > 0:
            to_left = to_left - at_step(g_left, t)
            to_right = to_right - at_step(g_right, t)
        to_left = edge_ref[0] * to_left
        to_right = edge_ref[1] * to_right
        ev_out[t * BLOCK : (t + 1) * BLOCK, :] = jnp.where(even, to_right, to_left)
        od_out[t * BLOCK : (t + 1) * BLOCK, :] = jnp.where(even, to_left, to_right)


def neumann_kernel(
    steps, c_ref, s_ref, r_ref, edge_ref, ev_own, od_own, ev_got, od_got, ev_out, od_out, first, last, left, right
):
    even, _, _ = flags()
    for t in range(steps):
        ev = at_step(ev_own, t) + at_step(ev_got, t)
        od = at_step(od_own, t) + at_step(od_got, t)
        left[t * BLOCK : (t + 1) * BLOCK, :] = jnp.where(even, od, ev)
        right[t * BLOCK : (t + 1) * BLOCK, :] = jnp.where(even, ev, od)
    zero = jnp.zeros((SUB, LANES), F32)
    march((zero,) * (2 * BLOCK), c_ref, s_ref, r_ref, None, left, right, first, last, None, steps)
    for t in range(steps):
        to_left = edge_ref[2] * at_step(first, t)
        to_right = edge_ref[3] * at_step(last, t)
        ev_out[t * BLOCK : (t + 1) * BLOCK, :] = jnp.where(even, to_right, to_left)
        od_out[t * BLOCK : (t + 1) * BLOCK, :] = jnp.where(even, to_left, to_right)


def natural_kernel(ends_ref, out, scratch):
    for e in range(2):
        tiles = from_blocks([ends_ref[r, e] for r in range(BLOCK)])
        for j in range(BLOCK):
            scratch[pl.ds(16 * j + e, SUB, stride=2), :] = tiles[j]
    for j in range(BLOCK):
        out[0, :, LANES * j : LANES * j + LANES] = scratch[16 * j : 16 * j + 16, :]


def join_kernel(steps, g_right, ev_own, od_own, ev_got, od_got, out, scratch):
    even, _, has_right = flags()
    for t in range(steps):
        ev = at_step(ev_own, t) + at_step(ev_got, t)
        od = at_step(od_own, t) + at_step(od_got, t)
        total = at_step(g_right, t) + THETA * jnp.where(even, ev, od)
        scratch[t * BLOCK : (t + 1) * BLOCK, :] = jnp.where(has_right, total, 0.0)
    for half in range(steps // SUB):
        base = half * SUB * BLOCK
        tiles = from_blocks([scratch[pl.ds(base + r, SUB, stride=BLOCK), :] for r in range(BLOCK)])
        for j in range(BLOCK):
            out[half * SUB : (half + 1) * SUB, j * LANES : (j + 1) * LANES] = tiles[j]


def call(kernel, name, inputs, outputs, scratch=(), space=pltpu.VMEM):
    single = not isinstance(outputs, list)
    shapes = [jax.ShapeDtypeStruct(s, F32) for s in ([outputs] if single else outputs)]
    result = pl.pallas_call(
        kernel,
        out_shape=shapes,
        in_specs=[pl.BlockSpec(memory_space=space)] * len(inputs),
        out_specs=[pl.BlockSpec(memory_space=pltpu.VMEM)] * len(shapes),
        scratch_shapes=[pltpu.VMEM(s, F32) if isinstance(s, tuple) else s for s in scratch],
        compiler_params=pltpu.CompilerParams(vmem_limit_bytes=6 << 20),
        name=name,
    )(*inputs)
    return result[0] if single else result


def body(start_states, sigma, labels, nu_table, coil, waveform):
    steps = waveform.shape[0]
    columns, rows = sigma.shape
    count = lax.axis_size("space")
    windows = lax.axis_size("tm")
    even_faces = [(i, i ^ 1) for i in range(count)]
    odd_faces = []
    for w in range(windows):
        for i in range(count):
            inner = 0 < i < count - 1
            partner = (w, i + 1 if i % 2 else i - 1) if inner else (w ^ 1, i)
            odd_faces.append((w * count + i, partner[0] * count + partner[1]))
    field = (BLOCK, 2, SUB, LANES)
    series = (steps * BLOCK, LANES)
    halo = (2, ROWS - BLOCK, 2, SUB, LANES)
    coefs = [(ROWS, 7, SUB, LANES), (ROWS, 2, SUB, LANES), (ROWS, 4, SUB, LANES), (4, BLOCK, LANES)]
    nu, sig, state, c_dir, s_dir, r_dir, edge_dir, scale_dir, wave = call(
        first_kernel, "first",
        [
            pltpu.with_memory_space_constraint(array, pltpu.HBM)
            for array in (labels, nu_table, sigma, coil, start_states, waveform)
        ],
        [field, field, field] + coefs + [field, (steps, LANES)],
        [
            pltpu.VMEM(labels.shape, jnp.int32), pltpu.SMEM(nu_table.shape, F32), sigma.shape, coil.shape,
            start_states.shape, pltpu.SMEM(waveform.shape, F32), field,
        ] + [(128, LANES)] * 4 + [pltpu.SemaphoreType.DMA((6,))],
        space=pltpu.HBM,
    )
    c_neu, s_neu, r_neu, edge_neu = call(neumann_coef_kernel, "coef_neu", [nu, sig], coefs)

    def swapped(ev, od):
        return lax.ppermute(ev, "space", even_faces), lax.ppermute(od, ("tm", "space"), odd_faces)

    ends, ev, od = call(
        functools.partial(dirichlet_kernel, 0, steps), "dir0",
        [state, c_dir, s_dir, r_dir, scale_dir, edge_dir, wave], [field, series, series], [series] * 2,
    )
    state = lax.ppermute(ends, "tm", [(i, (i + 1) % windows) for i in range(windows)])
    ev_got, od_got = swapped(ev, od)
    def neumann(*series_pairs):
        return call(
            functools.partial(neumann_kernel, steps), "neu",
            [c_neu, s_neu, r_neu, edge_neu, *series_pairs], [series] * 2, [series] * 4,
        )

    ev, od = neumann(ev, od, ev_got, od_got)
    ev_got, od_got = swapped(ev, od)
    ends, ev, od, g_right = call(
        functools.partial(dirichlet_kernel, 1, steps), "dir1",
        [state, c_dir, s_dir, r_dir, scale_dir, edge_dir, wave, ev, od, ev_got, od_got],
        [field, series, series, series], [series] * 5 + [halo],
    )
    ev_got, od_got = swapped(ev, od)
    end_states = call(natural_kernel, "natural", [ends], (1, columns, rows), [(128, LANES)])
    ev, od = neumann(ev, od, ev_got, od_got)
    ev_got, od_got = swapped(ev, od)
    traces = call(
        functools.partial(join_kernel, steps), "join", [g_right, ev, od, ev_got, od_got], (steps, rows), [series]
    )
    return end_states, traces


def solution(mesh):
    placed = (
        P("tm", "space", None),
        P("space", None),
        P("space", None),
        P(),
        P("space", None),
        P("tm"),
    )
    return jax.shard_map(
        body,
        mesh=mesh,
        in_specs=placed,
        out_specs=(P("tm", "space", None), P("tm", "space")),
        check_vma=False,
    )
```
